128 devices in a mesh: row: 16 (over y, x), col: 8 (over z, core).
Axes of the slice: x: 4, y: 4, z: 4, core: 2. Of those that a mesh axis runs over, the one named last changes fastest.
Arguments:
- right_side: float32 [4, 524288], P(None, ('row', 'col')), may hold values from -6 to 6
- geometry: float32 [4, 524288], P(None, ('row', 'col')), may hold values from -5 to 5, as said below
- pairs: int32 [7168, 2], P(('row', 'col')), may hold values from 0 to 1023, as said below
- near_count: int32 [128], P(('row', 'col')), may hold values from 1 to 16, as said below
- far_left_factor: bfloat16 [7168, 32, 512], P(('row', 'col')), may hold values from -0.3125 to 0.3125
- far_right: bfloat16 [7168, 32, 512], P(('row', 'col')), may hold values from -0.25 to 0.25
Outputs:
- solution: float32 [4, 524288], P(None, ('row', 'col'))
- residual: float32 [4, 524288], P(None, ('row', 'col'))
The draws below stay inside these ranges and needn't reach their ends.
Inputs may be any that keep to these rules, and one draw needn't show every extreme that they name: Of the 112 cluster ends of one owner's pairs, at most 2 lie on the clusters of any one device (device c // 8 holds cluster c), and exactly 2 on some device for every owner. `near_count`: some owner has exactly 16 near pairs. `geometry`: row 3 lies in 0.05 to 0.5.
All inputs are finite; a program needn't handle non-finite values.
Results may differ from the reference program's by a relative error of at most 0.0044.
Values may be sent and summed in bfloat16 or wider, within the bound.
No kernel may reach another device: no remote copies, remote signals or barrier semaphores. Data moves between devices by JAX's collectives and lax.ppermute only.
A program may use at most 64 MiB of HBM per device.

```python
import math
import jax
import jax.numpy as jnp
from jax import lax

CP = 512
RANK = 32
NRHS = 4
C_DEV = 8
P_DEV = 56
NEAR_MOST = 16
CAP = 2
CLUSTERS = 1024
NPAN = 524288
P_TOT = 7168


def draw_pairs(key, part):
    key = jax.random.fold_in(key, 11)
    owner_devices = P_TOT // P_DEV
    slots = owner_devices * CAP
    ends = 2 * P_DEV

    def one_owner(sub):
        k_first, k_rest, k_order, k_within = jax.random.split(sub, 4)
        first = jax.random.randint(k_first, (), 0, owner_devices)
        others = jax.random.permutation(k_rest, slots - CAP)
        others = jnp.where(others >= first * CAP, others + CAP, others)
        chosen = jnp.concatenate([first * CAP + jnp.arange(CAP), others[:ends - CAP]])
        chosen = jax.random.permutation(k_order, chosen)
        homes = chosen // CAP
        within = jax.random.randint(k_within, (ends,), 0, C_DEV)
        return (homes * C_DEV + within).reshape(P_DEV, 2)
    keys = jax.random.split(key, owner_devices)
    return jax.vmap(one_owner)(keys).reshape(P_TOT, 2).astype(jnp.int32)


def draw_near_count(key, part):
    key = jax.random.fold_in(key, 12)
    owner_devices = P_TOT // P_DEV
    k_counts, k_top = jax.random.split(key)
    counts = jax.random.randint(k_counts, (owner_devices,), 1, NEAR_MOST + 1)
    top = jax.random.randint(k_top, (), 0, owner_devices)
    counts = jnp.where(jnp.arange(owner_devices) == top, NEAR_MOST, counts)
    return counts.astype(jnp.int32)


def draw_geometry(key, part):
    key = jax.random.fold_in(key, 13)
    k_spread, k_size = jax.random.split(key)
    cluster = (jnp.arange(NPAN) // CP).astype(jnp.float32)
    angle = 2.0 * math.pi * cluster / CLUSTERS
    centre = jnp.stack([3.0 * jnp.cos(angle), 1.5 * jnp.sin(angle), 0.3 * (cluster - 4.0 * jnp.floor(cluster / 4.0))])
    spread = jax.random.uniform(k_spread, (3, NPAN), jnp.float32, -1.0, 1.0)
    size = jnp.exp(jax.random.uniform(k_size, (NPAN,), jnp.float32, math.log(0.05), math.log(0.5)))
    return jnp.concatenate([centre + spread, size[None, :]], axis=0).astype(jnp.float32)


def steps_of(stream_key, shape, pieces, low, largest):
    def one(axis_at, blocks):
        heights = jax.random.uniform(jax.random.fold_in(jax.random.fold_in(stream_key, 6), axis_at), (blocks,), jnp.float32, low / len(pieces), largest / len(pieces))
        return jnp.repeat(jnp.exp(heights), shape[axis_at] // blocks).reshape((-1,) + (1,) * (len(shape) - axis_at - 1))

    factor_of = one(*pieces[0])
    for cut in pieces[1:]:
        factor_of = factor_of * one(*cut)
    return factor_of


def gaussian(stream_key, shape, deviation, reach, cuts=(), kind=jnp.bfloat16):
    gain = steps_of(stream_key, shape, cuts, -0.22, 0.18) if cuts else 1.0
    values = jax.random.normal(stream_key, shape, jnp.float32) * deviation * gain
    return jnp.minimum(jnp.maximum(values, -reach), reach).astype(kind)


def setup_inputs(seed: int = 0) -> dict:
    streams_of = jax.random.split(jax.random.key(seed), 7)
    right_side = gaussian(streams_of[0], (NRHS, NPAN), 1.0, 6.0, ((1, 128),), jnp.float32)
    geometry = draw_geometry(jax.random.fold_in(streams_of[6], 71), 0)
    pairs = draw_pairs(jax.random.fold_in(streams_of[6], 71), 0)
    near_count = draw_near_count(jax.random.fold_in(streams_of[6], 71), 0)
    far_left_factor = gaussian(streams_of[4], (P_TOT, RANK, CP), (10 * RANK) ** -0.5, 0.3125, ((0, 128),))
    far_right = gaussian(streams_of[5], (P_TOT, RANK, CP), CP ** -0.5, 0.25, ((0, 128),))
    return {"right_side": right_side, "geometry": geometry, "pairs": pairs, "near_count": near_count, "far_left_factor": far_left_factor, "far_right": far_right}


inv_four_pi = 0.25 / math.pi
norm_eps = 1e-06

def tile_lookup(geo_i, geo_j):
    diff = geo_i[:3, :, None] - geo_j[:3, None, :]
    dist = lax.optimization_barrier(jnp.sum(diff * diff, axis=0)) + geo_i[3][:, None] + geo_j[3][None, :]
    return (inv_four_pi / jnp.sqrt(dist)).astype(jnp.bfloat16)

def apply_operator(vector, geometry, pairs, near_flag, far_left_factor, far_right):
    blocks = vector.reshape(NRHS, CLUSTERS, CP).transpose(1, 0, 2)
    geo = geometry.reshape(4, CLUSTERS, CP).transpose(1, 0, 2)

    def step(total, item):
        pair, flag, left, right = item
        first = pair[0]
        second = pair[1]
        x_first = blocks[first]
        x_second = blocks[second]

        def near_field_term(unused):
            tile = tile_lookup(geo[first], geo[second])
            y_first = lax.dot_general(x_second, tile, (((1,), (1,)), ((), ())), preferred_element_type=jnp.float32)
            y_second = jnp.dot(x_first, tile, preferred_element_type=jnp.float32)
            return (y_first, y_second)

        def far_term(unused):
            t_first = jnp.dot(x_second, right.T, preferred_element_type=jnp.float32).astype(jnp.bfloat16)
            y_first = jnp.dot(t_first, left, preferred_element_type=jnp.float32)
            t_second = jnp.dot(x_first, left.T, preferred_element_type=jnp.float32).astype(jnp.bfloat16)
            y_second = jnp.dot(t_second, right, preferred_element_type=jnp.float32)
            return (y_first, y_second)
        y_first, y_second = lax.cond(flag, near_field_term, far_term, 0)
        total = total.at[first].add(y_first)
        total = total.at[second].add(y_second)
        return (total, None)
    start = jnp.zeros((CLUSTERS, NRHS, CP), jnp.float32)
    total, unused = lax.scan(step, start, (pairs, near_flag, far_left_factor, far_right))
    return total.transpose(1, 0, 2).reshape(NRHS, NPAN)

def reference(right_side, geometry, pairs, near_count, far_left_factor, far_right):
    index = jnp.arange(P_TOT, dtype=jnp.int32)
    near_flag = index % P_DEV < near_count[index // P_DEV]

    def operator(vector):
        return apply_operator(vector.astype(jnp.bfloat16), geometry, pairs, near_flag, far_left_factor, far_right)

    def norm_of(w):
        return jnp.sqrt(lax.optimization_barrier(jnp.sum(w * w, axis=1)) + norm_eps)
    beta = norm_of(right_side)
    basis_one = right_side / beta[:, None]
    image = operator(basis_one)
    h11 = lax.optimization_barrier(jnp.sum(basis_one * image, axis=1))
    image = image - h11[:, None] * basis_one
    h21 = norm_of(image)
    basis_two = image / h21[:, None]
    image = operator(basis_two)
    h12 = lax.optimization_barrier(jnp.sum(basis_one * image, axis=1))
    h22 = lax.optimization_barrier(jnp.sum(basis_two * image, axis=1))
    image = image - h12[:, None] * basis_one - h22[:, None] * basis_two
    h32 = norm_of(image)
    basis_three = image / h32[:, None]
    rho_one = jnp.sqrt(h11 * h11 + h21 * h21)
    cos_one = h11 / rho_one
    sin_one = h21 / rho_one
    upper = cos_one * h12 + sin_one * h22
    lower = cos_one * h22 - sin_one * h12
    rho_two = jnp.sqrt(lower * lower + h32 * h32)
    coef_two = lower / rho_two * (-sin_one * beta) / rho_two
    coef_one = (cos_one * beta - upper * coef_two) / rho_one
    solution = coef_one[:, None] * basis_one + coef_two[:, None] * basis_two
    q_one = beta - h11 * coef_one - h12 * coef_two
    q_two = -h21 * coef_one - h22 * coef_two
    q_three = -h32 * coef_two
    residual = q_one[:, None] * basis_one + q_two[:, None] * basis_two + q_three[:, None] * basis_three
    return (solution, residual)
```

```python
import functools
import math

import jax
import jax.numpy as jnp
from jax import lax
from jax.experimental import pallas as pl
from jax.experimental.pallas import tpu as pltpu
from jax.sharding import PartitionSpec as P

CP = 512
RANK = 32
NRHS = 4
CDEV = 8
CAP = 2
NEAR_MOST = 16
GROUP = 8
EPS = 1e-06
CODE = 32767.0
GEO_MID = (0.0, 0.0, 0.0, 0.275)
GEO_HALF = (5.0, 5.0, 5.0, 0.225)
FOUR_PI = 4.0 * math.pi

bf16 = jnp.bfloat16
f32 = jnp.float32
i32 = jnp.int32
AXES = ("row", "col")
VMEM = pl.BlockSpec(memory_space=pltpu.VMEM)
SMEM = pl.BlockSpec(memory_space=pltpu.SMEM)
ANY = pl.BlockSpec(memory_space=pl.ANY)
PARAMS = pltpu.CompilerParams(vmem_limit_bytes=48 * 1024 * 1024)


def sds(shape, dtype):
    return jax.ShapeDtypeStruct(shape, dtype)


def all_to_all(x):
    return lax.all_to_all(x, AXES, split_axis=0, concat_axis=0, tiled=True)


def col4(values):
    row = lax.broadcasted_iota(i32, (4, 1), 0)
    out = jnp.full((4, 1), values[3], f32)
    for k in range(3):
        out = jnp.where(row == k, values[k], out)
    return out


def spread(columns):
    lane = lax.broadcasted_iota(i32, (4, 128), 1)
    row = lax.broadcasted_iota(i32, (4, 128), 0)
    out = jnp.zeros((4, 128), f32)
    for i, column in enumerate(columns):
        out = out + jnp.where(lane == 4 * i + row, column, 0.0)
    return jnp.sum(out, axis=0, keepdims=True)


def pick(row_vector, i):
    lane = lax.broadcasted_iota(i32, (4, 128), 1)
    row = lax.broadcasted_iota(i32, (4, 128), 0)
    return jnp.sum(jnp.where(lane == 4 * i + row, row_vector, 0.0), axis=1, keepdims=True)


def wish_kernel(ends_col, ends_row, rhs, payload, slots):
    n = ends_row.shape[1]
    home_c, local_c = ends_col[...] // CDEV, ends_col[...] % CDEV
    home_r, local_r = ends_row[...] // CDEV, ends_row[...] % CDEV
    sub = lax.broadcasted_iota(i32, (n, n), 0)
    lane = lax.broadcasted_iota(i32, (n, n), 1)
    before = jnp.logical_and(home_c == home_r, sub < lane)
    rank = jnp.sum(before.astype(i32), axis=0, keepdims=True)
    slots[...] = home_r * CAP + rank
    peers = payload.shape[0]
    home = lax.broadcasted_iota(i32, (peers, n), 0)
    wide = lax.broadcasted_iota(i32, (peers, 128), 1)
    out = jnp.zeros((peers, 128), f32)
    for k in range(CAP):
        hit = jnp.logical_and(home == home_r, rank == k)
        wish = jnp.sum(jnp.where(hit, local_r + 1, 0), axis=1, keepdims=True) - 1
        out = jnp.where(wide == k, wish.astype(f32), out)
    r = rhs[...]
    squares = jnp.sum(r * r, axis=1, keepdims=True)
    largest = jnp.max(jnp.abs(r), axis=1, keepdims=True)
    out = out + spread([jnp.zeros((4, 1), f32), squares, largest])
    payload[...] = out


def pack_first_kernel(wanted, got, own, rhs, geometry, out, factor, basis, codes):
    every = got[...]
    total = jnp.sum(every, axis=0, keepdims=True)
    beta = jnp.sqrt(pick(total, 1) + EPS)
    r = rhs[...]
    largest = pick(own[0:1, :], 2)
    scale = CODE / jnp.maximum(largest, 1e-30)
    for n in range(NRHS):
        factor[:, n, :] = jnp.broadcast_to(
            every[:, 8 + n : 9 + n] * ((1.0 / CODE) / beta[n : n + 1, :]), (every.shape[0], 128)
        )
    mid, half = col4(GEO_MID), col4([CODE / h for h in GEO_HALF])
    for c in range(CDEV):
        cut = slice(c * CP, (c + 1) * CP)
        rc = r[:, cut]
        basis[c] = rc / beta
        both = jnp.concatenate([rc * scale, (geometry[:, cut] - mid) * half], axis=0)
        both = jnp.minimum(jnp.maximum(both, -CODE), CODE)
        codes[c] = jnp.floor(both + 0.5).astype(i32).astype(jnp.int16)

    def step(s, carry):
        out[s] = codes[jnp.maximum(wanted[s], 0)]
        return carry

    lax.fori_loop(0, out.shape[0], step, 0, unroll=8)


def far_products(x_first, x_second, left, right, y_first, y_second):
    rows, wide = GROUP * NRHS, GROUP * RANK
    diagonal = (
        lax.broadcasted_iota(i32, (rows, wide), 0) // NRHS
        == lax.broadcasted_iota(i32, (rows, wide), 1) // RANK
    )
    transposed = (((1,), (1,)), ((), ()))
    for g in range(left.shape[0] // GROUP):
        at = slice(g * rows, (g + 1) * rows)
        lg = left[g * GROUP : (g + 1) * GROUP].reshape(wide, CP)
        rg = right[g * GROUP : (g + 1) * GROUP].reshape(wide, CP)
        t_first = lax.dot_general(
            x_second[at, :].astype(bf16), rg, transposed, preferred_element_type=f32
        )
        t_second = lax.dot_general(
            x_first[at, :].astype(bf16), lg, transposed, preferred_element_type=f32
        )
        t_first = jnp.where(diagonal, t_first, 0.0).astype(bf16)
        t_second = jnp.where(diagonal, t_second, 0.0).astype(bf16)
        y_first[at, :] = jnp.dot(t_first, lg, preferred_element_type=f32)
        y_second[at, :] = jnp.dot(t_second, rg, preferred_element_type=f32)


def near_products(q, near, tiles, x_first, x_second, y_first, y_second):
    at = pl.ds(pl.multiple_of(q * 8, 8), 8)
    x1, x2 = x_first[at, :].astype(bf16), x_second[at, :].astype(bf16)
    upper = lax.broadcasted_iota(i32, (8, CP), 0) < NRHS
    y1, y2 = y_first[at, :], y_second[at, :]
    for k in range(2):
        tile = tiles[2 * q + k]
        n1 = lax.dot_general(x2, tile, (((1,), (1,)), ((), ())), preferred_element_type=f32)
        n2 = jnp.dot(x1, tile, preferred_element_type=f32)
        mine = upper if k == 0 else jnp.logical_not(upper)
        mine = jnp.logical_and(mine, 2 * q + k < near)
        y1, y2 = jnp.where(mine, n1, y1), jnp.where(mine, n2, y2)
    y_first[at, :], y_second[at, :] = y1, y2


def send_products(slots, y_first, y_second, out):
    def step(q, carry):
        at = pl.ds(pl.multiple_of(q * 8, 8), 8)
        y1, y2 = y_first[at, :].astype(bf16), y_second[at, :].astype(bf16)
        out[slots[4 * q]] = y1[:NRHS]
        out[slots[4 * q + 1]] = y2[:NRHS]
        out[slots[4 * q + 2]] = y1[NRHS:]
        out[slots[4 * q + 3]] = y2[NRHS:]
        return carry

    lax.fori_loop(0, y_first.shape[0] // 8, step, 0, unroll=2)


def first_kernel(
    slots, live, got, factor, left, right, out, tiles_out,
    x_first, x_second, y_first, y_second, geo, tiles, sems,
):
    npair = left.shape[0]
    mid, half = col4(GEO_MID), col4([h / CODE for h in GEO_HALF])
    metre = col4([FOUR_PI, FOUR_PI, FOUR_PI, FOUR_PI * FOUR_PI])
    mid, half = mid * metre, half * metre

    def load(q, carry):
        at = pl.ds(pl.multiple_of(q * 8, 8), 8)
        for side, x in ((0, x_first), (1, x_second)):
            s, t = slots[4 * q + side], slots[4 * q + 2 + side]
            u = got[s].astype(i32).astype(f32)[:NRHS]
            w = got[t].astype(i32).astype(f32)[:NRHS]
            f = jnp.concatenate([factor[s // CAP], factor[t // CAP]], axis=0)
            x[at, :] = jnp.concatenate([u, w], axis=0) * jnp.concatenate([f, f, f, f], axis=1)
        return carry

    lax.fori_loop(0, npair // 2, load, 0, unroll=2)

    def load_geo(p, carry):
        for side in range(2):
            g = got[slots[2 * p + side]].astype(i32).astype(f32)[NRHS:]
            geo[side, p] = g * half + mid
        return carry

    near = live[0]
    steps = (near + 1) // 2
    lax.fori_loop(0, 2 * steps, load_geo, 0)
    far_products(x_first, x_second, left, right, y_first, y_second)

    def near_step(q, carry):
        for p in (2 * q, 2 * q + 1):
            gi = geo[0, p].T
            gj = geo[1, p]
            for a in range(0, CP, 32):
                cut = slice(a, a + 32)
                d = gi[cut, 3:4] + gj[3:4, :]
                for k in range(3):
                    e = gi[cut, k : k + 1] - gj[k : k + 1, :]
                    d = d + e * e
                tiles[p, cut, :] = lax.rsqrt(d).astype(bf16)
            pltpu.make_async_copy(tiles.at[p], tiles_out.at[p], sems.at[p]).start()
        near_products(q, near, tiles, x_first, x_second, y_first, y_second)
        return carry

    lax.fori_loop(0, steps, near_step, 0)
    send_products(slots, y_first, y_second, out)

    def finish(p, carry):
        pltpu.make_async_copy(tiles.at[p], tiles_out.at[p], sems.at[p]).wait()
        return carry

    lax.fori_loop(0, 2 * steps, finish, 0)


def second_kernel(
    slots, live, got, left, right, tiles_in, out,
    x_first, x_second, y_first, y_second, tiles, sems,
):
    npair = left.shape[0]
    near = live[0]

    def fetch(p, carry):
        pltpu.make_async_copy(tiles_in.at[p], tiles.at[p], sems.at[p]).start()
        return carry

    steps = (near + 1) // 2
    lax.fori_loop(0, 2 * steps, fetch, 0)

    def load(q, carry):
        at = pl.ds(pl.multiple_of(q * 8, 8), 8)
        for side, x in ((0, x_first), (1, x_second)):
            u, w = got[slots[4 * q + side]], got[slots[4 * q + 2 + side]]
            x[at, :] = jnp.concatenate([u.astype(f32), w.astype(f32)], axis=0)
        return carry

    lax.fori_loop(0, npair // 2, load, 0, unroll=2)
    far_products(x_first, x_second, left, right, y_first, y_second)

    def near_step(q, carry):
        for p in (2 * q, 2 * q + 1):
            pltpu.make_async_copy(tiles_in.at[p], tiles.at[p], sems.at[p]).wait()
        near_products(q, near, tiles, x_first, x_second, y_first, y_second)
        return carry

    lax.fori_loop(0, steps, near_step, 0)
    send_products(slots, y_first, y_second, out)


def gather_sum(wanted, got, total):
    total[...] = jnp.zeros(total.shape, f32)

    def step(s, carry):
        w = wanted[s]
        c = jnp.where(w < 0, CDEV, w)
        total[c] = total[c] + got[s].astype(f32)
        return carry

    lax.fori_loop(0, got.shape[0], step, 0, unroll=8)


def turn_kernel(wanted, got, image, out, total, half):
    gather_sum(wanted, got, total)
    image[...] = total[0:CDEV]
    half[...] = total[0:CDEV].astype(bf16)

    def step(s, carry):
        out[s] = half[jnp.maximum(wanted[s], 0)]
        return carry

    lax.fori_loop(0, out.shape[0], step, 0, unroll=8)


def inner(x, y):
    return jnp.sum(jnp.sum(x * y, axis=0), axis=1, keepdims=True)


def gram_kernel(wanted, got, basis, image, second, payload, total):
    gather_sum(wanted, got, total)
    s = total[0:CDEV]
    second[...] = s
    v, p = basis[...], image[...]
    row = spread([inner(v, v), inner(v, p), inner(p, p), inner(v, s), inner(p, s), inner(s, s)])
    payload[...] = jnp.broadcast_to(row, payload.shape)


def final_kernel(got, norms, basis, image, second, solution_out, residual_out):
    total = jnp.sum(got[...], axis=0, keepdims=True)
    vv, vp, pp, vs, ps, ss = (pick(total, i) for i in range(6))
    beta = jnp.sqrt(pick(jnp.sum(norms[...], axis=0, keepdims=True), 1) + EPS)
    zero = jnp.zeros_like(vv)
    h11 = vp
    first = jnp.maximum(pp - 2.0 * h11 * vp + h11 * h11 * vv, zero)
    h21 = jnp.sqrt(first + EPS)
    inv = 1.0 / h21
    v1w = (vs - h11 * vp) * inv
    v2w = (ps - h11 * pp - h11 * vs + h11 * h11 * vp) * inv * inv
    ww = (ss - 2.0 * h11 * ps + h11 * h11 * pp) * inv * inv
    v1v2 = (vp - h11 * vv) * inv
    v2v2 = first * inv * inv
    h12, h22 = v1w, v2w
    third = ww + h12 * h12 * vv + h22 * h22 * v2v2
    third = third - 2.0 * h12 * v1w - 2.0 * h22 * v2w + 2.0 * h12 * h22 * v1v2
    h32 = jnp.sqrt(jnp.maximum(third, zero) + EPS)
    rho_one = jnp.sqrt(h11 * h11 + h21 * h21)
    cos_one = h11 / rho_one
    sin_one = h21 / rho_one
    upper = cos_one * h12 + sin_one * h22
    lower = cos_one * h22 - sin_one * h12
    rho_two = jnp.sqrt(lower * lower + h32 * h32)
    coef_two = lower / rho_two * (-sin_one * beta) / rho_two
    coef_one = (cos_one * beta - upper * coef_two) / rho_one
    q_one = beta - h11 * coef_one - h12 * coef_two
    q_two = -h21 * coef_one - h22 * coef_two
    q_three = -h32 * coef_two / h32
    sol_v = coef_one - coef_two * h11 * inv
    sol_p = coef_two * inv
    res_v = q_one - q_two * h11 * inv + q_three * (h22 * h11 * inv - h12)
    res_p = q_two * inv - q_three * (h11 + h22) * inv
    res_s = q_three * inv
    for c in range(CDEV):
        cut = slice(c * CP, (c + 1) * CP)
        v, p, s = basis[c], image[c], second[c]
        solution_out[:, cut] = sol_v * v + sol_p * p
        residual_out[:, cut] = res_v * v + res_p * p + res_s * s


def shards(right_side, geometry, pairs, near_count, far_left_factor, far_right):
    devices = lax.axis_size(AXES)
    npair = pairs.shape[0]
    nslot = devices * CAP
    nends = 2 * npair
    width = right_side.shape[1]
    ends = pairs.reshape(-1)
    field = (CDEV, NRHS, CP)

    payload, slots = pl.pallas_call(
        wish_kernel,
        out_shape=(sds((devices, 128), f32), sds((1, nends), i32)),
        in_specs=[VMEM] * 3,
        out_specs=(VMEM, VMEM),
        name="wishes",
    )(ends.reshape(nends, 1), ends.reshape(1, nends), right_side)
    slots = slots.reshape(nends)
    met = all_to_all(payload.reshape(devices, 1, 128)).reshape(devices, 128)
    wanted = met[:, :CAP].astype(i32).reshape(nslot)

    outgoing, factor, basis = pl.pallas_call(
        pack_first_kernel,
        out_shape=(
            sds((nslot, 2 * NRHS, CP), jnp.int16),
            sds((devices, NRHS, 128), f32),
            sds(field, f32),
        ),
        in_specs=[SMEM] + [VMEM] * 4,
        out_specs=(VMEM,) * 3,
        scratch_shapes=[pltpu.VMEM((CDEV, 2 * NRHS, CP), jnp.int16)],
        compiler_params=PARAMS,
        name="pack_first",
    )(wanted, met, payload, right_side, geometry)
    incoming = all_to_all(outgoing.reshape(devices, CAP, 2 * NRHS, CP)).reshape(nslot, 2 * NRHS, CP)

    work = [pltpu.VMEM((npair * NRHS, CP), f32)] * 4
    cache = [pltpu.VMEM((NEAR_MOST, CP, CP), bf16), pltpu.SemaphoreType.DMA((NEAR_MOST,))]
    returning, tiles = pl.pallas_call(
        first_kernel,
        out_shape=(sds((nslot, NRHS, CP), bf16), sds((NEAR_MOST, CP, CP), bf16)),
        in_specs=[SMEM] * 2 + [VMEM] * 4,
        out_specs=(VMEM, ANY),
        scratch_shapes=work + [pltpu.VMEM((2, NEAR_MOST, NRHS, CP), f32)] + cache,
        compiler_params=PARAMS,
        name="first_operator",
    )(slots, near_count, incoming, factor, far_left_factor, far_right)

    def exchange(x):
        return all_to_all(x.reshape(devices, CAP, NRHS, CP)).reshape(nslot, NRHS, CP)

    image, outgoing = pl.pallas_call(
        turn_kernel,
        out_shape=(sds(field, f32), sds((nslot, NRHS, CP), bf16)),
        in_specs=[SMEM, VMEM],
        out_specs=(VMEM,) * 2,
        scratch_shapes=[pltpu.VMEM((CDEV + 1, NRHS, CP), f32), pltpu.VMEM(field, bf16)],
        compiler_params=PARAMS,
        name="turn",
    )(wanted, exchange(returning))

    returning = pl.pallas_call(
        second_kernel,
        out_shape=sds((nslot, NRHS, CP), bf16),
        in_specs=[SMEM] * 2 + [VMEM] * 3 + [ANY],
        out_specs=VMEM,
        scratch_shapes=work + cache,
        compiler_params=PARAMS,
        name="second_operator",
    )(slots, near_count, exchange(outgoing), far_left_factor, far_right, tiles)

    second, gram = pl.pallas_call(
        gram_kernel,
        out_shape=(sds(field, f32), sds((devices, 128), f32)),
        in_specs=[SMEM] + [VMEM] * 3,
        out_specs=(VMEM,) * 2,
        scratch_shapes=[pltpu.VMEM((CDEV + 1, NRHS, CP), f32)],
        compiler_params=PARAMS,
        name="gram",
    )(wanted, exchange(returning), basis, image)
    sums = all_to_all(gram.reshape(devices, 1, 128)).reshape(devices, 128)

    return pl.pallas_call(
        final_kernel,
        out_shape=(sds((NRHS, width), f32),) * 2,
        in_specs=[VMEM] * 5,
        out_specs=(VMEM,) * 2,
        compiler_params=PARAMS,
        name="combine",
    )(sums, met, basis, image, second)


def solution(mesh):
    spread_last = P(None, AXES)
    return jax.shard_map(
        shards,
        mesh=mesh,
        in_specs=(
            spread_last,
            spread_last,
            P(AXES, None),
            P(AXES),
            P(AXES, None, None),
            P(AXES, None, None),
        ),
        out_specs=(spread_last, spread_last),
        check_vma=False,
    )
```

```python
import functools
import math

import jax
import jax.numpy as jnp
from jax import lax
from jax.experimental import pallas as pl
from jax.experimental.pallas import tpu as pltpu
from jax.sharding import PartitionSpec as P

CP = 512
RANK = 32
NRHS = 4
CDEV = 8
CAP = 2
NEAR_MOST = 16
GROUP = 8
EPS = 1e-06
CODE = 32767.0
GEO_MID = (0.0, 0.0, 0.0, 0.275)
GEO_HALF = (5.0, 5.0, 5.0, 0.225)
FOUR_PI = 4.0 * math.pi

bf16 = jnp.bfloat16
f32 = jnp.float32
i32 = jnp.int32
AXES = ("row", "col")
VMEM = pl.BlockSpec(memory_space=pltpu.VMEM)
SMEM = pl.BlockSpec(memory_space=pltpu.SMEM)
ANY = pl.BlockSpec(memory_space=pl.ANY)


def room(mib):
    return pltpu.CompilerParams(vmem_limit_bytes=mib * 1024 * 1024)


def sds(shape, dtype):
    return jax.ShapeDtypeStruct(shape, dtype)


def all_to_all(x):
    return lax.all_to_all(x, AXES, split_axis=0, concat_axis=0, tiled=True)


def col4(values):
    row = lax.broadcasted_iota(i32, (4, 1), 0)
    out = jnp.full((4, 1), values[3], f32)
    for k in range(3):
        out = jnp.where(row == k, values[k], out)
    return out


def spread(columns):
    lane = lax.broadcasted_iota(i32, (4, 128), 1)
    row = lax.broadcasted_iota(i32, (4, 128), 0)
    out = jnp.zeros((4, 128), f32)
    for i, column in enumerate(columns):
        out = out + jnp.where(lane == 4 * i + row, column, 0.0)
    return jnp.sum(out, axis=0, keepdims=True)


def pick(row_vector, i):
    lane = lax.broadcasted_iota(i32, (4, 128), 1)
    row = lax.broadcasted_iota(i32, (4, 128), 0)
    return jnp.sum(jnp.where(lane == 4 * i + row, row_vector, 0.0), axis=1, keepdims=True)


def wish_kernel(pairs, rhs, geometry, payload, slots, codes):
    n = pairs.shape[1]
    sub = lax.broadcasted_iota(i32, (n, n), 0)
    lane = lax.broadcasted_iota(i32, (n, n), 1)
    homes, locals_, columns = [], [], []
    for k in range(2):
        ends = pairs[k : k + 1, :]
        homes.append(ends // CDEV)
        locals_.append(ends % CDEV)
        columns.append(jnp.sum(jnp.where(sub == lane, homes[k], 0), axis=1, keepdims=True))

    def count(column, row, limit):
        hit = jnp.logical_and(column == row, limit) if limit is not None else column == row
        return jnp.sum(hit.astype(i32), axis=0, keepdims=True)

    earlier = sub < lane
    ranks = [
        count(columns[0], homes[0], earlier),
        count(columns[0], homes[1], None) + count(columns[1], homes[1], earlier),
    ]
    peers = payload.shape[0]
    peer = lax.broadcasted_iota(i32, (peers, n), 0)
    wide = lax.broadcasted_iota(i32, (peers, 128), 1)
    out = jnp.zeros((peers, 128), f32)
    for j in range(CAP):
        wish = jnp.full((peers, 1), -1, i32)
        for k in range(2):
            hit = jnp.logical_and(peer == homes[k], ranks[k] == j)
            wish = wish + jnp.sum(jnp.where(hit, locals_[k] + 1, 0), axis=1, keepdims=True)
        out = jnp.where(wide == j, wish.astype(f32), out)
    for k in range(2):
        slots[k : k + 1, :] = homes[k] * CAP + ranks[k]
    r = rhs[...]
    squares = jnp.sum(r * r, axis=1, keepdims=True)
    largest = jnp.max(jnp.abs(r), axis=1, keepdims=True)
    payload[...] = out + spread([jnp.zeros((4, 1), f32), squares, largest])
    scale = CODE / jnp.maximum(largest, 1e-30)
    mid, half = col4(GEO_MID), col4([CODE / h for h in GEO_HALF])
    for c in range(CDEV):
        cut = slice(c * CP, (c + 1) * CP)
        both = jnp.concatenate([r[:, cut] * scale, (geometry[:, cut] - mid) * half], axis=0)
        both = jnp.minimum(jnp.maximum(both, -CODE), CODE)
        codes[c] = jnp.floor(both + 0.5).astype(i32).astype(jnp.int16)


def pack_kernel(wanted, codes, out):
    def step(s, carry):
        out[s] = codes[jnp.maximum(wanted[s], 0)]
        return carry

    lax.fori_loop(0, out.shape[0], step, 0, unroll=8)


def scale_kernel(met, factor):
    every = met[...]
    beta = jnp.sqrt(pick(jnp.sum(every, axis=0, keepdims=True), 1) + EPS)
    for n in range(NRHS):
        unit = every[:, 8 + n : 9 + n] * ((1.0 / CODE) / beta[n : n + 1, :])
        factor[:, n, :] = jnp.broadcast_to(unit, (every.shape[0], 128))


TRANSPOSED = (((1,), (1,)), ((), ()))


def far_products(left, right, x_first, x_second, t_first, t_second, y_first, y_second):
    rows, wide = GROUP * NRHS, GROUP * RANK
    diagonal = (
        lax.broadcasted_iota(i32, (rows, wide), 0) // NRHS
        == lax.broadcasted_iota(i32, (rows, wide), 1) // RANK
    )
    groups = left.shape[0] // GROUP
    for g in range(groups):
        at = slice(g * rows, (g + 1) * rows)
        for x, factor, t in ((x_second, right, t_first), (x_first, left, t_second)):
            f = factor[g * GROUP : (g + 1) * GROUP].reshape(wide, CP)
            value = lax.dot_general(x[at, :].astype(bf16), f, TRANSPOSED, preferred_element_type=f32)
            t[at, :] = jnp.where(diagonal, value, 0.0).astype(bf16)
    for g in range(groups):
        at = slice(g * rows, (g + 1) * rows)
        for t, factor, y in ((t_first, left, y_first), (t_second, right, y_second)):
            f = factor[g * GROUP : (g + 1) * GROUP].reshape(wide, CP)
            y[at, :] = jnp.dot(t[at, :], f, preferred_element_type=f32)


def near_products(q, near, tiles, x_first, x_second, y_first, y_second):
    at = pl.ds(pl.multiple_of(q * 8, 8), 8)
    x1, x2 = x_first[at, :].astype(bf16), x_second[at, :].astype(bf16)
    upper = lax.broadcasted_iota(i32, (8, CP), 0) < NRHS
    y1, y2 = y_first[at, :], y_second[at, :]
    for k in range(2):
        tile = tiles[2 * q + k]
        n1 = lax.dot_general(x2, tile, TRANSPOSED, preferred_element_type=f32)
        n2 = jnp.dot(x1, tile, preferred_element_type=f32)
        mine = upper if k == 0 else jnp.logical_not(upper)
        mine = jnp.logical_and(mine, 2 * q + k < near)
        y1, y2 = jnp.where(mine, n1, y1), jnp.where(mine, n2, y2)
    y_first[at, :], y_second[at, :] = y1, y2


def send_products(slots, y_first, y_second, out):
    def step(q, carry):
        at = pl.ds(pl.multiple_of(q * 8, 8), 8)
        y1, y2 = y_first[at, :].astype(bf16), y_second[at, :].astype(bf16)
        out[slots[0, 2 * q]] = y1[:NRHS]
        out[slots[1, 2 * q]] = y2[:NRHS]
        out[slots[0, 2 * q + 1]] = y1[NRHS:]
        out[slots[1, 2 * q + 1]] = y2[NRHS:]
        return carry

    lax.fori_loop(0, y_first.shape[0] // 8, step, 0, unroll=2)


def halves(x, parts):
    out = []
    for _ in range(parts):
        piece = x.astype(bf16).astype(f32)
        out.append(piece)
        x = x - piece
    return out


def distance_terms(code, side):
    unit = GEO_HALF[0] / CODE
    row = lax.broadcasted_iota(i32, (4, CP), 0)
    place = row < 3
    size = (GEO_MID[3] + code[3:4] * (GEO_HALF[3] / CODE)) * (1.0 / unit**2)
    square = jnp.sum(jnp.where(place, code * code, 0.0), axis=0, keepdims=True) + size
    n1, n2, n3 = halves(square, 3)
    high, low = halves(code, 2)
    one = jnp.ones((4, CP), f32)
    zero = jnp.zeros((4, CP), f32)
    if side == 0:
        parts = [
            jnp.where(place, high, n1), jnp.where(place, high, n2), jnp.where(place, low, n3),
            jnp.where(place, low, one), jnp.where(row < 2, one, zero),
        ]
    else:
        high, low = -2.0 * high, -2.0 * low
        parts = [
            jnp.where(place, high, one), jnp.where(place, low, one), jnp.where(place, high, one),
            jnp.where(place, low, n1), jnp.where(row == 0, n2, jnp.where(row == 1, n3, zero)),
        ]
    return jnp.concatenate(parts + [zero] * 3, axis=0)


def first_kernel(
    slots, live, got, factor, left, right, out, tiles_out,
    x_first, x_second, y_first, y_second, t_first, t_second, tiles, sems,
):
    npair = left.shape[0]
    near = live[0]

    def load(q, carry):
        at = pl.ds(pl.multiple_of(q * 8, 8), 8)
        for side, x in ((0, x_first), (1, x_second)):
            s, t = slots[side, 2 * q], slots[side, 2 * q + 1]
            u = got[s].astype(i32).astype(f32)[:NRHS]
            w = got[t].astype(i32).astype(f32)[:NRHS]
            f = jnp.concatenate([factor[s // CAP], factor[t // CAP]], axis=0)
            x[at, :] = jnp.concatenate([u, w], axis=0) * jnp.concatenate([f, f, f, f], axis=1)
        return carry

    lax.fori_loop(0, npair // 2, load, 0, unroll=2)
    far_products(left, right, x_first, x_second, t_first, t_second, y_first, y_second)
    unit = CODE / (GEO_HALF[0] * FOUR_PI)

    def near_step(q, carry):
        for k in range(2):
            p = 2 * q + k
            a = distance_terms(got[slots[0, p]].astype(i32).astype(f32)[NRHS:], 0).T.astype(bf16)
            b = distance_terms(got[slots[1, p]].astype(i32).astype(f32)[NRHS:], 1).astype(bf16)
            for cut in range(0, CP, 128):
                d = jnp.dot(a[cut : cut + 128], b, preferred_element_type=f32)
                tiles[p, cut : cut + 128, :] = (lax.rsqrt(d) * unit).astype(bf16)
            pltpu.make_async_copy(tiles.at[p], tiles_out.at[p], sems.at[p]).start()
        near_products(q, near, tiles, x_first, x_second, y_first, y_second)
        return carry

    lax.fori_loop(0, NEAR_MOST // 2, near_step, 0)
    send_products(slots, y_first, y_second, out)
    for p in range(NEAR_MOST):
        pltpu.make_async_copy(tiles.at[p], tiles_out.at[p], sems.at[p]).wait()


def second_kernel(
    slots, live, got, left, right, tiles_in, out,
    x_first, x_second, y_first, y_second, t_first, t_second, tiles, sems,
):
    npair = left.shape[0]
    near = live[0]
    for p in range(NEAR_MOST):
        pltpu.make_async_copy(tiles_in.at[p], tiles.at[p], sems.at[p]).start()

    def load(q, carry):
        at = pl.ds(pl.multiple_of(q * 8, 8), 8)
        for side, x in ((0, x_first), (1, x_second)):
            u, w = got[slots[side, 2 * q]], got[slots[side, 2 * q + 1]]
            x[at, :] = jnp.concatenate([u.astype(f32), w.astype(f32)], axis=0)
        return carry

    lax.fori_loop(0, npair // 2, load, 0, unroll=2)
    far_products(left, right, x_first, x_second, t_first, t_second, y_first, y_second)

    def near_step(q, carry):
        for p in (2 * q, 2 * q + 1):
            pltpu.make_async_copy(tiles_in.at[p], tiles.at[p], sems.at[p]).wait()
        near_products(q, near, tiles, x_first, x_second, y_first, y_second)
        return carry

    lax.fori_loop(0, NEAR_MOST // 2, near_step, 0)
    send_products(slots, y_first, y_second, out)


def gather_sum(wanted, got, total):
    total[...] = jnp.zeros(total.shape, f32)

    def step(s, carry):
        w = wanted[s]
        c = jnp.where(w < 0, CDEV, w)
        total[c] = total[c] + got[s].astype(f32)
        return carry

    lax.fori_loop(0, got.shape[0], step, 0, unroll=8)


def turn_kernel(wanted, got, image, out, total, half):
    gather_sum(wanted, got, total)
    image[...] = total[0:CDEV]
    half[...] = total[0:CDEV].astype(bf16)

    def step(s, carry):
        out[s] = half[jnp.maximum(wanted[s], 0)]
        return carry

    lax.fori_loop(0, out.shape[0], step, 0, unroll=8)


def inner(x, y):
    return jnp.sum(jnp.sum(x * y, axis=0), axis=1, keepdims=True)


def gram_kernel(wanted, got, met, rhs, image, second, basis, payload, total):
    gather_sum(wanted, got, total)
    s = total[0:CDEV]
    second[...] = s
    beta = jnp.sqrt(pick(jnp.sum(met[...], axis=0, keepdims=True), 1) + EPS)
    r = rhs[...] / beta
    for c in range(CDEV):
        basis[c] = r[:, c * CP : (c + 1) * CP]
    v, p = basis[...], image[...]
    row = spread([inner(v, v), inner(v, p), inner(p, p), inner(v, s), inner(p, s), inner(s, s)])
    payload[...] = jnp.broadcast_to(row, payload.shape)


def final_kernel(got, norms, basis, image, second, solution_out, residual_out):
    total = jnp.sum(got[...], axis=0, keepdims=True)
    vv, vp, pp, vs, ps, ss = (pick(total, i) for i in range(6))
    beta = jnp.sqrt(pick(jnp.sum(norms[...], axis=0, keepdims=True), 1) + EPS)
    zero = jnp.zeros_like(vv)
    h11 = vp
    first = jnp.maximum(pp - 2.0 * h11 * vp + h11 * h11 * vv, zero)
    h21 = jnp.sqrt(first + EPS)
    inv = 1.0 / h21
    v1w = (vs - h11 * vp) * inv
    v2w = (ps - h11 * pp - h11 * vs + h11 * h11 * vp) * inv * inv
    ww = (ss - 2.0 * h11 * ps + h11 * h11 * pp) * inv * inv
    v1v2 = (vp - h11 * vv) * inv
    v2v2 = first * inv * inv
    h12, h22 = v1w, v2w
    third = ww + h12 * h12 * vv + h22 * h22 * v2v2
    third = third - 2.0 * h12 * v1w - 2.0 * h22 * v2w + 2.0 * h12 * h22 * v1v2
    h32 = jnp.sqrt(jnp.maximum(third, zero) + EPS)
    rho_one = jnp.sqrt(h11 * h11 + h21 * h21)
    cos_one = h11 / rho_one
    sin_one = h21 / rho_one
    upper = cos_one * h12 + sin_one * h22
    lower = cos_one * h22 - sin_one * h12
    rho_two = jnp.sqrt(lower * lower + h32 * h32)
    coef_two = lower / rho_two * (-sin_one * beta) / rho_two
    coef_one = (cos_one * beta - upper * coef_two) / rho_one
    q_one = beta - h11 * coef_one - h12 * coef_two
    q_two = -h21 * coef_one - h22 * coef_two
    q_three = -h32 * coef_two / h32
    sol_v = coef_one - coef_two * h11 * inv
    sol_p = coef_two * inv
    res_v = q_one - q_two * h11 * inv + q_three * (h22 * h11 * inv - h12)
    res_p = q_two * inv - q_three * (h11 + h22) * inv
    res_s = q_three * inv
    for c in range(CDEV):
        cut = slice(c * CP, (c + 1) * CP)
        v, p, s = basis[c], image[c], second[c]
        solution_out[:, cut] = sol_v * v + sol_p * p
        residual_out[:, cut] = res_v * v + res_p * p + res_s * s


def shards(right_side, geometry, pairs, near_count, far_left_factor, far_right):
    devices = lax.axis_size(AXES)
    npair = pairs.shape[0]
    nslot = devices * CAP
    width = right_side.shape[1]
    field = (CDEV, NRHS, CP)
    coded = (nslot, 2 * NRHS, CP)

    payload, slots, codes = pl.pallas_call(
        wish_kernel,
        out_shape=(
            sds((devices, 128), f32),
            sds((2, npair), i32),
            sds((CDEV, 2 * NRHS, CP), jnp.int16),
        ),
        in_specs=[VMEM] * 3,
        out_specs=(VMEM,) * 3,
        compiler_params=room(8),
        name="wishes",
    )(pairs.T, right_side, geometry)
    met = all_to_all(payload.reshape(devices, 1, 128)).reshape(devices, 128)
    wanted = met[:, :CAP].astype(i32).reshape(nslot)

    outgoing = pl.pallas_call(
        pack_kernel,
        out_shape=sds(coded, jnp.int16),
        in_specs=[SMEM, VMEM],
        out_specs=VMEM,
        compiler_params=room(8),
        name="pack",
    )(wanted, codes)
    incoming = all_to_all(outgoing.reshape(devices, CAP, 2 * NRHS, CP)).reshape(coded)
    factor = pl.pallas_call(
        scale_kernel,
        out_shape=sds((devices, NRHS, 128), f32),
        in_specs=[VMEM],
        out_specs=VMEM,
        compiler_params=room(8),
        name="scales",
    )(met)

    work = [pltpu.VMEM((npair * NRHS, CP), f32)] * 4
    work += [pltpu.VMEM((npair * NRHS, GROUP * RANK), bf16)] * 2
    work += [pltpu.VMEM((NEAR_MOST, CP, CP), bf16), pltpu.SemaphoreType.DMA((NEAR_MOST,))]
    returning, tiles = pl.pallas_call(
        first_kernel,
        out_shape=(sds((nslot, NRHS, CP), bf16), sds((NEAR_MOST, CP, CP), bf16)),
        in_specs=[SMEM] * 2 + [VMEM] * 4,
        out_specs=(VMEM, ANY),
        scratch_shapes=work,
        compiler_params=room(28),
        name="first_operator",
    )(slots, near_count, incoming, factor, far_left_factor, far_right)

    def exchange(x):
        return all_to_all(x.reshape(devices, CAP, NRHS, CP)).reshape(nslot, NRHS, CP)

    image, outgoing = pl.pallas_call(
        turn_kernel,
        out_shape=(sds(field, f32), sds((nslot, NRHS, CP), bf16)),
        in_specs=[SMEM, VMEM],
        out_specs=(VMEM,) * 2,
        scratch_shapes=[pltpu.VMEM((CDEV + 1, NRHS, CP), f32), pltpu.VMEM(field, bf16)],
        compiler_params=room(8),
        name="turn",
    )(wanted, exchange(returning))

    returning = pl.pallas_call(
        second_kernel,
        out_shape=sds((nslot, NRHS, CP), bf16),
        in_specs=[SMEM] * 2 + [VMEM] * 3 + [ANY],
        out_specs=VMEM,
        scratch_shapes=work,
        compiler_params=room(28),
        name="second_operator",
    )(slots, near_count, exchange(outgoing), far_left_factor, far_right, tiles)

    second, basis, gram = pl.pallas_call(
        gram_kernel,
        out_shape=(sds(field, f32), sds(field, f32), sds((devices, 128), f32)),
        in_specs=[SMEM] + [VMEM] * 4,
        out_specs=(VMEM,) * 3,
        scratch_shapes=[pltpu.VMEM((CDEV + 1, NRHS, CP), f32)],
        compiler_params=room(8),
        name="gram",
    )(wanted, exchange(returning), met, right_side, image)
    sums = all_to_all(gram.reshape(devices, 1, 128)).reshape(devices, 128)

    return pl.pallas_call(
        final_kernel,
        out_shape=(sds((NRHS, width), f32),) * 2,
        in_specs=[VMEM] * 5,
        out_specs=(VMEM,) * 2,
        compiler_params=room(8),
        name="combine",
    )(sums, met, basis, image, second)


def solution(mesh):
    spread_last = P(None, AXES)
    return jax.shard_map(
        shards,
        mesh=mesh,
        in_specs=(
            spread_last,
            spread_last,
            P(AXES, None),
            P(AXES),
            P(AXES, None, None),
            P(AXES, None, None),
        ),
        out_specs=(spread_last, spread_last),
        check_vma=False,
    )
```

```python
import functools
import math

import jax
import jax.numpy as jnp
from jax import lax
from jax.experimental import pallas as pl
from jax.experimental.pallas import tpu as pltpu
from jax.sharding import PartitionSpec as P

CP = 512
RANK = 32
NRHS = 4
CDEV = 8
CAP = 2
NEAR_MOST = 16
GROUP = 8
EPS = 1e-06
CODE = 32767.0
GEO_MID = (0.0, 0.0, 0.0, 0.275)
GEO_HALF = (5.0, 5.0, 5.0, 0.225)
FOUR_PI = 4.0 * math.pi

bf16 = jnp.bfloat16
f32 = jnp.float32
i32 = jnp.int32
AXES = ("row", "col")
VMEM = pl.BlockSpec(memory_space=pltpu.VMEM)
SMEM = pl.BlockSpec(memory_space=pltpu.SMEM)
HBM = pl.BlockSpec(memory_space=pltpu.HBM)
BLOCK = (4 * NRHS, CP // 4)
LANES = CP // 4


def room(mib):
    return pltpu.CompilerParams(vmem_limit_bytes=mib * 1024 * 1024)


def sds(shape, dtype):
    return jax.ShapeDtypeStruct(shape, dtype)


def all_to_all(x):
    return lax.all_to_all(x, AXES, split_axis=0, concat_axis=0, tiled=True)


def col4(values):
    row = lax.broadcasted_iota(i32, (4, 1), 0)
    out = jnp.full((4, 1), values[3], f32)
    for k in range(3):
        out = jnp.where(row == k, values[k], out)
    return out


def spread(columns):
    lane = lax.broadcasted_iota(i32, (4, 128), 1)
    row = lax.broadcasted_iota(i32, (4, 128), 0)
    out = jnp.zeros((4, 128), f32)
    for i, column in enumerate(columns):
        out = out + jnp.where(lane == 4 * i + row, column, 0.0)
    return jnp.sum(out, axis=0, keepdims=True)


def pick(row_vector, i):
    lane = lax.broadcasted_iota(i32, (4, 128), 1)
    row = lax.broadcasted_iota(i32, (4, 128), 0)
    return jnp.sum(jnp.where(lane == 4 * i + row, row_vector, 0.0), axis=1, keepdims=True)


def fold(x):
    return jnp.concatenate([x[:, k * LANES : (k + 1) * LANES] for k in range(4)], axis=0)


def unfold(x):
    return jnp.concatenate([x[4 * k : 4 * k + 4] for k in range(4)], axis=1)


def wish_kernel(pairs_at, rhs_at, geometry_at, payload, slots, codes, pairs, rhs, geometry, sems):
    copies = [
        pltpu.make_async_copy(a, b, sems.at[k])
        for k, (a, b) in enumerate(((pairs_at, pairs), (rhs_at, rhs), (geometry_at, geometry)))
    ]
    for copy in copies:
        copy.start()
    for copy in copies:
        copy.wait()
    n = pairs.shape[1]
    sub = lax.broadcasted_iota(i32, (n, n), 0)
    lane = lax.broadcasted_iota(i32, (n, n), 1)
    homes, locals_, columns = [], [], []
    for k in range(2):
        ends = pairs[k : k + 1, :]
        homes.append(ends // CDEV)
        locals_.append(ends % CDEV)
        columns.append(jnp.sum(jnp.where(sub == lane, homes[k], 0), axis=1, keepdims=True))

    def count(column, row, limit):
        hit = jnp.logical_and(column == row, limit) if limit is not None else column == row
        return jnp.sum(hit.astype(i32), axis=0, keepdims=True)

    earlier = sub < lane
    ranks = [
        count(columns[0], homes[0], earlier),
        count(columns[0], homes[1], None) + count(columns[1], homes[1], earlier),
    ]
    peers = payload.shape[0]
    peer = lax.broadcasted_iota(i32, (peers, n), 0)
    wide = lax.broadcasted_iota(i32, (peers, 128), 1)
    out = jnp.zeros((peers, 128), f32)
    for j in range(CAP):
        wish = jnp.full((peers, 1), -1, i32)
        for k in range(2):
            hit = jnp.logical_and(peer == homes[k], ranks[k] == j)
            wish = wish + jnp.sum(jnp.where(hit, locals_[k] + 1, 0), axis=1, keepdims=True)
        out = jnp.where(wide == j, wish.astype(f32), out)
    for k in range(2):
        slots[k : k + 1, :] = homes[k] * CAP + ranks[k]
    r = rhs[...]
    squares = jnp.sum(r * r, axis=1, keepdims=True)
    largest = jnp.max(jnp.abs(r), axis=1, keepdims=True)
    payload[...] = out + spread([jnp.zeros((4, 1), f32), squares, largest])
    scale = CODE / jnp.maximum(largest, 1e-30)
    mid, half = col4(GEO_MID), col4([CODE / h for h in GEO_HALF])
    for c in range(CDEV):
        cut = slice(c * CP, (c + 1) * CP)
        both = jnp.concatenate(
            [fold(r[:, cut] * scale), fold((geometry[:, cut] - mid) * half)], axis=0
        )
        both = jnp.minimum(jnp.maximum(both, -CODE), CODE)
        codes[c] = jnp.floor(both + 0.5).astype(i32).astype(jnp.int16)


def pack_kernel(wanted, codes, out, staged, sems):
    chunk = out.shape[0] // sems.shape[0]

    def step(s, carry):
        staged[s] = codes[jnp.maximum(wanted[s], 0)]
        return carry

    copies = []
    for k in range(sems.shape[0]):
        lax.fori_loop(k * chunk, (k + 1) * chunk, step, 0, unroll=8)
        at = pl.ds(k * chunk, chunk)
        copies.append(pltpu.make_async_copy(staged.at[at], out.at[at], sems.at[k]))
        copies[k].start()
    for copy in copies:
        copy.wait()


def scale_kernel(met, factor):
    every = met[...]
    beta = jnp.sqrt(pick(jnp.sum(every, axis=0, keepdims=True), 1) + EPS)
    for n in range(NRHS):
        unit = every[:, 8 + n : 9 + n] * ((1.0 / CODE) / beta[n : n + 1, :])
        wide = jnp.broadcast_to(unit, (every.shape[0], 128))
        for k in range(4):
            factor[:, 4 * k + n, :] = wide


TRANSPOSED = (((1,), (1,)), ((), ()))


def far_products(left, right, x_first, x_second, t_first, t_second, y_first, y_second):
    rows, wide = GROUP * NRHS, GROUP * RANK
    diagonal = (
        lax.broadcasted_iota(i32, (rows, wide), 0) // NRHS
        == lax.broadcasted_iota(i32, (rows, wide), 1) // RANK
    )
    groups = left.shape[0] // GROUP
    for g in range(groups):
        at = slice(g * rows, (g + 1) * rows)
        for x, factor, t in ((x_second, right, t_first), (x_first, left, t_second)):
            f = factor[g * GROUP : (g + 1) * GROUP].reshape(wide, CP)
            value = lax.dot_general(x[at, :].astype(bf16), f, TRANSPOSED, preferred_element_type=f32)
            t[at, :] = jnp.where(diagonal, value, 0.0).astype(bf16)
    for g in range(groups):
        at = slice(g * rows, (g + 1) * rows)
        for t, factor, y in ((t_first, left, y_first), (t_second, right, y_second)):
            f = factor[g * GROUP : (g + 1) * GROUP].reshape(wide, CP)
            y[at, :] = jnp.dot(t[at, :], f, preferred_element_type=f32)


def near_products(q, near, tiles, x_first, x_second, y_first, y_second):
    at = pl.ds(pl.multiple_of(q * 8, 8), 8)
    x1, x2 = x_first[at, :].astype(bf16), x_second[at, :].astype(bf16)
    upper = lax.broadcasted_iota(i32, (8, CP), 0) < NRHS
    y1, y2 = y_first[at, :], y_second[at, :]
    for k in range(2):
        tile = tiles[2 * q + k]
        n1 = lax.dot_general(x2, tile, TRANSPOSED, preferred_element_type=f32)
        n2 = jnp.dot(x1, tile, preferred_element_type=f32)
        mine = upper if k == 0 else jnp.logical_not(upper)
        mine = jnp.logical_and(mine, 2 * q + k < near)
        y1, y2 = jnp.where(mine, n1, y1), jnp.where(mine, n2, y2)
    y_first[at, :], y_second[at, :] = y1, y2


def send_products(slots, y_first, y_second, out):
    def step(q, carry):
        at = pl.ds(pl.multiple_of(q * 8, 8), 8)
        for side, y in ((0, y_first), (1, y_second)):
            both = y[at, :]
            out[slots[side, 2 * q]] = fold(both[:NRHS]).astype(bf16)
            out[slots[side, 2 * q + 1]] = fold(both[NRHS:]).astype(bf16)
        return carry

    lax.fori_loop(0, y_first.shape[0] // 8, step, 0, unroll=2)


def halves(x, parts):
    out = []
    for _ in range(parts):
        piece = x.astype(bf16).astype(f32)
        out.append(piece)
        x = x - piece
    return out


def distance_terms(code, side):
    unit = GEO_HALF[0] / CODE
    row = lax.broadcasted_iota(i32, (4, CP), 0)
    place = row < 3
    size = (GEO_MID[3] + code[3:4] * (GEO_HALF[3] / CODE)) * (1.0 / unit**2)
    square = jnp.sum(jnp.where(place, code * code, 0.0), axis=0, keepdims=True) + size
    n1, n2, n3 = halves(square, 3)
    high, low = halves(code, 2)
    one = jnp.ones((4, CP), f32)
    zero = jnp.zeros((4, CP), f32)
    if side == 0:
        parts = [
            jnp.where(place, high, n1), jnp.where(place, high, n2), jnp.where(place, low, n3),
            jnp.where(place, low, one), jnp.where(row < 2, one, zero),
        ]
    else:
        high, low = -2.0 * high, -2.0 * low
        parts = [
            jnp.where(place, high, one), jnp.where(place, low, one), jnp.where(place, high, one),
            jnp.where(place, low, n1), jnp.where(row == 0, n2, jnp.where(row == 1, n3, zero)),
        ]
    return jnp.concatenate(parts + [zero] * 3, axis=0)


def first_kernel(
    slots, live, got, factor, left_at, right_at, out, tiles, left, right,
    x_first, x_second, y_first, y_second, t_first, t_second, sems,
):
    copies = [
        pltpu.make_async_copy(a, b, sems.at[k])
        for k, (a, b) in enumerate(((left_at, left), (right_at, right)))
    ]
    for copy in copies:
        copy.start()

    def load(q, carry):
        at = pl.ds(pl.multiple_of(q * 8, 8), 8)
        for side, x in ((0, x_first), (1, x_second)):
            s, t = slots[side, 2 * q], slots[side, 2 * q + 1]
            u = got[s, : BLOCK[0]].astype(i32).astype(f32) * factor[s // CAP]
            w = got[t, : BLOCK[0]].astype(i32).astype(f32) * factor[t // CAP]
            x[at, :] = jnp.concatenate([unfold(u), unfold(w)], axis=0)
        return carry

    lax.fori_loop(0, left.shape[0] // 2, load, 0, unroll=2)
    for copy in copies:
        copy.wait()
    far_products(left, right, x_first, x_second, t_first, t_second, y_first, y_second)
    unit = CODE / (GEO_HALF[0] * FOUR_PI)

    def near_step(q, carry):
        for k in range(2):
            p = 2 * q + k
            place = [
                unfold(got[slots[side, p], BLOCK[0] :].astype(i32).astype(f32)) for side in range(2)
            ]
            a = distance_terms(place[0], 0).T.astype(bf16)
            b = distance_terms(place[1], 1).astype(bf16)
            for cut in range(0, CP, 128):
                d = jnp.dot(a[cut : cut + 128], b, preferred_element_type=f32)
                tiles[p, cut : cut + 128, :] = (lax.rsqrt(d) * unit).astype(bf16)
        near_products(q, live[0], tiles, x_first, x_second, y_first, y_second)
        return carry

    lax.fori_loop(0, NEAR_MOST // 2, near_step, 0, unroll=2)
    send_products(slots, y_first, y_second, out)


def second_kernel(
    slots, live, got, left, right, tiles, out,
    x_first, x_second, y_first, y_second, t_first, t_second,
):
    def load(q, carry):
        at = pl.ds(pl.multiple_of(q * 8, 8), 8)
        for side, x in ((0, x_first), (1, x_second)):
            u, w = got[slots[side, 2 * q]], got[slots[side, 2 * q + 1]]
            x[at, :] = jnp.concatenate([unfold(u.astype(f32)), unfold(w.astype(f32))], axis=0)
        return carry

    lax.fori_loop(0, left.shape[0] // 2, load, 0, unroll=2)
    far_products(left, right, x_first, x_second, t_first, t_second, y_first, y_second)

    def near_step(q, carry):
        near_products(q, live[0], tiles, x_first, x_second, y_first, y_second)
        return carry

    lax.fori_loop(0, NEAR_MOST // 2, near_step, 0, unroll=4)
    send_products(slots, y_first, y_second, out)


def gather_sum(wanted, got, total):
    total[...] = jnp.zeros(total.shape, f32)

    def step(s, carry):
        w = wanted[s]
        c = jnp.where(w < 0, CDEV, w)
        total[c] = total[c] + got[s].astype(f32)
        return carry

    lax.fori_loop(0, got.shape[0], step, 0, unroll=8)


def turn_kernel(wanted, got, image, out, total, half):
    gather_sum(wanted, got, total)
    image[...] = total[0:CDEV]
    half[...] = total[0:CDEV].astype(bf16)

    def step(s, carry):
        out[s] = half[jnp.maximum(wanted[s], 0)]
        return carry

    lax.fori_loop(0, out.shape[0], step, 0, unroll=8)


def inner(x, y):
    rows = jnp.sum(jnp.sum(x * y, axis=0), axis=1, keepdims=True)
    return rows[0:4] + rows[4:8] + rows[8:12] + rows[12:16]


def gram_kernel(wanted, got, met, rhs, image, second, basis, payload, total):
    gather_sum(wanted, got, total)
    s = total[0:CDEV]
    second[...] = s
    beta = jnp.sqrt(pick(jnp.sum(met[...], axis=0, keepdims=True), 1) + EPS)
    r = rhs[...] / beta
    for c in range(CDEV):
        basis[c] = fold(r[:, c * CP : (c + 1) * CP])
    v, p = basis[...], image[...]
    row = spread([inner(v, v), inner(v, p), inner(p, p), inner(v, s), inner(p, s), inner(s, s)])
    payload[...] = jnp.broadcast_to(row, payload.shape)


def final_kernel(got, norms, basis, image, second, solution_out, residual_out):
    total = jnp.sum(got[...], axis=0, keepdims=True)
    vv, vp, pp, vs, ps, ss = (pick(total, i) for i in range(6))
    beta = jnp.sqrt(pick(jnp.sum(norms[...], axis=0, keepdims=True), 1) + EPS)
    zero = jnp.zeros_like(vv)
    h11 = vp
    first = jnp.maximum(pp - 2.0 * h11 * vp + h11 * h11 * vv, zero)
    h21 = jnp.sqrt(first + EPS)
    inv = 1.0 / h21
    v1w = (vs - h11 * vp) * inv
    v2w = (ps - h11 * pp - h11 * vs + h11 * h11 * vp) * inv * inv
    ww = (ss - 2.0 * h11 * ps + h11 * h11 * pp) * inv * inv
    v1v2 = (vp - h11 * vv) * inv
    v2v2 = first * inv * inv
    h12, h22 = v1w, v2w
    third = ww + h12 * h12 * vv + h22 * h22 * v2v2
    third = third - 2.0 * h12 * v1w - 2.0 * h22 * v2w + 2.0 * h12 * h22 * v1v2
    h32 = jnp.sqrt(jnp.maximum(third, zero) + EPS)
    rho_one = jnp.sqrt(h11 * h11 + h21 * h21)
    cos_one = h11 / rho_one
    sin_one = h21 / rho_one
    upper = cos_one * h12 + sin_one * h22
    lower = cos_one * h22 - sin_one * h12
    rho_two = jnp.sqrt(lower * lower + h32 * h32)
    coef_two = lower / rho_two * (-sin_one * beta) / rho_two
    coef_one = (cos_one * beta - upper * coef_two) / rho_one
    q_one = beta - h11 * coef_one - h12 * coef_two
    q_two = -h21 * coef_one - h22 * coef_two
    q_three = -h32 * coef_two / h32
    sol_v = coef_one - coef_two * h11 * inv
    sol_p = coef_two * inv
    res_v = q_one - q_two * h11 * inv + q_three * (h22 * h11 * inv - h12)
    res_p = q_two * inv - q_three * (h11 + h22) * inv
    res_s = q_three * inv
    sol_v, sol_p, res_v, res_p, res_s = (
        jnp.concatenate([x, x, x, x], axis=0) for x in (sol_v, sol_p, res_v, res_p, res_s)
    )
    for c in range(CDEV):
        cut = slice(c * CP, (c + 1) * CP)
        v, p, s = basis[c], image[c], second[c]
        solution_out[:, cut] = unfold(sol_v * v + sol_p * p)
        residual_out[:, cut] = unfold(res_v * v + res_p * p + res_s * s)


def shards(right_side, geometry, pairs, near_count, far_left_factor, far_right):
    devices = lax.axis_size(AXES)
    npair = pairs.shape[0]
    nslot = devices * CAP
    width = right_side.shape[1]
    field = (CDEV,) + BLOCK
    plain = (nslot,) + BLOCK
    coded = (nslot, 2 * BLOCK[0], BLOCK[1])

    payload, slots, codes = pl.pallas_call(
        wish_kernel,
        out_shape=(
            sds((devices, 128), f32),
            sds((2, npair), i32),
            sds((CDEV,) + coded[1:], jnp.int16),
        ),
        in_specs=[HBM] * 3,
        out_specs=(VMEM,) * 3,
        scratch_shapes=[
            pltpu.VMEM((2, npair), i32),
            pltpu.VMEM((NRHS, width), f32),
            pltpu.VMEM((4, width), f32),
            pltpu.SemaphoreType.DMA((3,)),
        ],
        compiler_params=room(8),
        name="wishes",
    )(pairs.T, right_side, geometry)
    met = all_to_all(payload.reshape(devices, 1, 128)).reshape(devices, 128)
    wanted = met[:, :CAP].astype(i32).reshape(nslot)

    outgoing = pl.pallas_call(
        pack_kernel,
        out_shape=sds(coded, jnp.int16),
        in_specs=[SMEM, VMEM],
        out_specs=HBM,
        scratch_shapes=[pltpu.VMEM(coded, jnp.int16), pltpu.SemaphoreType.DMA((4,))],
        compiler_params=room(8),
        name="pack",
    )(wanted, codes)
    incoming = all_to_all(outgoing.reshape(devices, CAP * coded[1], LANES)).reshape(coded)
    factor = pl.pallas_call(
        scale_kernel,
        out_shape=sds((devices,) + BLOCK, f32),
        in_specs=[VMEM],
        out_specs=VMEM,
        compiler_params=room(8),
        name="scales",
    )(met)

    work = [pltpu.VMEM((npair * NRHS, CP), f32)] * 4
    work += [pltpu.VMEM((npair * NRHS, GROUP * RANK), bf16)] * 2
    returning, tiles, left, right = pl.pallas_call(
        first_kernel,
        out_shape=(
            sds(plain, bf16),
            sds((NEAR_MOST, CP, CP), bf16),
            sds(far_left_factor.shape, bf16),
            sds(far_right.shape, bf16),
        ),
        in_specs=[SMEM] * 2 + [VMEM] * 2 + [HBM] * 2,
        out_specs=(VMEM,) * 4,
        scratch_shapes=work + [pltpu.SemaphoreType.DMA((2,))],
        compiler_params=room(26),
        name="first_operator",
    )(slots, near_count, incoming, factor, far_left_factor, far_right)

    def exchange(x):
        return all_to_all(x.reshape(devices, CAP * BLOCK[0], LANES)).reshape(plain)

    image, outgoing = pl.pallas_call(
        turn_kernel,
        out_shape=(sds(field, f32), sds(plain, bf16)),
        in_specs=[SMEM, VMEM],
        out_specs=(VMEM,) * 2,
        scratch_shapes=[pltpu.VMEM((CDEV + 1,) + BLOCK, f32), pltpu.VMEM(field, bf16)],
        compiler_params=room(8),
        name="turn",
    )(wanted, exchange(returning))

    returning = pl.pallas_call(
        second_kernel,
        out_shape=sds(plain, bf16),
        in_specs=[SMEM] * 2 + [VMEM] * 4,
        out_specs=VMEM,
        scratch_shapes=work,
        compiler_params=room(26),
        name="second_operator",
    )(slots, near_count, exchange(outgoing), left, right, tiles)

    second, basis, gram = pl.pallas_call(
        gram_kernel,
        out_shape=(sds(field, f32), sds(field, f32), sds((devices, 128), f32)),
        in_specs=[SMEM] + [VMEM] * 4,
        out_specs=(VMEM,) * 3,
        scratch_shapes=[pltpu.VMEM((CDEV + 1,) + BLOCK, f32)],
        compiler_params=room(8),
        name="gram",
    )(wanted, exchange(returning), met, right_side, image)
    sums = all_to_all(gram.reshape(devices, 1, 128)).reshape(devices, 128)

    return pl.pallas_call(
        final_kernel,
        out_shape=(sds((NRHS, width), f32),) * 2,
        in_specs=[VMEM] * 5,
        out_specs=(VMEM,) * 2,
        compiler_params=room(8),
        name="combine",
    )(sums, met, basis, image, second)


def solution(mesh):
    spread_last = P(None, AXES)
    return jax.shard_map(
        shards,
        mesh=mesh,
        in_specs=(
            spread_last,
            spread_last,
            P(AXES, None),
            P(AXES),
            P(AXES, None, None),
            P(AXES, None, None),
        ),
        out_specs=(spread_last, spread_last),
        check_vma=False,
    )
```

```python
import functools
import math

import jax
import jax.numpy as jnp
from jax import lax
from jax.experimental import pallas as pl
from jax.experimental.pallas import tpu as pltpu
from jax.sharding import PartitionSpec as P

CP = 512
RANK = 32
NRHS = 4
CDEV = 8
CAP = 2
NEAR_MOST = 16
GROUP = 8
EPS = 1e-06
CODE = 32767.0
GEO_MID = (0.0, 0.0, 0.0, 0.275)
GEO_HALF = (5.0, 5.0, 5.0, 0.225)
FOUR_PI = 4.0 * math.pi

bf16 = jnp.bfloat16
f32 = jnp.float32
i32 = jnp.int32
AXES = ("row", "col")
VMEM = pl.BlockSpec(memory_space=pltpu.VMEM)
SMEM = pl.BlockSpec(memory_space=pltpu.SMEM)
BLOCK = (4 * NRHS, CP // 4)
LANES = CP // 4


def room(mib):
    return pltpu.CompilerParams(vmem_limit_bytes=mib * 1024 * 1024)


def sds(shape, dtype):
    return jax.ShapeDtypeStruct(shape, dtype)


def all_to_all(x):
    return lax.all_to_all(x, AXES, split_axis=0, concat_axis=0, tiled=True)


def col4(values):
    row = lax.broadcasted_iota(i32, (4, 1), 0)
    out = jnp.full((4, 1), values[3], f32)
    for k in range(3):
        out = jnp.where(row == k, values[k], out)
    return out


def spread(columns):
    lane = lax.broadcasted_iota(i32, (4, 128), 1)
    row = lax.broadcasted_iota(i32, (4, 128), 0)
    out = jnp.zeros((4, 128), f32)
    for i, column in enumerate(columns):
        out = out + jnp.where(lane == 4 * i + row, column, 0.0)
    return jnp.sum(out, axis=0, keepdims=True)


def pick(row_vector, i):
    lane = lax.broadcasted_iota(i32, (4, 128), 1)
    row = lax.broadcasted_iota(i32, (4, 128), 0)
    return jnp.sum(jnp.where(lane == 4 * i + row, row_vector, 0.0), axis=1, keepdims=True)


def fold(x):
    return jnp.concatenate([x[:, k * LANES : (k + 1) * LANES] for k in range(4)], axis=0)


def unfold(x):
    return jnp.concatenate([x[4 * k : 4 * k + 4] for k in range(4)], axis=1)


def wish_kernel(live, pairs, rhs, geometry, payload, slots, codes):
    n = pairs.shape[1]
    sub = lax.broadcasted_iota(i32, (n, n), 0)
    lane = lax.broadcasted_iota(i32, (n, n), 1)
    homes, locals_, columns = [], [], []
    for k in range(2):
        ends = pairs[k : k + 1, :]
        homes.append(ends // CDEV)
        locals_.append(ends % CDEV)
        columns.append(jnp.sum(jnp.where(sub == lane, homes[k], 0), axis=1, keepdims=True))

    def count(column, row, limit):
        hit = jnp.logical_and(column == row, limit) if limit is not None else column == row
        return jnp.sum(hit.astype(i32), axis=0, keepdims=True)

    earlier = sub < lane
    ranks = [
        count(columns[0], homes[0], earlier),
        count(columns[0], homes[1], None) + count(columns[1], homes[1], earlier),
    ]
    peers = payload.shape[0]
    peer = lax.broadcasted_iota(i32, (peers, n), 0)
    wide = lax.broadcasted_iota(i32, (peers, 128), 1)
    out = jnp.zeros((peers, 128), f32)
    for j in range(CAP):
        wish = jnp.full((peers, 1), -1, i32)
        for k in range(2):
            hit = jnp.logical_and(peer == homes[k], ranks[k] == j)
            wish = wish + jnp.sum(jnp.where(hit, locals_[k] + 1, 0), axis=1, keepdims=True)
        out = jnp.where(wide == j, wish.astype(f32), out)
    for k in range(2):
        slots[k : k + 1, 0:n] = homes[k] * CAP + ranks[k]
        slots[k : k + 1, n : n + 8] = jnp.broadcast_to(live[0], (1, 8))
    r = rhs[...]
    squares = jnp.sum(r * r, axis=1, keepdims=True)
    largest = jnp.max(jnp.abs(r), axis=1, keepdims=True)
    payload[...] = out + spread([jnp.zeros((4, 1), f32), squares, largest])
    scale = CODE / jnp.maximum(largest, 1e-30)
    mid, half = col4(GEO_MID), col4([CODE / h for h in GEO_HALF])
    for c in range(CDEV):
        cut = slice(c * CP, (c + 1) * CP)
        both = jnp.concatenate(
            [fold(r[:, cut] * scale), fold((geometry[:, cut] - mid) * half)], axis=0
        )
        both = jnp.minimum(jnp.maximum(both, -CODE), CODE)
        codes[c] = jnp.floor(both + 0.5).astype(i32).astype(jnp.int16)


def pack_kernel(wanted, codes, met, out, factor):
    every = met[...]
    beta = jnp.sqrt(pick(jnp.sum(every, axis=0, keepdims=True), 1) + EPS)
    for n in range(NRHS):
        unit = every[:, 8 + n : 9 + n] * ((1.0 / CODE) / beta[n : n + 1, :])
        wide = jnp.broadcast_to(unit, (every.shape[0], 128))
        factor[:, n, :] = wide
        factor[:, NRHS + n, :] = wide

    def step(s, carry):
        out[s] = codes[jnp.maximum(wanted[s], 0)]
        return carry

    lax.fori_loop(0, out.shape[0], step, 0, unroll=16)


TRANSPOSED = (((1,), (1,)), ((), ()))


def far_products(left, right, x_first, x_second, t_first, t_second, y_first, y_second):
    rows, wide = GROUP * NRHS, GROUP * RANK
    diagonal = (
        lax.broadcasted_iota(i32, (rows, wide), 0) // NRHS
        == lax.broadcasted_iota(i32, (rows, wide), 1) // RANK
    )
    groups = left.shape[0] // GROUP
    for g in range(groups):
        at = slice(g * rows, (g + 1) * rows)
        for x, factor, t in ((x_second, right, t_first), (x_first, left, t_second)):
            f = factor[g * GROUP : (g + 1) * GROUP].reshape(wide, CP)
            value = lax.dot_general(x[at, :].astype(bf16), f, TRANSPOSED, preferred_element_type=f32)
            t[at, :] = jnp.where(diagonal, value, 0.0).astype(bf16)
    for g in range(groups):
        at = slice(g * rows, (g + 1) * rows)
        for t, factor, y in ((t_first, left, y_first), (t_second, right, y_second)):
            f = factor[g * GROUP : (g + 1) * GROUP].reshape(wide, CP)
            y[at, :] = jnp.dot(t[at, :], f, preferred_element_type=f32)


def near_product(p, near, tile, x_first, x_second, y_first, y_second):
    at = pl.ds(pl.multiple_of(p // 2 * 8, 8), 8)
    mine = lax.broadcasted_iota(i32, (8, CP), 0) // NRHS == p % 2
    mine = jnp.logical_and(mine, p < near)
    n1 = lax.dot_general(
        x_second[at, :].astype(bf16), tile, TRANSPOSED, preferred_element_type=f32
    )
    n2 = jnp.dot(x_first[at, :].astype(bf16), tile, preferred_element_type=f32)
    y_first[at, :] = jnp.where(mine, n1, y_first[at, :])
    y_second[at, :] = jnp.where(mine, n2, y_second[at, :])


def send_products(slots, y_first, y_second, out):
    def step(q, carry):
        at = pl.ds(pl.multiple_of(q * 8, 8), 8)
        for side, y in ((0, y_first), (1, y_second)):
            both = y[at, :]
            out[slots[side, 2 * q]] = fold(both[:NRHS]).astype(bf16)
            out[slots[side, 2 * q + 1]] = fold(both[NRHS:]).astype(bf16)
        return carry

    lax.fori_loop(0, y_first.shape[0] // 8, step, 0, unroll=2)


def halves(x, parts):
    out = []
    for _ in range(parts):
        piece = x.astype(bf16).astype(f32)
        out.append(piece)
        x = x - piece
    return out


def distance_terms(code, side):
    unit = GEO_HALF[0] / CODE
    row = lax.broadcasted_iota(i32, (4, CP), 0)
    place = row < 3
    size = (GEO_MID[3] + code[3:4] * (GEO_HALF[3] / CODE)) * (1.0 / unit**2)
    square = jnp.sum(jnp.where(place, code * code, 0.0), axis=0, keepdims=True) + size
    n1, n2, n3 = halves(square, 3)
    high, low = halves(code, 2)
    one = jnp.ones((4, CP), f32)
    zero = jnp.zeros((4, CP), f32)
    if side == 0:
        parts = [
            jnp.where(place, high, n1), jnp.where(place, high, n2), jnp.where(place, low, n3),
            jnp.where(place, low, one), jnp.where(row < 2, one, zero),
        ]
    else:
        high, low = -2.0 * high, -2.0 * low
        parts = [
            jnp.where(place, high, one), jnp.where(place, low, one), jnp.where(place, high, one),
            jnp.where(place, low, n1), jnp.where(row == 0, n2, jnp.where(row == 1, n3, zero)),
        ]
    return jnp.concatenate(parts + [zero] * 3, axis=0)


def first_kernel(
    slots, got, factor, left, right, out, even, odd,
    x_first, x_second, y_first, y_second, t_first, t_second,
):
    npair = left.shape[0]
    near = slots[0, npair]

    def load(q, carry):
        at = pl.ds(pl.multiple_of(q * 8, 8), 8)
        for side, x in ((0, x_first), (1, x_second)):
            s, t = slots[side, 2 * q], slots[side, 2 * q + 1]
            f, g = factor[s // CAP], factor[t // CAP]
            u = got[s, : BLOCK[0]].astype(i32).astype(f32) * jnp.concatenate([f, f], axis=0)
            w = got[t, : BLOCK[0]].astype(i32).astype(f32) * jnp.concatenate([g, g], axis=0)
            x[at, :] = jnp.concatenate([unfold(u), unfold(w)], axis=0)
        return carry

    lax.fori_loop(0, npair // 2, load, 0, unroll=2)
    far_products(left, right, x_first, x_second, t_first, t_second, y_first, y_second)
    unit = CODE / (GEO_HALF[0] * FOUR_PI)

    def make(p, tiles, q):
        place = [
            unfold(got[slots[side, p], BLOCK[0] :].astype(i32).astype(f32)) for side in range(2)
        ]
        a = distance_terms(place[0], 0).T.astype(bf16)
        b = distance_terms(place[1], 1).astype(bf16)
        for cut in range(0, CP, 128):
            d = jnp.dot(a[cut : cut + 128], b, preferred_element_type=f32)
            tiles[q, cut : cut + 128, :] = (lax.rsqrt(d) * unit).astype(bf16)

    def use(p, tiles, q):
        near_product(p, near, tiles[q], x_first, x_second, y_first, y_second)

    def near_step(q, carry):
        use(2 * q, even, q)
        make(2 * q + 1, odd, q)
        use(2 * q + 1, odd, q)
        make(2 * q + 2, even, q + 1)
        return carry

    last = NEAR_MOST // 2 - 1
    make(0, even, 0)
    lax.fori_loop(0, last, near_step, 0)
    use(2 * last, even, last)
    make(2 * last + 1, odd, last)
    use(2 * last + 1, odd, last)
    send_products(slots, y_first, y_second, out)


def second_kernel(
    slots, got, left, right, even, odd, out,
    x_first, x_second, y_first, y_second, t_first, t_second,
):
    npair = left.shape[0]
    near = slots[0, npair]

    def load(q, carry):
        at = pl.ds(pl.multiple_of(q * 8, 8), 8)
        for side, x in ((0, x_first), (1, x_second)):
            u, w = got[slots[side, 2 * q]], got[slots[side, 2 * q + 1]]
            x[at, :] = jnp.concatenate([unfold(u.astype(f32)), unfold(w.astype(f32))], axis=0)
        return carry

    lax.fori_loop(0, npair // 2, load, 0, unroll=2)
    far_products(left, right, x_first, x_second, t_first, t_second, y_first, y_second)

    def near_step(q, carry):
        near_product(2 * q, near, even[q], x_first, x_second, y_first, y_second)
        near_product(2 * q + 1, near, odd[q], x_first, x_second, y_first, y_second)
        return carry

    lax.fori_loop(0, NEAR_MOST // 2, near_step, 0, unroll=4)
    send_products(slots, y_first, y_second, out)


LOOSE = 8


def gather_sum(wanted, got, totals):
    for total in totals:
        total[...] = jnp.zeros(total.shape, f32)

    def step(q, carry):
        for k, total in enumerate(totals):
            w = wanted[q * LOOSE + k]
            c = jnp.where(w < 0, CDEV, w)
            total[c] = total[c] + got[q * LOOSE + k].astype(f32)
        return carry

    lax.fori_loop(0, got.shape[0] // LOOSE, step, 0, unroll=2)
    parts = [total[0:CDEV] for total in totals]
    while len(parts) > 1:
        parts = [a + b for a, b in zip(parts[::2], parts[1::2])]
    return parts[0]


def turn_kernel(wanted, got, image, out, half, *totals):
    total = gather_sum(wanted, got, totals)
    image[...] = total
    half[...] = total.astype(bf16)

    def step(s, carry):
        out[s] = half[jnp.maximum(wanted[s], 0)]
        return carry

    lax.fori_loop(0, out.shape[0], step, 0, unroll=16)


def inner(x, y):
    rows = jnp.sum(jnp.sum(x * y, axis=0), axis=1, keepdims=True)
    return rows[0:4] + rows[4:8] + rows[8:12] + rows[12:16]


def gram_kernel(wanted, got, met, rhs, image, second, basis, payload, *totals):
    s = gather_sum(wanted, got, totals)
    second[...] = s
    beta = jnp.sqrt(pick(jnp.sum(met[...], axis=0, keepdims=True), 1) + EPS)
    r = rhs[...] / beta
    for c in range(CDEV):
        basis[c] = fold(r[:, c * CP : (c + 1) * CP])
    v, p = basis[...], image[...]
    row = spread([inner(v, v), inner(v, p), inner(p, p), inner(v, s), inner(p, s), inner(s, s)])
    payload[...] = jnp.broadcast_to(row, payload.shape)


def final_kernel(got, norms, basis, image, second, solution_out, residual_out):
    total = jnp.sum(got[...], axis=0, keepdims=True)
    vv, vp, pp, vs, ps, ss = (pick(total, i) for i in range(6))
    beta = jnp.sqrt(pick(jnp.sum(norms[...], axis=0, keepdims=True), 1) + EPS)
    zero = jnp.zeros_like(vv)
    h11 = vp
    first = jnp.maximum(pp - 2.0 * h11 * vp + h11 * h11 * vv, zero)
    h21 = jnp.sqrt(first + EPS)
    inv = 1.0 / h21
    v1w = (vs - h11 * vp) * inv
    v2w = (ps - h11 * pp - h11 * vs + h11 * h11 * vp) * inv * inv
    ww = (ss - 2.0 * h11 * ps + h11 * h11 * pp) * inv * inv
    v1v2 = (vp - h11 * vv) * inv
    v2v2 = first * inv * inv
    h12, h22 = v1w, v2w
    third = ww + h12 * h12 * vv + h22 * h22 * v2v2
    third = third - 2.0 * h12 * v1w - 2.0 * h22 * v2w + 2.0 * h12 * h22 * v1v2
    h32 = jnp.sqrt(jnp.maximum(third, zero) + EPS)
    rho_one = jnp.sqrt(h11 * h11 + h21 * h21)
    cos_one = h11 / rho_one
    sin_one = h21 / rho_one
    upper = cos_one * h12 + sin_one * h22
    lower = cos_one * h22 - sin_one * h12
    rho_two = jnp.sqrt(lower * lower + h32 * h32)
    coef_two = lower / rho_two * (-sin_one * beta) / rho_two
    coef_one = (cos_one * beta - upper * coef_two) / rho_one
    q_one = beta - h11 * coef_one - h12 * coef_two
    q_two = -h21 * coef_one - h22 * coef_two
    q_three = -h32 * coef_two / h32
    sol_v = coef_one - coef_two * h11 * inv
    sol_p = coef_two * inv
    res_v = q_one - q_two * h11 * inv + q_three * (h22 * h11 * inv - h12)
    res_p = q_two * inv - q_three * (h11 + h22) * inv
    res_s = q_three * inv
    sol_v, sol_p, res_v, res_p, res_s = (
        jnp.concatenate([x, x, x, x], axis=0) for x in (sol_v, sol_p, res_v, res_p, res_s)
    )
    for c in range(CDEV):
        cut = slice(c * CP, (c + 1) * CP)
        v, p, s = basis[c], image[c], second[c]
        solution_out[:, cut] = unfold(sol_v * v + sol_p * p)
        residual_out[:, cut] = unfold(res_v * v + res_p * p + res_s * s)


def shards(right_side, geometry, pairs, near_count, far_left_factor, far_right):
    devices = lax.axis_size(AXES)
    npair = pairs.shape[0]
    nslot = devices * CAP
    width = right_side.shape[1]
    field = (CDEV,) + BLOCK
    plain = (nslot,) + BLOCK
    coded = (nslot, 2 * BLOCK[0], BLOCK[1])

    payload, slots, codes = pl.pallas_call(
        wish_kernel,
        out_shape=(
            sds((devices, 128), f32),
            sds((2, npair + 8), i32),
            sds((CDEV,) + coded[1:], jnp.int16),
        ),
        in_specs=[SMEM] + [VMEM] * 3,
        out_specs=(VMEM,) * 3,
        compiler_params=room(8),
        name="wishes",
    )(near_count, pairs.T, right_side, geometry)
    met = all_to_all(payload.reshape(devices, 1, 128)).reshape(devices, 128)
    wanted = met[:, :CAP].astype(i32).reshape(nslot)

    outgoing, factor = pl.pallas_call(
        pack_kernel,
        out_shape=(sds(coded, jnp.int16), sds((devices, 2 * NRHS, 128), f32)),
        in_specs=[SMEM] + [VMEM] * 2,
        out_specs=(VMEM,) * 2,
        compiler_params=room(8),
        name="pack",
    )(wanted, codes, met)
    incoming = all_to_all(outgoing.reshape(devices, CAP * coded[1], LANES)).reshape(coded)

    work = [pltpu.VMEM((npair * NRHS, CP), f32)] * 4
    work += [pltpu.VMEM((npair * NRHS, GROUP * RANK), bf16)] * 2
    half_tiles = sds((NEAR_MOST // 2, CP, CP), bf16)
    returning, even, odd = pl.pallas_call(
        first_kernel,
        out_shape=(sds(plain, bf16), half_tiles, half_tiles),
        in_specs=[SMEM] + [VMEM] * 4,
        out_specs=(VMEM,) * 3,
        scratch_shapes=work,
        compiler_params=room(24),
        name="first_operator",
    )(slots, incoming, factor, far_left_factor, far_right)

    def exchange(x):
        return all_to_all(x.reshape(devices, CAP * BLOCK[0], LANES)).reshape(plain)

    totals = [pltpu.VMEM((CDEV + 1,) + BLOCK, f32)] * LOOSE
    image, outgoing = pl.pallas_call(
        turn_kernel,
        out_shape=(sds(field, f32), sds(plain, bf16)),
        in_specs=[SMEM, VMEM],
        out_specs=(VMEM,) * 2,
        scratch_shapes=[pltpu.VMEM(field, bf16)] + totals,
        compiler_params=room(8),
        name="turn",
    )(wanted, exchange(returning))

    returning = pl.pallas_call(
        second_kernel,
        out_shape=sds(plain, bf16),
        in_specs=[SMEM] + [VMEM] * 5,
        out_specs=VMEM,
        scratch_shapes=work,
        compiler_params=room(24),
        name="second_operator",
    )(slots, exchange(outgoing), far_left_factor, far_right, even, odd)

    second, basis, gram = pl.pallas_call(
        gram_kernel,
        out_shape=(sds(field, f32), sds(field, f32), sds((devices, 128), f32)),
        in_specs=[SMEM] + [VMEM] * 4,
        out_specs=(VMEM,) * 3,
        scratch_shapes=totals,
        compiler_params=room(8),
        name="gram",
    )(wanted, exchange(returning), met, right_side, image)
    sums = all_to_all(gram.reshape(devices, 1, 128)).reshape(devices, 128)

    return pl.pallas_call(
        final_kernel,
        out_shape=(sds((NRHS, width), f32),) * 2,
        in_specs=[VMEM] * 5,
        out_specs=(VMEM,) * 2,
        compiler_params=room(8),
        name="combine",
    )(sums, met, basis, image, second)


def solution(mesh):
    spread_last = P(None, AXES)
    return jax.shard_map(
        shards,
        mesh=mesh,
        in_specs=(
            spread_last,
            spread_last,
            P(AXES, None),
            P(AXES),
            P(AXES, None, None),
            P(AXES, None, None),
        ),
        out_specs=(spread_last, spread_last),
        check_vma=False,
    )
```

```python
import functools
import math

import jax
import jax.numpy as jnp
from jax import lax
from jax.experimental import pallas as pl
from jax.experimental.pallas import tpu as pltpu
from jax.sharding import PartitionSpec as P

CP = 512
RANK = 32
NRHS = 4
CDEV = 8
CAP = 2
NEAR_MOST = 16
GROUP = 8
EPS = 1e-06
CODE = 32767.0
GEO_MID = (0.0, 0.0, 0.0, 0.275)
GEO_HALF = (5.0, 5.0, 5.0, 0.225)
FOUR_PI = 4.0 * math.pi

bf16 = jnp.bfloat16
f32 = jnp.float32
i32 = jnp.int32
AXES = ("row", "col")
VMEM = pl.BlockSpec(memory_space=pltpu.VMEM)
SMEM = pl.BlockSpec(memory_space=pltpu.SMEM)
BLOCK = (4 * NRHS, CP // 4)
LANES = CP // 4


def room(mib):
    return pltpu.CompilerParams(vmem_limit_bytes=mib * 1024 * 1024)


def sds(shape, dtype):
    return jax.ShapeDtypeStruct(shape, dtype)


def all_to_all(x):
    return lax.all_to_all(x, AXES, split_axis=0, concat_axis=0, tiled=True)


def col4(values):
    row = lax.broadcasted_iota(i32, (4, 1), 0)
    out = jnp.full((4, 1), values[3], f32)
    for k in range(3):
        out = jnp.where(row == k, values[k], out)
    return out


def spread(columns):
    lane = lax.broadcasted_iota(i32, (4, 128), 1)
    row = lax.broadcasted_iota(i32, (4, 128), 0)
    out = jnp.zeros((4, 128), f32)
    for i, column in enumerate(columns):
        out = out + jnp.where(lane == 4 * i + row, column, 0.0)
    return jnp.sum(out, axis=0, keepdims=True)


def pick(row_vector, i):
    lane = lax.broadcasted_iota(i32, (4, 128), 1)
    row = lax.broadcasted_iota(i32, (4, 128), 0)
    return jnp.sum(jnp.where(lane == 4 * i + row, row_vector, 0.0), axis=1, keepdims=True)


def fold(x):
    return jnp.concatenate([x[:, k * LANES : (k + 1) * LANES] for k in range(4)], axis=0)


def upper_half():
    return lax.broadcasted_iota(i32, (8, LANES), 0) < 4


def swap(x):
    return pltpu.roll(x, 4, axis=0)


def fold_two(x):
    up = upper_half()
    a, b, c, d = (x[:, k * LANES : (k + 1) * LANES] for k in range(4))
    first = [jnp.where(up, a, swap(b)), jnp.where(up, c, swap(d))]
    second = [jnp.where(up, swap(a), b), jnp.where(up, swap(c), d)]
    return jnp.concatenate(first, axis=0), jnp.concatenate(second, axis=0)


def unfold_two(u, w):
    up = upper_half()
    out = []
    for at in (slice(0, 8), slice(8, 16)):
        out += [jnp.where(up, u[at], swap(w[at])), jnp.where(up, swap(u[at]), w[at])]
    return jnp.concatenate(out, axis=1)


def unfold(x):
    return jnp.concatenate([x[4 * k : 4 * k + 4] for k in range(4)], axis=1)


def wish_kernel(live, pairs, rhs, geometry, payload, slots, codes):
    n = pairs.shape[1]
    sub = lax.broadcasted_iota(i32, (n, n), 0)
    lane = lax.broadcasted_iota(i32, (n, n), 1)
    homes, locals_, columns = [], [], []
    for k in range(2):
        ends = pairs[k : k + 1, :]
        homes.append(ends // CDEV)
        locals_.append(ends % CDEV)
        columns.append(jnp.sum(jnp.where(sub == lane, homes[k], 0), axis=1, keepdims=True))

    def count(column, row, limit):
        hit = jnp.logical_and(column == row, limit) if limit is not None else column == row
        return jnp.sum(hit.astype(i32), axis=0, keepdims=True)

    earlier = sub < lane
    ranks = [
        count(columns[0], homes[0], earlier),
        count(columns[0], homes[1], None) + count(columns[1], homes[1], earlier),
    ]
    peers = payload.shape[0]
    peer = lax.broadcasted_iota(i32, (peers, n), 0)
    wide = lax.broadcasted_iota(i32, (peers, 128), 1)
    out = jnp.zeros((peers, 128), f32)
    for j in range(CAP):
        wish = jnp.full((peers, 1), -1, i32)
        for k in range(2):
            hit = jnp.logical_and(peer == homes[k], ranks[k] == j)
            wish = wish + jnp.sum(jnp.where(hit, locals_[k] + 1, 0), axis=1, keepdims=True)
        out = jnp.where(wide == j, wish.astype(f32), out)
    for k in range(2):
        slots[k : k + 1, 0:n] = homes[k] * CAP + ranks[k]
        slots[k : k + 1, n : n + 8] = jnp.broadcast_to(live[0], (1, 8))
    r = rhs[...]
    squares = jnp.sum(r * r, axis=1, keepdims=True)
    largest = jnp.max(jnp.abs(r), axis=1, keepdims=True)
    payload[...] = out + spread([jnp.zeros((4, 1), f32), squares, largest])
    scale = CODE / jnp.maximum(largest, 1e-30)
    mid, half = col4(GEO_MID), col4([CODE / h for h in GEO_HALF])
    for c in range(CDEV):
        cut = slice(c * CP, (c + 1) * CP)
        both = jnp.concatenate(
            [fold(r[:, cut] * scale), fold((geometry[:, cut] - mid) * half)], axis=0
        )
        both = jnp.minimum(jnp.maximum(both, -CODE), CODE)
        codes[c] = jnp.floor(both + 0.5).astype(i32).astype(jnp.int16)


def pack_kernel(wanted, codes, met, out, factor):
    every = met[...]
    beta = jnp.sqrt(pick(jnp.sum(every, axis=0, keepdims=True), 1) + EPS)
    for n in range(NRHS):
        unit = every[:, 8 + n : 9 + n] * ((1.0 / CODE) / beta[n : n + 1, :])
        wide = jnp.broadcast_to(unit, (every.shape[0], 128))
        factor[:, n, :] = wide
        factor[:, NRHS + n, :] = wide

    def step(s, carry):
        out[s] = codes[jnp.maximum(wanted[s], 0)]
        return carry

    lax.fori_loop(0, out.shape[0], step, 0, unroll=16)


TRANSPOSED = (((1,), (1,)), ((), ()))


def far_products(left, right, x_first, x_second, t_first, t_second, y_first, y_second):
    rows, wide = GROUP * NRHS, GROUP * RANK
    diagonal = (
        lax.broadcasted_iota(i32, (rows, wide), 0) // NRHS
        == lax.broadcasted_iota(i32, (rows, wide), 1) // RANK
    )
    groups = left.shape[0] // GROUP
    for g in range(groups):
        at = slice(g * rows, (g + 1) * rows)
        for x, factor, t in ((x_second, right, t_first), (x_first, left, t_second)):
            f = factor[g * GROUP : (g + 1) * GROUP].reshape(wide, CP)
            value = lax.dot_general(x[at, :].astype(bf16), f, TRANSPOSED, preferred_element_type=f32)
            t[at, :] = jnp.where(diagonal, value, 0.0).astype(bf16)
    for g in range(groups):
        at = slice(g * rows, (g + 1) * rows)
        for t, factor, y in ((t_first, left, y_first), (t_second, right, y_second)):
            f = factor[g * GROUP : (g + 1) * GROUP].reshape(wide, CP)
            y[at, :] = jnp.dot(t[at, :], f, preferred_element_type=f32)


def near_products(q, near, tiles, x_first, x_second, y_first, y_second, between=None):
    at = pl.ds(pl.multiple_of(q * 8, 8), 8)
    row = lax.broadcasted_iota(i32, (8, CP), 0)
    mine = 2 * q + row // NRHS < near
    x1, x2 = x_first[at, :], x_second[at, :]
    n1 = n2 = 0.0
    for k in range(2):
        tile = tiles[q // 2, k]
        here = row // NRHS == k
        n1 += lax.dot_general(
            jnp.where(here, x2, 0.0).astype(bf16), tile, TRANSPOSED, preferred_element_type=f32
        )
        if between:
            between(2 * k)
        n2 += jnp.dot(jnp.where(here, x1, 0.0).astype(bf16), tile, preferred_element_type=f32)
        if between:
            between(2 * k + 1)
    y_first[at, :] = jnp.where(mine, n1, y_first[at, :])
    y_second[at, :] = jnp.where(mine, n2, y_second[at, :])


def send_products(slots, y_first, y_second, out):
    def step(q, carry):
        at = pl.ds(pl.multiple_of(q * 8, 8), 8)
        for side, y in ((0, y_first), (1, y_second)):
            a, b = fold_two(y[at, :])
            out[slots[side, 2 * q]] = a.astype(bf16)
            out[slots[side, 2 * q + 1]] = b.astype(bf16)
        return carry

    lax.fori_loop(0, y_first.shape[0] // 8, step, 0, unroll=4)


def halves(x, parts):
    out = []
    for _ in range(parts):
        piece = x.astype(bf16).astype(f32)
        out.append(piece)
        x = x - piece
    return out


TERMS = 48


def distance_terms(code, side):
    unit = GEO_HALF[0] / CODE
    row = lax.broadcasted_iota(i32, (8, CP), 0)
    place = row % 4 < 3
    squares = jnp.where(place, code * code, 0.0)
    sizes = (GEO_MID[3] + code * (GEO_HALF[3] / CODE)) * (1.0 / unit**2)
    squares = jnp.where(place, squares, sizes)
    totals = [jnp.sum(squares[k : k + 4], axis=0, keepdims=True) for k in (0, 4)]
    total = jnp.where(row < 4, totals[0], totals[1])
    n1, n2, n3 = halves(total, 3)
    high, low = halves(code, 2)
    one = jnp.ones((8, CP), f32)
    zero = jnp.zeros((8, CP), f32)
    if side == 0:
        parts = [
            jnp.where(place, high, n1), jnp.where(place, high, n2), jnp.where(place, low, n3),
            jnp.where(place, low, one), jnp.where(row % 4 < 2, one, zero),
        ]
    else:
        high, low = -2.0 * high, -2.0 * low
        parts = [
            jnp.where(place, high, one), jnp.where(place, low, one), jnp.where(place, high, one),
            jnp.where(place, low, n1),
            jnp.where(row % 4 == 0, n2, jnp.where(row % 4 == 1, n3, zero)),
        ]
    return jnp.concatenate(parts + [zero], axis=0)


def first_kernel(
    slots, got, factor, left, right, out, even, odd,
    x_first, x_second, y_first, y_second, t_first, t_second, terms_first, terms_second,
):
    npair = left.shape[0]
    near = slots[0, npair]

    def load(q, carry):
        at = pl.ds(pl.multiple_of(q * 8, 8), 8)
        for side, x in ((0, x_first), (1, x_second)):
            s, t = slots[side, 2 * q], slots[side, 2 * q + 1]
            f, g = factor[s // CAP], factor[t // CAP]
            u = got[s, : BLOCK[0]].astype(i32).astype(f32) * jnp.concatenate([f, f], axis=0)
            w = got[t, : BLOCK[0]].astype(i32).astype(f32) * jnp.concatenate([g, g], axis=0)
            x[at, :] = unfold_two(u, w)
        return carry

    lax.fori_loop(0, npair // 2, load, 0, unroll=4)
    term = lax.broadcasted_iota(i32, (TERMS, CP), 0)

    def load_terms(q, carry):
        place = [
            unfold_two(*(got[slots[side, 2 * q + k], BLOCK[0] :].astype(i32).astype(f32) for k in range(2)))
            for side in range(2)
        ]
        terms_first[q] = distance_terms(place[0], 0).T.astype(bf16)
        both = distance_terms(place[1], 1)
        for k in range(2):
            terms_second[2 * q + k] = jnp.where(term % 8 // 4 == k, both, 0.0).astype(bf16)
        return carry

    lax.fori_loop(0, NEAR_MOST // 2, load_terms, 0, unroll=2)
    far_products(left, right, x_first, x_second, t_first, t_second, y_first, y_second)
    unit = CODE / (GEO_HALF[0] * FOUR_PI)

    def make(q, tiles, part):
        k = part // 2
        for cut in range(part % 2 * 256, part % 2 * 256 + 256, 128):
            d = jnp.dot(
                terms_first[q, cut : cut + 128, :], terms_second[2 * q + k],
                preferred_element_type=f32,
            )
            tiles[q // 2, k, cut : cut + 128, :] = (lax.rsqrt(d) * unit).astype(bf16)

    def use(q, tiles, between=None):
        near_products(q, near, tiles, x_first, x_second, y_first, y_second, between)

    def near_step(h, carry):
        use(2 * h, even, lambda part: make(2 * h + 1, odd, part))
        use(2 * h + 1, odd, lambda part: make(2 * h + 2, even, part))
        return carry

    last = NEAR_MOST // 2 - 1
    for part in range(4):
        make(0, even, part)
    lax.fori_loop(0, last // 2, near_step, 0)
    use(last - 1, even, lambda part: make(last, odd, part))
    use(last, odd)
    send_products(slots, y_first, y_second, out)


def second_kernel(
    slots, got, left, right, even, odd, out,
    x_first, x_second, y_first, y_second, t_first, t_second,
):
    npair = left.shape[0]
    near = slots[0, npair]

    def load(q, carry):
        at = pl.ds(pl.multiple_of(q * 8, 8), 8)
        for side, x in ((0, x_first), (1, x_second)):
            u, w = got[slots[side, 2 * q]], got[slots[side, 2 * q + 1]]
            x[at, :] = unfold_two(u.astype(f32), w.astype(f32))
        return carry

    lax.fori_loop(0, npair // 2, load, 0, unroll=4)
    far_products(left, right, x_first, x_second, t_first, t_second, y_first, y_second)

    def near_step(h, carry):
        near_products(2 * h, near, even, x_first, x_second, y_first, y_second)
        near_products(2 * h + 1, near, odd, x_first, x_second, y_first, y_second)
        return carry

    lax.fori_loop(0, NEAR_MOST // 4, near_step, 0, unroll=2)
    send_products(slots, y_first, y_second, out)


LOOSE = 8


def gather_sum(wanted, got, totals):
    for total in totals:
        total[...] = jnp.zeros(total.shape, f32)

    def step(q, carry):
        for k, total in enumerate(totals):
            w = wanted[q * LOOSE + k]
            c = jnp.where(w < 0, CDEV, w)
            total[c] = total[c] + got[q * LOOSE + k].astype(f32)
        return carry

    lax.fori_loop(0, got.shape[0] // LOOSE, step, 0, unroll=2)
    parts = [total[0:CDEV] for total in totals]
    while len(parts) > 1:
        parts = [a + b for a, b in zip(parts[::2], parts[1::2])]
    return parts[0]


def turn_kernel(wanted, got, image, out, half, *totals):
    total = gather_sum(wanted, got, totals)
    image[...] = total
    half[...] = total.astype(bf16)

    def step(s, carry):
        out[s] = half[jnp.maximum(wanted[s], 0)]
        return carry

    lax.fori_loop(0, out.shape[0], step, 0, unroll=16)


def inner(x, y):
    rows = jnp.sum(jnp.sum(x * y, axis=0), axis=1, keepdims=True)
    return rows[0:4] + rows[4:8] + rows[8:12] + rows[12:16]


def gram_kernel(wanted, got, met, rhs, image, second, basis, payload, *totals):
    s = gather_sum(wanted, got, totals)
    second[...] = s
    beta = jnp.sqrt(pick(jnp.sum(met[...], axis=0, keepdims=True), 1) + EPS)
    r = rhs[...] / beta
    for c in range(CDEV):
        basis[c] = fold(r[:, c * CP : (c + 1) * CP])
    v, p = basis[...], image[...]
    row = spread([inner(v, v), inner(v, p), inner(p, p), inner(v, s), inner(p, s), inner(s, s)])
    payload[...] = jnp.broadcast_to(row, payload.shape)


def final_kernel(got, norms, basis, image, second, solution_out, residual_out):
    total = jnp.sum(got[...], axis=0, keepdims=True)
    vv, vp, pp, vs, ps, ss = (pick(total, i) for i in range(6))
    beta = jnp.sqrt(pick(jnp.sum(norms[...], axis=0, keepdims=True), 1) + EPS)
    zero = jnp.zeros_like(vv)
    h11 = vp
    first = jnp.maximum(pp - 2.0 * h11 * vp + h11 * h11 * vv, zero)
    h21 = jnp.sqrt(first + EPS)
    inv = 1.0 / h21
    v1w = (vs - h11 * vp) * inv
    v2w = (ps - h11 * pp - h11 * vs + h11 * h11 * vp) * inv * inv
    ww = (ss - 2.0 * h11 * ps + h11 * h11 * pp) * inv * inv
    v1v2 = (vp - h11 * vv) * inv
    v2v2 = first * inv * inv
    h12, h22 = v1w, v2w
    third = ww + h12 * h12 * vv + h22 * h22 * v2v2
    third = third - 2.0 * h12 * v1w - 2.0 * h22 * v2w + 2.0 * h12 * h22 * v1v2
    h32 = jnp.sqrt(jnp.maximum(third, zero) + EPS)
    rho_one = jnp.sqrt(h11 * h11 + h21 * h21)
    cos_one = h11 / rho_one
    sin_one = h21 / rho_one
    upper = cos_one * h12 + sin_one * h22
    lower = cos_one * h22 - sin_one * h12
    rho_two = jnp.sqrt(lower * lower + h32 * h32)
    coef_two = lower / rho_two * (-sin_one * beta) / rho_two
    coef_one = (cos_one * beta - upper * coef_two) / rho_one
    q_one = beta - h11 * coef_one - h12 * coef_two
    q_two = -h21 * coef_one - h22 * coef_two
    q_three = -h32 * coef_two / h32
    sol_v = coef_one - coef_two * h11 * inv
    sol_p = coef_two * inv
    res_v = q_one - q_two * h11 * inv + q_three * (h22 * h11 * inv - h12)
    res_p = q_two * inv - q_three * (h11 + h22) * inv
    res_s = q_three * inv
    sol_v, sol_p, res_v, res_p, res_s = (
        jnp.concatenate([x, x, x, x], axis=0) for x in (sol_v, sol_p, res_v, res_p, res_s)
    )
    for c in range(CDEV):
        cut = slice(c * CP, (c + 1) * CP)
        v, p, s = basis[c], image[c], second[c]
        solution_out[:, cut] = unfold(sol_v * v + sol_p * p)
        residual_out[:, cut] = unfold(res_v * v + res_p * p + res_s * s)


def shards(right_side, geometry, pairs, near_count, far_left_factor, far_right):
    devices = lax.axis_size(AXES)
    npair = pairs.shape[0]
    nslot = devices * CAP
    width = right_side.shape[1]
    field = (CDEV,) + BLOCK
    plain = (nslot,) + BLOCK
    coded = (nslot, 2 * BLOCK[0], BLOCK[1])

    payload, slots, codes = pl.pallas_call(
        wish_kernel,
        out_shape=(
            sds((devices, 128), f32),
            sds((2, npair + 8), i32),
            sds((CDEV,) + coded[1:], jnp.int16),
        ),
        in_specs=[SMEM] + [VMEM] * 3,
        out_specs=(VMEM,) * 3,
        compiler_params=room(8),
        name="wishes",
    )(near_count, pairs.T, right_side, geometry)
    met = all_to_all(payload.reshape(devices, 1, 128)).reshape(devices, 128)
    wanted = met[:, :CAP].astype(i32).reshape(nslot)

    outgoing, factor = pl.pallas_call(
        pack_kernel,
        out_shape=(sds(coded, jnp.int16), sds((devices, 2 * NRHS, 128), f32)),
        in_specs=[SMEM] + [VMEM] * 2,
        out_specs=(VMEM,) * 2,
        compiler_params=room(8),
        name="pack",
    )(wanted, codes, met)
    incoming = all_to_all(outgoing.reshape(devices, CAP * coded[1], LANES)).reshape(coded)

    work = [pltpu.VMEM((npair * NRHS, CP), f32)] * 4
    work += [pltpu.VMEM((npair * NRHS, GROUP * RANK), bf16)] * 2
    terms = [
        pltpu.VMEM((NEAR_MOST // 2, CP, TERMS), bf16),
        pltpu.VMEM((NEAR_MOST, TERMS, CP), bf16),
    ]
    some = sds((NEAR_MOST // 4, 2, CP, CP), bf16)
    returning, even, odd = pl.pallas_call(
        first_kernel,
        out_shape=(sds(plain, bf16), some, some),
        in_specs=[SMEM] + [VMEM] * 4,
        out_specs=(VMEM,) * 3,
        scratch_shapes=work + terms,
        compiler_params=room(24),
        name="first_operator",
    )(slots, incoming, factor, far_left_factor, far_right)

    def exchange(x):
        return all_to_all(x.reshape(devices, CAP * BLOCK[0], LANES)).reshape(plain)

    totals = [pltpu.VMEM((CDEV + 1,) + BLOCK, f32)] * LOOSE
    image, outgoing = pl.pallas_call(
        turn_kernel,
        out_shape=(sds(field, f32), sds(plain, bf16)),
        in_specs=[SMEM, VMEM],
        out_specs=(VMEM,) * 2,
        scratch_shapes=[pltpu.VMEM(field, bf16)] + totals,
        compiler_params=room(8),
        name="turn",
    )(wanted, exchange(returning))

    returning = pl.pallas_call(
        second_kernel,
        out_shape=sds(plain, bf16),
        in_specs=[SMEM] + [VMEM] * 5,
        out_specs=VMEM,
        scratch_shapes=work,
        compiler_params=room(24),
        name="second_operator",
    )(slots, exchange(outgoing), far_left_factor, far_right, even, odd)

    second, basis, gram = pl.pallas_call(
        gram_kernel,
        out_shape=(sds(field, f32), sds(field, f32), sds((devices, 128), f32)),
        in_specs=[SMEM] + [VMEM] * 4,
        out_specs=(VMEM,) * 3,
        scratch_shapes=totals,
        compiler_params=room(8),
        name="gram",
    )(wanted, exchange(returning), met, right_side, image)
    sums = all_to_all(gram.reshape(devices, 1, 128)).reshape(devices, 128)

    return pl.pallas_call(
        final_kernel,
        out_shape=(sds((NRHS, width), f32),) * 2,
        in_specs=[VMEM] * 5,
        out_specs=(VMEM,) * 2,
        compiler_params=room(8),
        name="combine",
    )(sums, met, basis, image, second)


def solution(mesh):
    spread_last = P(None, AXES)
    return jax.shard_map(
        shards,
        mesh=mesh,
        in_specs=(
            spread_last,
            spread_last,
            P(AXES, None),
            P(AXES),
            P(AXES, None, None),
            P(AXES, None, None),
        ),
        out_specs=(spread_last, spread_last),
        check_vma=False,
    )
```

```python
import functools
import math

import jax
import jax.numpy as jnp
from jax import lax
from jax.experimental import pallas as pl
from jax.experimental.pallas import tpu as pltpu
from jax.sharding import Mesh
from jax.sharding import PartitionSpec as P

CP = 512
RANK = 32
NRHS = 4
CDEV = 8
CORES = 2
CAP = 2 * CORES
CCHIP = CDEV * CORES
NEAR_MOST = 16
GROUP = 8
EPS = 1e-06
CODE = 32767.0
GEO_MID = (0.0, 0.0, 0.0, 0.275)
GEO_HALF = (5.0, 5.0, 5.0, 0.225)
FOUR_PI = 4.0 * math.pi

bf16 = jnp.bfloat16
f32 = jnp.float32
i32 = jnp.int32
AXES = ("chip", "core")
VMEM = pl.BlockSpec(memory_space=pltpu.VMEM)
SMEM = pl.BlockSpec(memory_space=pltpu.SMEM)
BLOCK = (4 * NRHS, CP // 4)
LANES = CP // 4


def room(mib):
    return pltpu.CompilerParams(vmem_limit_bytes=mib * 1024 * 1024)


def sds(shape, dtype):
    return jax.ShapeDtypeStruct(shape, dtype)


def all_to_all(x):
    return lax.all_to_all(x, "chip", split_axis=0, concat_axis=0, tiled=True)


def other_core(x):
    return lax.ppermute(x, "core", [(0, 1), (1, 0)])


def col4(values):
    row = lax.broadcasted_iota(i32, (4, 1), 0)
    out = jnp.full((4, 1), values[3], f32)
    for k in range(3):
        out = jnp.where(row == k, values[k], out)
    return out


def spread(columns):
    lane = lax.broadcasted_iota(i32, (4, 128), 1)
    row = lax.broadcasted_iota(i32, (4, 128), 0)
    out = jnp.zeros((4, 128), f32)
    for i, column in enumerate(columns):
        out = out + jnp.where(lane == 4 * i + row, column, 0.0)
    return jnp.sum(out, axis=0, keepdims=True)


def pick(row_vector, i):
    lane = lax.broadcasted_iota(i32, (4, 128), 1)
    row = lax.broadcasted_iota(i32, (4, 128), 0)
    return jnp.sum(jnp.where(lane == 4 * i + row, row_vector, 0.0), axis=1, keepdims=True)


def fold(x):
    return jnp.concatenate([x[:, k * LANES : (k + 1) * LANES] for k in range(4)], axis=0)


def upper_half():
    return lax.broadcasted_iota(i32, (8, LANES), 0) < 4


def swap(x):
    return pltpu.roll(x, 4, axis=0)


def fold_two(x):
    up = upper_half()
    a, b, c, d = (x[:, k * LANES : (k + 1) * LANES] for k in range(4))
    first = [jnp.where(up, a, swap(b)), jnp.where(up, c, swap(d))]
    second = [jnp.where(up, swap(a), b), jnp.where(up, swap(c), d)]
    return jnp.concatenate(first, axis=0), jnp.concatenate(second, axis=0)


def unfold_two(u, w):
    up = upper_half()
    out = []
    for at in (slice(0, 8), slice(8, 16)):
        out += [jnp.where(up, u[at], swap(w[at])), jnp.where(up, swap(u[at]), w[at])]
    return jnp.concatenate(out, axis=1)


def unfold(x):
    return jnp.concatenate([x[4 * k : 4 * k + 4] for k in range(4)], axis=1)


def wish_kernel(live, pairs, rhs, geometry, payload, slots, codes):
    core = lax.axis_index("core")
    n = pairs.shape[1]
    sub = lax.broadcasted_iota(i32, (n, n), 0)
    lane = lax.broadcasted_iota(i32, (n, n), 1)
    homes, far_cores, locals_, columns = [], [], [], []
    for k in range(2):
        ends = pairs[k : k + 1, :]
        homes.append(ends // CCHIP)
        far_cores.append((ends // CDEV % CORES != core).astype(i32))
        locals_.append(far_cores[k] * CDEV + ends % CDEV)
        columns.append(jnp.sum(jnp.where(sub == lane, homes[k], 0), axis=1, keepdims=True))

    def count(column, row, limit):
        hit = jnp.logical_and(column == row, limit) if limit is not None else column == row
        return jnp.sum(hit.astype(i32), axis=0, keepdims=True)

    earlier = sub < lane
    ranks = [
        count(columns[0], homes[0], earlier),
        count(columns[0], homes[1], None) + count(columns[1], homes[1], earlier),
    ]
    peers = payload.shape[0]
    peer = lax.broadcasted_iota(i32, (peers, n), 0)
    wide = lax.broadcasted_iota(i32, (peers, 128), 1)
    out = jnp.zeros((peers, 128), f32)
    for j in range(CAP):
        wish = jnp.full((peers, 1), -1, i32)
        for k in range(2):
            hit = jnp.logical_and(peer == homes[k], ranks[k] == j)
            wish = wish + jnp.sum(jnp.where(hit, locals_[k] + 1, 0), axis=1, keepdims=True)
        out = jnp.where(wide == j, wish.astype(f32), out)
    for k in range(2):
        slots[k : k + 1, 0:n] = homes[k] * CAP + ranks[k]
        slots[k : k + 1, n : n + 8] = jnp.broadcast_to(live[0], (1, 8))
        slots[2 + k : 3 + k, 0:n] = far_cores[k]
    r = rhs[...]
    squares = jnp.sum(r * r, axis=1, keepdims=True)
    largest = jnp.max(jnp.abs(r), axis=1, keepdims=True)
    payload[...] = out + spread([jnp.zeros((4, 1), f32), squares, largest])
    scale = CODE / jnp.maximum(largest, 1e-30)
    mid, half = col4(GEO_MID), col4([CODE / h for h in GEO_HALF])
    for c in range(CDEV):
        cut = slice(c * CP, (c + 1) * CP)
        both = jnp.concatenate(
            [fold(r[:, cut] * scale), fold((geometry[:, cut] - mid) * half)], axis=0
        )
        both = jnp.minimum(jnp.maximum(both, -CODE), CODE)
        codes[c] = jnp.floor(both + 0.5).astype(i32).astype(jnp.int16)


def pack_kernel(wanted, own, other, out, codes):
    codes[0:CDEV] = own[...]
    codes[CDEV:] = other[...]

    def step(s, carry):
        out[s] = codes[jnp.maximum(wanted[s], 0)]
        return carry

    lax.fori_loop(0, out.shape[0], step, 0, unroll=16)


def start_norm(met, met_other):
    total = jnp.sum(met[...] + met_other[...], axis=0, keepdims=True)
    return jnp.sqrt(pick(total, 1) + EPS)


TRANSPOSED = (((1,), (1,)), ((), ()))


def far_products(left, right, x_first, x_second, t_first, t_second, y_first, y_second):
    rows, wide = GROUP * NRHS, GROUP * RANK
    diagonal = (
        lax.broadcasted_iota(i32, (rows, wide), 0) // NRHS
        == lax.broadcasted_iota(i32, (rows, wide), 1) // RANK
    )
    groups = left.shape[0] // GROUP
    for g in range(groups):
        at = slice(g * rows, (g + 1) * rows)
        for x, factor, t in ((x_second, right, t_first), (x_first, left, t_second)):
            f = factor[g * GROUP : (g + 1) * GROUP].reshape(wide, CP)
            value = lax.dot_general(x[at, :].astype(bf16), f, TRANSPOSED, preferred_element_type=f32)
            t[at, :] = jnp.where(diagonal, value, 0.0).astype(bf16)
    for g in range(groups):
        at = slice(g * rows, (g + 1) * rows)
        for t, factor, y in ((t_first, left, y_first), (t_second, right, y_second)):
            f = factor[g * GROUP : (g + 1) * GROUP].reshape(wide, CP)
            y[at, :] = jnp.dot(t[at, :], f, preferred_element_type=f32)


def near_products(q, near, tiles, x_first, x_second, y_first, y_second, between=None):
    at = pl.ds(pl.multiple_of(q * 8, 8), 8)
    row = lax.broadcasted_iota(i32, (8, CP), 0)
    mine = 2 * q + row // NRHS < near
    x1, x2 = x_first[at, :], x_second[at, :]
    n1 = n2 = 0.0
    for k in range(2):
        tile = tiles[q // 2, k]
        here = row // NRHS == k
        n1 += lax.dot_general(
            jnp.where(here, x2, 0.0).astype(bf16), tile, TRANSPOSED, preferred_element_type=f32
        )
        if between:
            between(2 * k)
        n2 += jnp.dot(jnp.where(here, x1, 0.0).astype(bf16), tile, preferred_element_type=f32)
        if between:
            between(2 * k + 1)
    y_first[at, :] = jnp.where(mine, n1, y_first[at, :])
    y_second[at, :] = jnp.where(mine, n2, y_second[at, :])


def send_products(slots, y_first, y_second, out):
    def step(q, carry):
        at = pl.ds(pl.multiple_of(q * 8, 8), 8)
        for side, y in ((0, y_first), (1, y_second)):
            a, b = fold_two(y[at, :])
            out[slots[side, 2 * q]] = a.astype(bf16)
            out[slots[side, 2 * q + 1]] = b.astype(bf16)
        return carry

    lax.fori_loop(0, y_first.shape[0] // 8, step, 0, unroll=4)


def halves(x, parts):
    out = []
    for _ in range(parts):
        piece = x.astype(bf16).astype(f32)
        out.append(piece)
        x = x - piece
    return out


TERMS = 48


def distance_terms(code, side):
    unit = GEO_HALF[0] / CODE
    row = lax.broadcasted_iota(i32, (8, CP), 0)
    place = row % 4 < 3
    squares = jnp.where(place, code * code, 0.0)
    sizes = (GEO_MID[3] + code * (GEO_HALF[3] / CODE)) * (1.0 / unit**2)
    squares = jnp.where(place, squares, sizes)
    totals = [jnp.sum(squares[k : k + 4], axis=0, keepdims=True) for k in (0, 4)]
    total = jnp.where(row < 4, totals[0], totals[1])
    n1, n2, n3 = halves(total, 3)
    high, low = halves(code, 2)
    one = jnp.ones((8, CP), f32)
    zero = jnp.zeros((8, CP), f32)
    if side == 0:
        parts = [
            jnp.where(place, high, n1), jnp.where(place, high, n2), jnp.where(place, low, n3),
            jnp.where(place, low, one), jnp.where(row % 4 < 2, one, zero),
        ]
    else:
        high, low = -2.0 * high, -2.0 * low
        parts = [
            jnp.where(place, high, one), jnp.where(place, low, one), jnp.where(place, high, one),
            jnp.where(place, low, n1),
            jnp.where(row % 4 == 0, n2, jnp.where(row % 4 == 1, n3, zero)),
        ]
    return jnp.concatenate(parts + [zero], axis=0)


def first_kernel(
    slots, got, met, met_other, left, right, out, even, odd,
    x_first, x_second, y_first, y_second, t_first, t_second, terms_first, terms_second, units,
):
    npair = left.shape[0]
    near = slots[0, npair]
    scale = (1.0 / CODE) / start_norm(met, met_other)
    for n in range(NRHS):
        for k, table in enumerate((met, met_other)):
            unit = table[:, 8 + n : 9 + n] * scale[n : n + 1, :]
            units[n, k] = jnp.broadcast_to(unit, units.shape[2:])
    row = lax.broadcasted_iota(i32, (8, LANES), 0) % NRHS

    def value(side, p):
        s, core = slots[side, p], slots[2 + side, p]
        by = [units[n, core, pl.ds(s // CAP, 1), :] for n in range(NRHS)]
        f = jnp.where(row == 0, by[0], jnp.where(row == 1, by[1], jnp.where(row == 2, by[2], by[3])))
        return got[s, : BLOCK[0]].astype(i32).astype(f32) * jnp.concatenate([f, f], axis=0)

    def load(q, carry):
        at = pl.ds(pl.multiple_of(q * 8, 8), 8)
        for side, x in ((0, x_first), (1, x_second)):
            x[at, :] = unfold_two(value(side, 2 * q), value(side, 2 * q + 1))
        return carry

    lax.fori_loop(0, npair // 2, load, 0, unroll=4)
    term = lax.broadcasted_iota(i32, (TERMS, CP), 0)

    def load_terms(q, carry):
        place = [
            unfold_two(*(got[slots[side, 2 * q + k], BLOCK[0] :].astype(i32).astype(f32) for k in range(2)))
            for side in range(2)
        ]
        terms_first[q] = distance_terms(place[0], 0).T.astype(bf16)
        both = distance_terms(place[1], 1)
        for k in range(2):
            terms_second[2 * q + k] = jnp.where(term % 8 // 4 == k, both, 0.0).astype(bf16)
        return carry

    lax.fori_loop(0, NEAR_MOST // 2, load_terms, 0, unroll=2)
    far_products(left, right, x_first, x_second, t_first, t_second, y_first, y_second)
    unit = CODE / (GEO_HALF[0] * FOUR_PI)

    def make(q, tiles, part):
        k = part // 2
        for cut in range(part % 2 * 256, part % 2 * 256 + 256, 128):
            d = jnp.dot(
                terms_first[q, cut : cut + 128, :], terms_second[2 * q + k],
                preferred_element_type=f32,
            )
            tiles[q // 2, k, cut : cut + 128, :] = (lax.rsqrt(d) * unit).astype(bf16)

    def use(q, tiles, between=None):
        near_products(q, near, tiles, x_first, x_second, y_first, y_second, between)

    def near_step(h, carry):
        use(2 * h, even, lambda part: make(2 * h + 1, odd, part))
        use(2 * h + 1, odd, lambda part: make(2 * h + 2, even, part))
        return carry

    last = NEAR_MOST // 2 - 1
    for part in range(4):
        make(0, even, part)
    lax.fori_loop(0, last // 2, near_step, 0)
    use(last - 1, even, lambda part: make(last, odd, part))
    use(last, odd)
    send_products(slots, y_first, y_second, out)


def second_kernel(
    slots, got, left, right, even, odd, out,
    x_first, x_second, y_first, y_second, t_first, t_second,
):
    npair = left.shape[0]
    near = slots[0, npair]

    def load(q, carry):
        at = pl.ds(pl.multiple_of(q * 8, 8), 8)
        for side, x in ((0, x_first), (1, x_second)):
            u, w = got[slots[side, 2 * q]], got[slots[side, 2 * q + 1]]
            x[at, :] = unfold_two(u.astype(f32), w.astype(f32))
        return carry

    lax.fori_loop(0, npair // 2, load, 0, unroll=4)
    far_products(left, right, x_first, x_second, t_first, t_second, y_first, y_second)

    def near_step(h, carry):
        near_products(2 * h, near, even, x_first, x_second, y_first, y_second)
        near_products(2 * h + 1, near, odd, x_first, x_second, y_first, y_second)
        return carry

    lax.fori_loop(0, NEAR_MOST // 4, near_step, 0, unroll=2)
    send_products(slots, y_first, y_second, out)


LOOSE = 8


def gather_kernel(wanted, got, out, *totals):
    for total in totals:
        total[...] = jnp.zeros(total.shape, f32)

    def step(q, carry):
        for k, total in enumerate(totals):
            w = wanted[q * LOOSE + k]
            c = jnp.where(w < 0, CCHIP, w)
            total[c] = total[c] + got[q * LOOSE + k].astype(f32)
        return carry

    lax.fori_loop(0, got.shape[0] // LOOSE, step, 0, unroll=2)
    parts = [total[0:CCHIP] for total in totals]
    while len(parts) > 1:
        parts = [a + b for a, b in zip(parts[::2], parts[1::2])]
    out[...] = parts[0]


def chip_sum(mine, theirs):
    return jnp.concatenate(
        [mine[0:CDEV] + theirs[CDEV:CCHIP], mine[CDEV:CCHIP] + theirs[0:CDEV]], axis=0
    )


def turn_kernel(wanted, mine, theirs, image, out, half):
    total = chip_sum(mine, theirs)
    image[...] = total
    half[...] = total.astype(bf16)

    def step(s, carry):
        out[s] = half[jnp.maximum(wanted[s], 0)]
        return carry

    lax.fori_loop(0, out.shape[0], step, 0, unroll=16)


def inner(x, y):
    rows = jnp.sum(jnp.sum(x * y, axis=0), axis=1, keepdims=True)
    return rows[0:4] + rows[4:8] + rows[8:12] + rows[12:16]


def gram_kernel(mine, theirs, met, met_other, rhs, rhs_other, image, second, basis, payload, chip):
    s = chip_sum(mine, theirs)
    second[...] = s[0:CDEV]
    beta = start_norm(met, met_other)
    for k, r in enumerate((rhs[...], rhs_other[...])):
        r = r / beta
        for c in range(CDEV):
            chip[k * CDEV + c] = fold(r[:, c * CP : (c + 1) * CP])
    v, p = chip[...], image[...]
    basis[...] = v[0:CDEV]
    row = spread([inner(v, v), inner(v, p), inner(p, p), inner(v, s), inner(p, s), inner(s, s)])
    payload[...] = jnp.broadcast_to(row, payload.shape)


def final_kernel(got, met, met_other, basis, image, second, solution_out, residual_out):
    total = jnp.sum(got[...], axis=0, keepdims=True)
    vv, vp, pp, vs, ps, ss = (pick(total, i) for i in range(6))
    beta = start_norm(met, met_other)
    zero = jnp.zeros_like(vv)
    h11 = vp
    first = jnp.maximum(pp - 2.0 * h11 * vp + h11 * h11 * vv, zero)
    h21 = jnp.sqrt(first + EPS)
    inv = 1.0 / h21
    v1w = (vs - h11 * vp) * inv
    v2w = (ps - h11 * pp - h11 * vs + h11 * h11 * vp) * inv * inv
    ww = (ss - 2.0 * h11 * ps + h11 * h11 * pp) * inv * inv
    v1v2 = (vp - h11 * vv) * inv
    v2v2 = first * inv * inv
    h12, h22 = v1w, v2w
    third = ww + h12 * h12 * vv + h22 * h22 * v2v2
    third = third - 2.0 * h12 * v1w - 2.0 * h22 * v2w + 2.0 * h12 * h22 * v1v2
    h32 = jnp.sqrt(jnp.maximum(third, zero) + EPS)
    rho_one = jnp.sqrt(h11 * h11 + h21 * h21)
    cos_one = h11 / rho_one
    sin_one = h21 / rho_one
    upper = cos_one * h12 + sin_one * h22
    lower = cos_one * h22 - sin_one * h12
    rho_two = jnp.sqrt(lower * lower + h32 * h32)
    coef_two = lower / rho_two * (-sin_one * beta) / rho_two
    coef_one = (cos_one * beta - upper * coef_two) / rho_one
    q_one = beta - h11 * coef_one - h12 * coef_two
    q_two = -h21 * coef_one - h22 * coef_two
    q_three = -h32 * coef_two / h32
    sol_v = coef_one - coef_two * h11 * inv
    sol_p = coef_two * inv
    res_v = q_one - q_two * h11 * inv + q_three * (h22 * h11 * inv - h12)
    res_p = q_two * inv - q_three * (h11 + h22) * inv
    res_s = q_three * inv
    sol_v, sol_p, res_v, res_p, res_s = (
        jnp.concatenate([x, x, x, x], axis=0) for x in (sol_v, sol_p, res_v, res_p, res_s)
    )
    for c in range(CDEV):
        cut = slice(c * CP, (c + 1) * CP)
        v, p, s = basis[c], image[c], second[c]
        solution_out[:, cut] = unfold(sol_v * v + sol_p * p)
        residual_out[:, cut] = unfold(res_v * v + res_p * p + res_s * s)


def shards(right_side, geometry, pairs, near_count, far_left_factor, far_right):
    chips = lax.axis_size("chip")
    npair = pairs.shape[0]
    nslot = chips * CAP
    width = right_side.shape[1]
    own = (CDEV,) + BLOCK
    chip = (CCHIP,) + BLOCK
    plain = (nslot,) + BLOCK
    coded = (nslot, 2 * BLOCK[0], BLOCK[1])

    payload, slots, codes = pl.pallas_call(
        wish_kernel,
        out_shape=(
            sds((chips, 128), f32),
            sds((4, npair + 8), i32),
            sds((CDEV,) + coded[1:], jnp.int16),
        ),
        in_specs=[SMEM] + [VMEM] * 3,
        out_specs=(VMEM,) * 3,
        compiler_params=room(8),
        name="wishes",
    )(near_count, pairs.T, right_side, geometry)
    codes_other = other_core(codes)
    rhs_other = other_core(right_side)
    met = all_to_all(payload.reshape(chips, 1, 128)).reshape(chips, 128)
    met_other = other_core(met)
    wanted = met[:, :CAP].astype(i32).reshape(nslot)

    outgoing = pl.pallas_call(
        pack_kernel,
        out_shape=sds(coded, jnp.int16),
        in_specs=[SMEM] + [VMEM] * 2,
        out_specs=VMEM,
        scratch_shapes=[pltpu.VMEM((CCHIP,) + coded[1:], jnp.int16)],
        compiler_params=room(8),
        name="pack",
    )(wanted, codes, codes_other)
    incoming = all_to_all(outgoing.reshape(chips, CAP * coded[1], LANES)).reshape(coded)

    work = [pltpu.VMEM((npair * NRHS, CP), f32)] * 4
    work += [pltpu.VMEM((npair * NRHS, GROUP * RANK), bf16)] * 2
    terms = [
        pltpu.VMEM((NEAR_MOST // 2, CP, TERMS), bf16),
        pltpu.VMEM((NEAR_MOST, TERMS, CP), bf16),
        pltpu.VMEM((NRHS, CORES, chips, 128), f32),
    ]
    some = sds((NEAR_MOST // 4, 2, CP, CP), bf16)
    returning, even, odd = pl.pallas_call(
        first_kernel,
        out_shape=(sds(plain, bf16), some, some),
        in_specs=[SMEM] + [VMEM] * 5,
        out_specs=(VMEM,) * 3,
        scratch_shapes=work + terms,
        compiler_params=room(24),
        name="first_operator",
    )(slots, incoming, met, met_other, far_left_factor, far_right)

    def exchange(x):
        return all_to_all(x.reshape(chips, CAP * BLOCK[0], LANES)).reshape(plain)

    def gather(x):
        mine = pl.pallas_call(
            gather_kernel,
            out_shape=sds(chip, f32),
            in_specs=[SMEM, VMEM],
            out_specs=VMEM,
            scratch_shapes=[pltpu.VMEM((CCHIP + 1,) + BLOCK, f32)] * LOOSE,
            compiler_params=room(8),
            name="gather",
        )(wanted, exchange(x))
        return mine, other_core(mine)

    image, outgoing = pl.pallas_call(
        turn_kernel,
        out_shape=(sds(chip, f32), sds(plain, bf16)),
        in_specs=[SMEM] + [VMEM] * 2,
        out_specs=(VMEM,) * 2,
        scratch_shapes=[pltpu.VMEM(chip, bf16)],
        compiler_params=room(8),
        name="turn",
    )(wanted, *gather(returning))

    returning = pl.pallas_call(
        second_kernel,
        out_shape=sds(plain, bf16),
        in_specs=[SMEM] + [VMEM] * 5,
        out_specs=VMEM,
        scratch_shapes=work,
        compiler_params=room(24),
        name="second_operator",
    )(slots, exchange(outgoing), far_left_factor, far_right, even, odd)

    second, basis, gram = pl.pallas_call(
        gram_kernel,
        out_shape=(sds(own, f32), sds(own, f32), sds((chips, 128), f32)),
        in_specs=[VMEM] * 7,
        out_specs=(VMEM,) * 3,
        scratch_shapes=[pltpu.VMEM(chip, f32)],
        compiler_params=room(8),
        name="gram",
    )(*gather(returning), met, met_other, right_side, rhs_other, image)
    sums = all_to_all(gram.reshape(chips, 1, 128)).reshape(chips, 128)

    return pl.pallas_call(
        final_kernel,
        out_shape=(sds((NRHS, width), f32),) * 2,
        in_specs=[VMEM] * 6,
        out_specs=(VMEM,) * 2,
        compiler_params=room(8),
        name="combine",
    )(sums, met, met_other, basis, image, second)


def solution(mesh):
    spread_last = P(None, AXES)
    return jax.shard_map(
        shards,
        mesh=Mesh(mesh.devices.reshape(-1, CORES), AXES),
        in_specs=(
            spread_last,
            spread_last,
            P(AXES, None),
            P(AXES),
            P(AXES, None, None),
            P(AXES, None, None),
        ),
        out_specs=(spread_last, spread_last),
        check_vma=False,
    )
```

```python
import functools
import math

import jax
import jax.numpy as jnp
from jax import lax
from jax.experimental import pallas as pl
from jax.experimental.pallas import tpu as pltpu
from jax.sharding import PartitionSpec as P

CP = 512
RANK = 32
NRHS = 4
CDEV = 8
CAP = 2
NEAR_MOST = 16
GROUP = 8
EPS = 1e-06
CODE = 32767.0
GEO_MID = (0.0, 0.0, 0.0, 0.275)
GEO_HALF = (5.0, 5.0, 5.0, 0.225)
FOUR_PI = 4.0 * math.pi

bf16 = jnp.bfloat16
f32 = jnp.float32
i32 = jnp.int32
AXES = ("row", "col")
VMEM = pl.BlockSpec(memory_space=pltpu.VMEM)
SMEM = pl.BlockSpec(memory_space=pltpu.SMEM)
BLOCK = (4 * NRHS, CP // 4)
LANES = CP // 4


def room(mib):
    return pltpu.CompilerParams(vmem_limit_bytes=mib * 1024 * 1024)


def sds(shape, dtype):
    return jax.ShapeDtypeStruct(shape, dtype)


def all_to_all(x):
    return lax.all_to_all(x, AXES, split_axis=0, concat_axis=0, tiled=True)


def col4(values):
    row = lax.broadcasted_iota(i32, (4, 1), 0)
    out = jnp.full((4, 1), values[3], f32)
    for k in range(3):
        out = jnp.where(row == k, values[k], out)
    return out


def spread(columns):
    lane = lax.broadcasted_iota(i32, (4, 128), 1)
    row = lax.broadcasted_iota(i32, (4, 128), 0)
    out = jnp.zeros((4, 128), f32)
    for i, column in enumerate(columns):
        out = out + jnp.where(lane == 4 * i + row, column, 0.0)
    return jnp.sum(out, axis=0, keepdims=True)


def pick(row_vector, i):
    lane = lax.broadcasted_iota(i32, (4, 128), 1)
    row = lax.broadcasted_iota(i32, (4, 128), 0)
    return jnp.sum(jnp.where(lane == 4 * i + row, row_vector, 0.0), axis=1, keepdims=True)


def fold(x):
    return jnp.concatenate([x[:, k * LANES : (k + 1) * LANES] for k in range(4)], axis=0)


def upper_half():
    return lax.broadcasted_iota(i32, (8, LANES), 0) < 4


def swap(x):
    return pltpu.roll(x, 4, axis=0)


def fold_two(x):
    up = upper_half()
    a, b, c, d = (x[:, k * LANES : (k + 1) * LANES] for k in range(4))
    first = [jnp.where(up, a, swap(b)), jnp.where(up, c, swap(d))]
    second = [jnp.where(up, swap(a), b), jnp.where(up, swap(c), d)]
    return jnp.concatenate(first, axis=0), jnp.concatenate(second, axis=0)


def unfold_two(u, w):
    up = upper_half()
    out = []
    for at in (slice(0, 8), slice(8, 16)):
        out += [jnp.where(up, u[at], swap(w[at])), jnp.where(up, swap(u[at]), w[at])]
    return jnp.concatenate(out, axis=1)


def unfold(x):
    return jnp.concatenate([x[4 * k : 4 * k + 4] for k in range(4)], axis=1)


def wish_kernel(live, given, payload, slots, codes):
    n = slots.shape[1] - 8
    sub = lax.broadcasted_iota(i32, (n, n), 0)
    lane = lax.broadcasted_iota(i32, (n, n), 1)
    homes, locals_, columns = [], [], []
    for k in range(2):
        ends = given[8 + k : 9 + k, 0:n].astype(i32)
        homes.append(ends // CDEV)
        locals_.append(ends % CDEV)
        columns.append(jnp.sum(jnp.where(sub == lane, homes[k], 0), axis=1, keepdims=True))

    def count(column, row, limit):
        hit = jnp.logical_and(column == row, limit) if limit is not None else column == row
        return jnp.sum(hit.astype(i32), axis=0, keepdims=True)

    earlier = sub < lane
    ranks = [
        count(columns[0], homes[0], earlier),
        count(columns[0], homes[1], None) + count(columns[1], homes[1], earlier),
    ]
    peers = payload.shape[0]
    peer = lax.broadcasted_iota(i32, (peers, n), 0)
    wide = lax.broadcasted_iota(i32, (peers, 128), 1)
    out = jnp.zeros((peers, 128), f32)
    for j in range(CAP):
        wish = jnp.full((peers, 1), -1, i32)
        for k in range(2):
            hit = jnp.logical_and(peer == homes[k], ranks[k] == j)
            wish = wish + jnp.sum(jnp.where(hit, locals_[k] + 1, 0), axis=1, keepdims=True)
        out = jnp.where(wide == j, wish.astype(f32), out)
    for k in range(2):
        slots[k : k + 1, 0:n] = homes[k] * CAP + ranks[k]
        slots[k : k + 1, n : n + 8] = jnp.broadcast_to(live[0], (1, 8))
    r = given[0:NRHS, :]
    squares = jnp.sum(r * r, axis=1, keepdims=True)
    largest = jnp.max(jnp.abs(r), axis=1, keepdims=True)
    payload[...] = out + spread([jnp.zeros((4, 1), f32), squares, largest, largest])
    scale = CODE / jnp.maximum(largest, 1e-30)
    mid, half = col4(GEO_MID), col4([CODE / h for h in GEO_HALF])
    for c in range(CDEV):
        cut = slice(c * CP, (c + 1) * CP)
        both = jnp.concatenate(
            [fold(r[:, cut] * scale), fold((given[NRHS:8, cut] - mid) * half)], axis=0
        )
        both = jnp.minimum(jnp.maximum(both, -CODE), CODE)
        codes[c] = jnp.floor(both + 0.5).astype(i32).astype(jnp.int16)


def pack_kernel(wanted, codes, met, out, factor):
    columns = met[...].T
    beta = jnp.sqrt(jnp.sum(columns[4:8], axis=1, keepdims=True) + EPS)
    units = columns[8:16] * ((1.0 / CODE) / jnp.concatenate([beta, beta], axis=0))
    for sender in range(met.shape[0]):
        factor[sender] = jnp.broadcast_to(units[:, sender : sender + 1], factor.shape[1:])

    def step(s, carry):
        out[s] = codes[jnp.maximum(wanted[s], 0)]
        return carry

    lax.fori_loop(0, out.shape[0], step, 0, unroll=16)


TRANSPOSED = (((1,), (1,)), ((), ()))


def far_products(near, left, right, x_first, x_second, t_first, t_second, y_first, y_second):
    rows, wide = GROUP * NRHS, GROUP * RANK
    diagonal = (
        lax.broadcasted_iota(i32, (rows, wide), 0) // NRHS
        == lax.broadcasted_iota(i32, (rows, wide), 1) // RANK
    )

    def into_rank(g):
        at = slice(g * rows, (g + 1) * rows)
        for x, factor, t in ((x_second, right, t_first), (x_first, left, t_second)):
            f = factor[g * GROUP : (g + 1) * GROUP].reshape(wide, CP)
            value = lax.dot_general(x[at, :].astype(bf16), f, TRANSPOSED, preferred_element_type=f32)
            t[at, :] = jnp.where(diagonal, value, 0.0).astype(bf16)

    def out_of_rank(g):
        at = slice(g * rows, (g + 1) * rows)
        for t, factor, y in ((t_first, left, y_first), (t_second, right, y_second)):
            f = factor[g * GROUP : (g + 1) * GROUP].reshape(wide, CP)
            y[at, :] = jnp.dot(t[at, :], f, preferred_element_type=f32)

    always = NEAR_MOST // GROUP
    for g in range(always):

        @pl.when(near < (g + 1) * GROUP)
        def _(g=g):
            into_rank(g)
            out_of_rank(g)

    for g in range(always, left.shape[0] // GROUP):
        into_rank(g)
    for g in range(always, left.shape[0] // GROUP):
        out_of_rank(g)


def near_products(q, near, tiles, x_first, x_second, y_first, y_second, between=None):
    at = pl.ds(pl.multiple_of(q * 8, 8), 8)
    row = lax.broadcasted_iota(i32, (8, CP), 0)
    mine = 2 * q + row // NRHS < near
    x1, x2 = x_first[at, :], x_second[at, :]
    n1 = n2 = 0.0
    for k in range(2):
        tile = tiles[q // 2, k]
        here = row // NRHS == k
        n1 += lax.dot_general(
            jnp.where(here, x2, 0.0).astype(bf16), tile, TRANSPOSED, preferred_element_type=f32
        )
        if between:
            between(2 * k)
        n2 += jnp.dot(jnp.where(here, x1, 0.0).astype(bf16), tile, preferred_element_type=f32)
        if between:
            between(2 * k + 1)
    y_first[at, :] = jnp.where(mine, n1, y_first[at, :])
    y_second[at, :] = jnp.where(mine, n2, y_second[at, :])


def send_products(slots, y_first, y_second, out):
    def step(q, carry):
        at = pl.ds(pl.multiple_of(q * 8, 8), 8)
        for side, y in ((0, y_first), (1, y_second)):
            a, b = fold_two(y[at, :])
            out[slots[side, 2 * q]] = a.astype(bf16)
            out[slots[side, 2 * q + 1]] = b.astype(bf16)
        return carry

    lax.fori_loop(0, y_first.shape[0] // 8, step, 0, unroll=4)


def halves(x, parts):
    out = []
    for _ in range(parts):
        piece = x.astype(bf16).astype(f32)
        out.append(piece)
        x = x - piece
    return out


TERMS = 48


def distance_terms(code, side):
    unit = GEO_HALF[0] / CODE
    row = lax.broadcasted_iota(i32, (8, CP), 0)
    place = row % 4 < 3
    squares = jnp.where(place, code * code, 0.0)
    sizes = (GEO_MID[3] + code * (GEO_HALF[3] / CODE)) * (1.0 / unit**2)
    squares = jnp.where(place, squares, sizes)
    totals = [jnp.sum(squares[k : k + 4], axis=0, keepdims=True) for k in (0, 4)]
    total = jnp.where(row < 4, totals[0], totals[1])
    n1, n2, n3 = halves(total, 3)
    high, low = halves(code, 2)
    one = jnp.ones((8, CP), f32)
    zero = jnp.zeros((8, CP), f32)
    if side == 0:
        parts = [
            jnp.where(place, high, n1), jnp.where(place, high, n2), jnp.where(place, low, n3),
            jnp.where(place, low, one), jnp.where(row % 4 < 2, one, zero),
        ]
    else:
        high, low = -2.0 * high, -2.0 * low
        parts = [
            jnp.where(place, high, one), jnp.where(place, low, one), jnp.where(place, high, one),
            jnp.where(place, low, n1),
            jnp.where(row % 4 == 0, n2, jnp.where(row % 4 == 1, n3, zero)),
        ]
    return jnp.concatenate(parts + [zero], axis=0)


def first_kernel(
    slots, got, factor, left, right, out, even, odd,
    x_first, x_second, y_first, y_second, t_first, t_second, terms_first, terms_second,
):
    npair = left.shape[0]
    near = slots[0, npair]

    def load(q, carry):
        at = pl.ds(pl.multiple_of(q * 8, 8), 8)
        for side, x in ((0, x_first), (1, x_second)):
            s, t = slots[side, 2 * q], slots[side, 2 * q + 1]
            f, g = factor[s // CAP], factor[t // CAP]
            u = got[s, : BLOCK[0]].astype(i32).astype(f32) * jnp.concatenate([f, f], axis=0)
            w = got[t, : BLOCK[0]].astype(i32).astype(f32) * jnp.concatenate([g, g], axis=0)
            x[at, :] = unfold_two(u, w)
        return carry

    lax.fori_loop(0, npair // 2, load, 0, unroll=4)
    term = lax.broadcasted_iota(i32, (TERMS, CP), 0)

    def load_terms(q, carry):
        place = [
            unfold_two(*(got[slots[side, 2 * q + k], BLOCK[0] :].astype(i32).astype(f32) for k in range(2)))
            for side in range(2)
        ]
        terms_first[q] = distance_terms(place[0], 0).T.astype(bf16)
        both = distance_terms(place[1], 1)
        for k in range(2):
            terms_second[2 * q + k] = jnp.where(term % 8 // 4 == k, both, 0.0).astype(bf16)
        return carry

    lax.fori_loop(0, NEAR_MOST // 2, load_terms, 0, unroll=2)
    far_products(near, left, right, x_first, x_second, t_first, t_second, y_first, y_second)
    unit = CODE / (GEO_HALF[0] * FOUR_PI)

    def make(q, tiles, part):
        k = part // 2
        for cut in range(part % 2 * 256, part % 2 * 256 + 256, 128):
            d = jnp.dot(
                terms_first[q, cut : cut + 128, :], terms_second[2 * q + k],
                preferred_element_type=f32,
            )
            tiles[q // 2, k, cut : cut + 128, :] = (lax.rsqrt(d) * unit).astype(bf16)

    def use(q, tiles, between=None):
        near_products(q, near, tiles, x_first, x_second, y_first, y_second, between)

    def near_step(h, carry):
        use(2 * h, even, lambda part: make(2 * h + 1, odd, part))
        use(2 * h + 1, odd, lambda part: make(2 * h + 2, even, part))
        return carry

    last = NEAR_MOST // 2 - 1
    for part in range(4):
        make(0, even, part)
    lax.fori_loop(0, last // 2, near_step, 0)
    use(last - 1, even, lambda part: make(last, odd, part))
    use(last, odd)
    send_products(slots, y_first, y_second, out)


def second_kernel(
    slots, got, left, right, even, odd, out,
    x_first, x_second, y_first, y_second, t_first, t_second,
):
    npair = left.shape[0]
    near = slots[0, npair]

    def load(q, carry):
        at = pl.ds(pl.multiple_of(q * 8, 8), 8)
        for side, x in ((0, x_first), (1, x_second)):
            u, w = got[slots[side, 2 * q]], got[slots[side, 2 * q + 1]]
            x[at, :] = unfold_two(u.astype(f32), w.astype(f32))
        return carry

    lax.fori_loop(0, npair // 2, load, 0, unroll=4)
    far_products(near, left, right, x_first, x_second, t_first, t_second, y_first, y_second)

    def near_step(h, carry):
        near_products(2 * h, near, even, x_first, x_second, y_first, y_second)
        near_products(2 * h + 1, near, odd, x_first, x_second, y_first, y_second)
        return carry

    lax.fori_loop(0, NEAR_MOST // 4, near_step, 0, unroll=2)
    send_products(slots, y_first, y_second, out)


LOOSE = 4


def gather_sum(wanted, got, totals):
    for total in totals:
        total[...] = jnp.zeros(total.shape, f32)

    def step(q, carry):
        for k, total in enumerate(totals):
            w = wanted[q * LOOSE + k]
            c = jnp.where(w < 0, CDEV, w)
            total[c] = total[c] + got[q * LOOSE + k].astype(f32)
        return carry

    lax.fori_loop(0, got.shape[0] // LOOSE, step, 0, unroll=4)
    parts = [total[0:CDEV] for total in totals]
    while len(parts) > 1:
        parts = [a + b for a, b in zip(parts[::2], parts[1::2])]
    return parts[0]


def turn_kernel(wanted, got, image, out, half, *totals):
    total = gather_sum(wanted, got, totals)
    image[...] = total
    half[...] = total.astype(bf16)

    def step(s, carry):
        out[s] = half[jnp.maximum(wanted[s], 0)]
        return carry

    lax.fori_loop(0, out.shape[0], step, 0, unroll=16)


def inner(x, y):
    rows = jnp.sum(jnp.sum(x * y, axis=0), axis=1, keepdims=True)
    return rows[0:4] + rows[4:8] + rows[8:12] + rows[12:16]


def gram_kernel(wanted, got, met, rhs, image, second, basis, payload, *totals):
    s = gather_sum(wanted, got, totals)
    second[...] = s
    beta = jnp.sqrt(pick(jnp.sum(met[...], axis=0, keepdims=True), 1) + EPS)
    r = rhs[...] / beta
    for c in range(CDEV):
        basis[c] = fold(r[:, c * CP : (c + 1) * CP])
    v, p = basis[...], image[...]
    row = spread([inner(v, v), inner(v, p), inner(p, p), inner(v, s), inner(p, s), inner(s, s)])
    payload[...] = jnp.broadcast_to(row, payload.shape)


def final_kernel(got, norms, basis, image, second, solution_out, residual_out):
    total = jnp.sum(got[...], axis=0, keepdims=True)
    vv, vp, pp, vs, ps, ss = (pick(total, i) for i in range(6))
    beta = jnp.sqrt(pick(jnp.sum(norms[...], axis=0, keepdims=True), 1) + EPS)
    zero = jnp.zeros_like(vv)
    h11 = vp
    first = jnp.maximum(pp - 2.0 * h11 * vp + h11 * h11 * vv, zero)
    h21 = jnp.sqrt(first + EPS)
    inv = 1.0 / h21
    v1w = (vs - h11 * vp) * inv
    v2w = (ps - h11 * pp - h11 * vs + h11 * h11 * vp) * inv * inv
    ww = (ss - 2.0 * h11 * ps + h11 * h11 * pp) * inv * inv
    v1v2 = (vp - h11 * vv) * inv
    v2v2 = first * inv * inv
    h12, h22 = v1w, v2w
    third = ww + h12 * h12 * vv + h22 * h22 * v2v2
    third = third - 2.0 * h12 * v1w - 2.0 * h22 * v2w + 2.0 * h12 * h22 * v1v2
    h32 = jnp.sqrt(jnp.maximum(third, zero) + EPS)
    rho_one = jnp.sqrt(h11 * h11 + h21 * h21)
    cos_one = h11 / rho_one
    sin_one = h21 / rho_one
    upper = cos_one * h12 + sin_one * h22
    lower = cos_one * h22 - sin_one * h12
    rho_two = jnp.sqrt(lower * lower + h32 * h32)
    coef_two = lower / rho_two * (-sin_one * beta) / rho_two
    coef_one = (cos_one * beta - upper * coef_two) / rho_one
    q_one = beta - h11 * coef_one - h12 * coef_two
    q_two = -h21 * coef_one - h22 * coef_two
    q_three = -h32 * coef_two / h32
    sol_v = coef_one - coef_two * h11 * inv
    sol_p = coef_two * inv
    res_v = q_one - q_two * h11 * inv + q_three * (h22 * h11 * inv - h12)
    res_p = q_two * inv - q_three * (h11 + h22) * inv
    res_s = q_three * inv
    sol_v, sol_p, res_v, res_p, res_s = (
        jnp.concatenate([x, x, x, x], axis=0) for x in (sol_v, sol_p, res_v, res_p, res_s)
    )
    for c in range(CDEV):
        cut = slice(c * CP, (c + 1) * CP)
        v, p, s = basis[c], image[c], second[c]
        solution_out[:, cut] = unfold(sol_v * v + sol_p * p)
        residual_out[:, cut] = unfold(res_v * v + res_p * p + res_s * s)


def shards(right_side, geometry, pairs, near_count, far_left_factor, far_right):
    devices = lax.axis_size(AXES)
    npair = pairs.shape[0]
    nslot = devices * CAP
    width = right_side.shape[1]
    field = (CDEV,) + BLOCK
    plain = (nslot,) + BLOCK
    coded = (nslot, 2 * BLOCK[0], BLOCK[1])

    ends = jnp.pad(pairs.T.astype(f32), ((0, 6), (0, width - npair)))
    given = jnp.concatenate([right_side, geometry, ends], axis=0)
    payload, slots, codes = pl.pallas_call(
        wish_kernel,
        out_shape=(
            sds((devices, 128), f32),
            sds((2, npair + 8), i32),
            sds((CDEV,) + coded[1:], jnp.int16),
        ),
        in_specs=[SMEM, VMEM],
        out_specs=(VMEM,) * 3,
        compiler_params=room(8),
        name="wishes",
    )(near_count, given)
    met = all_to_all(payload.reshape(devices, 1, 128)).reshape(devices, 128)
    wanted = met[:, :CAP].astype(i32).reshape(nslot)

    outgoing, factor = pl.pallas_call(
        pack_kernel,
        out_shape=(sds(coded, jnp.int16), sds((devices, 2 * NRHS, 128), f32)),
        in_specs=[SMEM] + [VMEM] * 2,
        out_specs=(VMEM,) * 2,
        compiler_params=room(8),
        name="pack",
    )(wanted, codes, met)
    incoming = all_to_all(outgoing.reshape(devices, CAP * coded[1], LANES)).reshape(coded)

    work = [pltpu.VMEM((npair * NRHS, CP), f32)] * 4
    work += [pltpu.VMEM((npair * NRHS, GROUP * RANK), bf16)] * 2
    terms = [
        pltpu.VMEM((NEAR_MOST // 2, CP, TERMS), bf16),
        pltpu.VMEM((NEAR_MOST, TERMS, CP), bf16),
    ]
    some = sds((NEAR_MOST // 4, 2, CP, CP), bf16)
    returning, even, odd = pl.pallas_call(
        first_kernel,
        out_shape=(sds(plain, bf16), some, some),
        in_specs=[SMEM] + [VMEM] * 4,
        out_specs=(VMEM,) * 3,
        scratch_shapes=work + terms,
        compiler_params=room(24),
        name="first_operator",
    )(slots, incoming, factor, far_left_factor, far_right)

    def exchange(x):
        return all_to_all(x.reshape(devices, CAP * BLOCK[0], LANES)).reshape(plain)

    totals = [pltpu.VMEM((CDEV + 1,) + BLOCK, f32)] * LOOSE
    image, outgoing = pl.pallas_call(
        turn_kernel,
        out_shape=(sds(field, f32), sds(plain, bf16)),
        in_specs=[SMEM, VMEM],
        out_specs=(VMEM,) * 2,
        scratch_shapes=[pltpu.VMEM(field, bf16)] + totals,
        compiler_params=room(8),
        name="turn",
    )(wanted, exchange(returning))

    returning = pl.pallas_call(
        second_kernel,
        out_shape=sds(plain, bf16),
        in_specs=[SMEM] + [VMEM] * 5,
        out_specs=VMEM,
        scratch_shapes=work,
        compiler_params=room(24),
        name="second_operator",
    )(slots, exchange(outgoing), far_left_factor, far_right, even, odd)

    second, basis, gram = pl.pallas_call(
        gram_kernel,
        out_shape=(sds(field, f32), sds(field, f32), sds((devices, 128), f32)),
        in_specs=[SMEM] + [VMEM] * 4,
        out_specs=(VMEM,) * 3,
        scratch_shapes=totals,
        compiler_params=room(8),
        name="gram",
    )(wanted, exchange(returning), met, right_side, image)
    sums = all_to_all(gram.reshape(devices, 1, 128)).reshape(devices, 128)

    return pl.pallas_call(
        final_kernel,
        out_shape=(sds((NRHS, width), f32),) * 2,
        in_specs=[VMEM] * 5,
        out_specs=(VMEM,) * 2,
        compiler_params=room(8),
        name="combine",
    )(sums, met, basis, image, second)


def solution(mesh):
    spread_last = P(None, AXES)
    return jax.shard_map(
        shards,
        mesh=mesh,
        in_specs=(
            spread_last,
            spread_last,
            P(AXES, None),
            P(AXES),
            P(AXES, None, None),
            P(AXES, None, None),
        ),
        out_specs=(spread_last, spread_last),
        check_vma=False,
    )
```

```python
import functools
import math

import jax
import jax.numpy as jnp
from jax import lax
from jax.experimental import pallas as pl
from jax.experimental.pallas import tpu as pltpu
from jax.sharding import PartitionSpec as P

CP = 512
RANK = 32
NRHS = 4
CDEV = 8
CAP = 2
NEAR_MOST = 16
GROUP = 8
EPS = 1e-06
CODE = 32767.0
GEO_MID = (0.0, 0.0, 0.0, 0.275)
GEO_HALF = (5.0, 5.0, 5.0, 0.225)
FOUR_PI = 4.0 * math.pi

bf16 = jnp.bfloat16
f32 = jnp.float32
i32 = jnp.int32
AXES = ("row", "col")
VMEM = pl.BlockSpec(memory_space=pltpu.VMEM)
SMEM = pl.BlockSpec(memory_space=pltpu.SMEM)
BLOCK = (4 * NRHS, CP // 4)
LANES = CP // 4


def room(mib):
    return pltpu.CompilerParams(vmem_limit_bytes=mib * 1024 * 1024)


def sds(shape, dtype):
    return jax.ShapeDtypeStruct(shape, dtype)


def all_to_all(x):
    return lax.all_to_all(x, AXES, split_axis=0, concat_axis=0, tiled=True)


def col4(values):
    row = lax.broadcasted_iota(i32, (4, 1), 0)
    out = jnp.full((4, 1), values[3], f32)
    for k in range(3):
        out = jnp.where(row == k, values[k], out)
    return out


def spread(columns):
    lane = lax.broadcasted_iota(i32, (4, 128), 1)
    row = lax.broadcasted_iota(i32, (4, 128), 0)
    out = jnp.zeros((4, 128), f32)
    for i, column in enumerate(columns):
        out = out + jnp.where(lane == 4 * i + row, column, 0.0)
    return jnp.sum(out, axis=0, keepdims=True)


def pick(row_vector, i):
    lane = lax.broadcasted_iota(i32, (4, 128), 1)
    row = lax.broadcasted_iota(i32, (4, 128), 0)
    return jnp.sum(jnp.where(lane == 4 * i + row, row_vector, 0.0), axis=1, keepdims=True)


def fold(x):
    return jnp.concatenate([x[:, k * LANES : (k + 1) * LANES] for k in range(4)], axis=0)


def upper_half():
    return lax.broadcasted_iota(i32, (8, LANES), 0) < 4


def swap(x):
    return pltpu.roll(x, 4, axis=0)


def fold_two(x):
    up = upper_half()
    a, b, c, d = (x[:, k * LANES : (k + 1) * LANES] for k in range(4))
    first = [jnp.where(up, a, swap(b)), jnp.where(up, c, swap(d))]
    second = [jnp.where(up, swap(a), b), jnp.where(up, swap(c), d)]
    return jnp.concatenate(first, axis=0), jnp.concatenate(second, axis=0)


def unfold_two(u, w):
    up = upper_half()
    out = []
    for at in (slice(0, 8), slice(8, 16)):
        out += [jnp.where(up, u[at], swap(w[at])), jnp.where(up, swap(u[at]), w[at])]
    return jnp.concatenate(out, axis=1)


def unfold(x):
    return jnp.concatenate([x[4 * k : 4 * k + 4] for k in range(4)], axis=1)


def wish_kernel(live, given, payload, slots, codes):
    n = slots.shape[1] - 8
    sub = lax.broadcasted_iota(i32, (n, n), 0)
    lane = lax.broadcasted_iota(i32, (n, n), 1)
    homes, locals_, columns = [], [], []
    for k in range(2):
        ends = given[8 + k : 9 + k, 0:n].astype(i32)
        homes.append(ends // CDEV)
        locals_.append(ends % CDEV)
        columns.append(jnp.sum(jnp.where(sub == lane, homes[k], 0), axis=1, keepdims=True))

    def count(column, row, limit):
        hit = jnp.logical_and(column == row, limit) if limit is not None else column == row
        return jnp.sum(hit.astype(i32), axis=0, keepdims=True)

    earlier = sub < lane
    ranks = [
        count(columns[0], homes[0], earlier),
        count(columns[0], homes[1], None) + count(columns[1], homes[1], earlier),
    ]
    peers = payload.shape[0]
    peer = lax.broadcasted_iota(i32, (peers, n), 0)
    wide = lax.broadcasted_iota(i32, (peers, 128), 1)
    out = jnp.zeros((peers, 128), f32)
    for j in range(CAP):
        wish = jnp.full((peers, 1), -1, i32)
        for k in range(2):
            hit = jnp.logical_and(peer == homes[k], ranks[k] == j)
            wish = wish + jnp.sum(jnp.where(hit, locals_[k] + 1, 0), axis=1, keepdims=True)
        out = jnp.where(wide == j, wish.astype(f32), out)
    for k in range(2):
        slots[k : k + 1, 0:n] = homes[k] * CAP + ranks[k]
        slots[k : k + 1, n : n + 8] = jnp.broadcast_to(live[0], (1, 8))
    r = given[0:NRHS, :]
    squares = jnp.sum(r * r, axis=1, keepdims=True)
    largest = jnp.max(jnp.abs(r), axis=1, keepdims=True)
    payload[...] = out + spread([jnp.zeros((4, 1), f32), squares, largest, largest])
    scale = CODE / jnp.maximum(largest, 1e-30)
    mid, half = col4(GEO_MID), col4([CODE / h for h in GEO_HALF])
    for c in range(CDEV):
        cut = slice(c * CP, (c + 1) * CP)
        both = jnp.concatenate(
            [fold(r[:, cut] * scale), fold((given[NRHS:8, cut] - mid) * half)], axis=0
        )
        both = jnp.minimum(jnp.maximum(both, -CODE), CODE)
        codes[c] = jnp.floor(both + 0.5).astype(i32).astype(jnp.int16)


def pack_kernel(wishes, codes, met, out, factor, wanted, sem):
    table = pltpu.make_async_copy(wishes, wanted, sem)
    table.start()
    columns = met[...].T
    beta = jnp.sqrt(jnp.sum(columns[4:8], axis=1, keepdims=True) + EPS)
    units = columns[8:16] * ((1.0 / CODE) / jnp.concatenate([beta, beta], axis=0))
    for sender in range(met.shape[0]):
        factor[sender] = jnp.broadcast_to(units[:, sender : sender + 1], factor.shape[1:])
    table.wait()

    def step(s, carry):
        out[s] = codes[jnp.maximum(wanted[s], 0)]
        return carry

    lax.fori_loop(0, out.shape[0], step, 0, unroll=16)


TRANSPOSED = (((1,), (1,)), ((), ()))


def far_products(left, right, x_first, x_second, t_first, t_second, y_first, y_second):
    rows, wide = GROUP * NRHS, GROUP * RANK
    diagonal = (
        lax.broadcasted_iota(i32, (rows, wide), 0) // NRHS
        == lax.broadcasted_iota(i32, (rows, wide), 1) // RANK
    )

    def into_rank(g):
        at = slice(g * rows, (g + 1) * rows)
        for x, factor, t in ((x_second, right, t_first), (x_first, left, t_second)):
            f = factor[g * GROUP : (g + 1) * GROUP].reshape(wide, CP)
            value = lax.dot_general(x[at, :].astype(bf16), f, TRANSPOSED, preferred_element_type=f32)
            t[at, :] = jnp.where(diagonal, value, 0.0).astype(bf16)

    def out_of_rank(g):
        at = slice(g * rows, (g + 1) * rows)
        for t, factor, y in ((t_first, left, y_first), (t_second, right, y_second)):
            f = factor[g * GROUP : (g + 1) * GROUP].reshape(wide, CP)
            y[at, :] = jnp.dot(t[at, :], f, preferred_element_type=f32)

    groups = left.shape[0] // GROUP
    for g in range(groups):
        into_rank(g)
    for g in range(groups):
        out_of_rank(g)


def near_products(q, near, tiles, x_first, x_second, y_first, y_second, between=None):
    at = pl.ds(pl.multiple_of(q * 8, 8), 8)
    row = lax.broadcasted_iota(i32, (8, CP), 0)
    mine = 2 * q + row // NRHS < near
    x1, x2 = x_first[at, :], x_second[at, :]
    n1 = n2 = 0.0
    for k in range(2):
        tile = tiles[q // 2, k]
        here = row // NRHS == k
        n1 += lax.dot_general(
            jnp.where(here, x2, 0.0).astype(bf16), tile, TRANSPOSED, preferred_element_type=f32
        )
        if between:
            between(2 * k)
        n2 += jnp.dot(jnp.where(here, x1, 0.0).astype(bf16), tile, preferred_element_type=f32)
        if between:
            between(2 * k + 1)
    y_first[at, :] = jnp.where(mine, n1, y_first[at, :])
    y_second[at, :] = jnp.where(mine, n2, y_second[at, :])


def send_products(slots, y_first, y_second, out):
    def step(q, carry):
        at = pl.ds(pl.multiple_of(q * 8, 8), 8)
        for side, y in ((0, y_first), (1, y_second)):
            a, b = fold_two(y[at, :])
            out[slots[side, 2 * q]] = a.astype(bf16)
            out[slots[side, 2 * q + 1]] = b.astype(bf16)
        return carry

    lax.fori_loop(0, y_first.shape[0] // 8, step, 0, unroll=4)


def halves(x, parts):
    out = []
    for _ in range(parts):
        piece = x.astype(bf16).astype(f32)
        out.append(piece)
        x = x - piece
    return out


TERMS = 48


def distance_terms(code, side):
    unit = GEO_HALF[0] / CODE
    row = lax.broadcasted_iota(i32, (8, CP), 0)
    place = row % 4 < 3
    squares = jnp.where(place, code * code, 0.0)
    sizes = (GEO_MID[3] + code * (GEO_HALF[3] / CODE)) * (1.0 / unit**2)
    squares = jnp.where(place, squares, sizes)
    totals = [jnp.sum(squares[k : k + 4], axis=0, keepdims=True) for k in (0, 4)]
    total = jnp.where(row < 4, totals[0], totals[1])
    n1, n2, n3 = halves(total, 3)
    high, low = halves(code, 2)
    one = jnp.ones((8, CP), f32)
    zero = jnp.zeros((8, CP), f32)
    if side == 0:
        parts = [
            jnp.where(place, high, n1), jnp.where(place, high, n2), jnp.where(place, low, n3),
            jnp.where(place, low, one), jnp.where(row % 4 < 2, one, zero),
        ]
    else:
        high, low = -2.0 * high, -2.0 * low
        parts = [
            jnp.where(place, high, one), jnp.where(place, low, one), jnp.where(place, high, one),
            jnp.where(place, low, n1),
            jnp.where(row % 4 == 0, n2, jnp.where(row % 4 == 1, n3, zero)),
        ]
    return jnp.concatenate(parts + [zero], axis=0)


def first_kernel(
    slots, got, factor, left, right, out, even, odd,
    x_first, x_second, y_first, y_second, t_first, t_second, terms_first, terms_second,
):
    npair = left.shape[0]
    near = slots[0, npair]

    def load(q, carry):
        at = pl.ds(pl.multiple_of(q * 8, 8), 8)
        for side, x in ((0, x_first), (1, x_second)):
            s, t = slots[side, 2 * q], slots[side, 2 * q + 1]
            f, g = factor[s // CAP], factor[t // CAP]
            u = got[s, : BLOCK[0]].astype(i32).astype(f32) * jnp.concatenate([f, f], axis=0)
            w = got[t, : BLOCK[0]].astype(i32).astype(f32) * jnp.concatenate([g, g], axis=0)
            x[at, :] = unfold_two(u, w)
        return carry

    lax.fori_loop(0, npair // 2, load, 0, unroll=4)
    term = lax.broadcasted_iota(i32, (TERMS, CP), 0)

    def load_terms(q, carry):
        place = [
            unfold_two(*(got[slots[side, 2 * q + k], BLOCK[0] :].astype(i32).astype(f32) for k in range(2)))
            for side in range(2)
        ]
        terms_first[q] = distance_terms(place[0], 0).T.astype(bf16)
        both = distance_terms(place[1], 1)
        for k in range(2):
            terms_second[2 * q + k] = jnp.where(term % 8 // 4 == k, both, 0.0).astype(bf16)
        return carry

    lax.fori_loop(0, NEAR_MOST // 2, load_terms, 0, unroll=2)
    far_products(left, right, x_first, x_second, t_first, t_second, y_first, y_second)
    unit = CODE / (GEO_HALF[0] * FOUR_PI)

    def make(q, tiles, part):
        k = part // 2
        for cut in range(part % 2 * 256, part % 2 * 256 + 256, 128):
            d = jnp.dot(
                terms_first[q, cut : cut + 128, :], terms_second[2 * q + k],
                preferred_element_type=f32,
            )
            tiles[q // 2, k, cut : cut + 128, :] = (lax.rsqrt(d) * unit).astype(bf16)

    def use(q, tiles, between=None):
        near_products(q, near, tiles, x_first, x_second, y_first, y_second, between)

    def near_step(h, carry):
        use(2 * h, even, lambda part: make(2 * h + 1, odd, part))
        use(2 * h + 1, odd, lambda part: make(2 * h + 2, even, part))
        return carry

    last = NEAR_MOST // 2 - 1
    for part in range(4):
        make(0, even, part)
    lax.fori_loop(0, last // 2, near_step, 0)
    use(last - 1, even, lambda part: make(last, odd, part))
    use(last, odd)
    send_products(slots, y_first, y_second, out)


def second_kernel(
    slots, got, left, right, even, odd, out,
    x_first, x_second, y_first, y_second, t_first, t_second,
):
    npair = left.shape[0]
    near = slots[0, npair]

    def load(q, carry):
        at = pl.ds(pl.multiple_of(q * 8, 8), 8)
        for side, x in ((0, x_first), (1, x_second)):
            u, w = got[slots[side, 2 * q]], got[slots[side, 2 * q + 1]]
            x[at, :] = unfold_two(u.astype(f32), w.astype(f32))
        return carry

    lax.fori_loop(0, npair // 2, load, 0, unroll=4)
    far_products(left, right, x_first, x_second, t_first, t_second, y_first, y_second)

    def near_step(h, carry):
        near_products(2 * h, near, even, x_first, x_second, y_first, y_second)
        near_products(2 * h + 1, near, odd, x_first, x_second, y_first, y_second)
        return carry

    lax.fori_loop(0, NEAR_MOST // 4, near_step, 0, unroll=2)
    send_products(slots, y_first, y_second, out)


LOOSE = 4


def clear(totals):
    for total in totals:
        total[...] = jnp.zeros(total.shape, f32)


def gather_sum(wanted, got, totals):
    def step(q, carry):
        for k, total in enumerate(totals):
            w = wanted[q * LOOSE + k]
            c = jnp.where(w < 0, CDEV, w)
            total[c] = total[c] + got[q * LOOSE + k].astype(f32)
        return carry

    lax.fori_loop(0, got.shape[0] // LOOSE, step, 0, unroll=4)
    parts = [total[0:CDEV] for total in totals]
    while len(parts) > 1:
        parts = [a + b for a, b in zip(parts[::2], parts[1::2])]
    return parts[0]


def turn_kernel(wishes, got, image, out, half, wanted, sem, *totals):
    table = pltpu.make_async_copy(wishes, wanted, sem)
    table.start()
    clear(totals)
    table.wait()
    total = gather_sum(wanted, got, totals)
    image[...] = total
    half[...] = total.astype(bf16)

    def step(s, carry):
        out[s] = half[jnp.maximum(wanted[s], 0)]
        return carry

    lax.fori_loop(0, out.shape[0], step, 0, unroll=16)


def inner(x, y):
    rows = jnp.sum(jnp.sum(x * y, axis=0), axis=1, keepdims=True)
    return rows[0:4] + rows[4:8] + rows[8:12] + rows[12:16]


def gram_kernel(wishes, got, met, rhs, image, second, basis, payload, wanted, sem, *totals):
    table = pltpu.make_async_copy(wishes, wanted, sem)
    table.start()
    clear(totals)
    beta = jnp.sqrt(pick(jnp.sum(met[...], axis=0, keepdims=True), 1) + EPS)
    r = rhs[...] / beta
    for c in range(CDEV):
        basis[c] = fold(r[:, c * CP : (c + 1) * CP])
    v, p = basis[...], image[...]
    known = [inner(v, v), inner(v, p), inner(p, p)]
    table.wait()
    s = gather_sum(wanted, got, totals)
    second[...] = s
    row = spread(known + [inner(v, s), inner(p, s), inner(s, s)])
    payload[...] = jnp.broadcast_to(row, payload.shape)


def final_kernel(got, norms, basis, image, second, solution_out, residual_out):
    total = jnp.sum(got[...], axis=0, keepdims=True)
    vv, vp, pp, vs, ps, ss = (pick(total, i) for i in range(6))
    beta = jnp.sqrt(pick(jnp.sum(norms[...], axis=0, keepdims=True), 1) + EPS)
    zero = jnp.zeros_like(vv)
    h11 = vp
    first = jnp.maximum(pp - 2.0 * h11 * vp + h11 * h11 * vv, zero)
    h21 = jnp.sqrt(first + EPS)
    inv = 1.0 / h21
    v1w = (vs - h11 * vp) * inv
    v2w = (ps - h11 * pp - h11 * vs + h11 * h11 * vp) * inv * inv
    ww = (ss - 2.0 * h11 * ps + h11 * h11 * pp) * inv * inv
    v1v2 = (vp - h11 * vv) * inv
    v2v2 = first * inv * inv
    h12, h22 = v1w, v2w
    third = ww + h12 * h12 * vv + h22 * h22 * v2v2
    third = third - 2.0 * h12 * v1w - 2.0 * h22 * v2w + 2.0 * h12 * h22 * v1v2
    h32 = jnp.sqrt(jnp.maximum(third, zero) + EPS)
    rho_one = jnp.sqrt(h11 * h11 + h21 * h21)
    cos_one = h11 / rho_one
    sin_one = h21 / rho_one
    upper = cos_one * h12 + sin_one * h22
    lower = cos_one * h22 - sin_one * h12
    rho_two = jnp.sqrt(lower * lower + h32 * h32)
    coef_two = lower / rho_two * (-sin_one * beta) / rho_two
    coef_one = (cos_one * beta - upper * coef_two) / rho_one
    q_one = beta - h11 * coef_one - h12 * coef_two
    q_two = -h21 * coef_one - h22 * coef_two
    q_three = -h32 * coef_two / h32
    sol_v = coef_one - coef_two * h11 * inv
    sol_p = coef_two * inv
    res_v = q_one - q_two * h11 * inv + q_three * (h22 * h11 * inv - h12)
    res_p = q_two * inv - q_three * (h11 + h22) * inv
    res_s = q_three * inv
    sol_v, sol_p, res_v, res_p, res_s = (
        jnp.concatenate([x, x, x, x], axis=0) for x in (sol_v, sol_p, res_v, res_p, res_s)
    )
    for c in range(CDEV):
        cut = slice(c * CP, (c + 1) * CP)
        v, p, s = basis[c], image[c], second[c]
        solution_out[:, cut] = unfold(sol_v * v + sol_p * p)
        residual_out[:, cut] = unfold(res_v * v + res_p * p + res_s * s)


def shards(right_side, geometry, pairs, near_count, far_left_factor, far_right):
    devices = lax.axis_size(AXES)
    npair = pairs.shape[0]
    nslot = devices * CAP
    width = right_side.shape[1]
    field = (CDEV,) + BLOCK
    plain = (nslot,) + BLOCK
    coded = (nslot, 2 * BLOCK[0], BLOCK[1])

    ends = jnp.pad(pairs.T.astype(f32), ((0, 6), (0, width - npair)))
    given = jnp.concatenate([right_side, geometry, ends], axis=0)
    payload, slots, codes = pl.pallas_call(
        wish_kernel,
        out_shape=(
            sds((devices, 128), f32),
            sds((2, npair + 8), i32),
            sds((CDEV,) + coded[1:], jnp.int16),
        ),
        in_specs=[SMEM, VMEM],
        out_specs=(VMEM,) * 3,
        compiler_params=room(8),
        name="wishes",
    )(near_count, given)
    met = all_to_all(payload.reshape(devices, 1, 128)).reshape(devices, 128)
    wanted = met[:, :CAP].astype(i32).reshape(nslot)

    table = [pltpu.SMEM((nslot,), i32), pltpu.SemaphoreType.DMA(())]
    outgoing, factor = pl.pallas_call(
        pack_kernel,
        out_shape=(sds(coded, jnp.int16), sds((devices, 2 * NRHS, 128), f32)),
        in_specs=[VMEM] * 3,
        out_specs=(VMEM,) * 2,
        scratch_shapes=table,
        compiler_params=room(8),
        name="pack",
    )(wanted, codes, met)
    incoming = all_to_all(outgoing.reshape(devices, CAP * coded[1], LANES)).reshape(coded)

    work = [pltpu.VMEM((npair * NRHS, CP), f32)] * 4
    work += [pltpu.VMEM((npair * NRHS, GROUP * RANK), bf16)] * 2
    terms = [
        pltpu.VMEM((NEAR_MOST // 2, CP, TERMS), bf16),
        pltpu.VMEM((NEAR_MOST, TERMS, CP), bf16),
    ]
    some = sds((NEAR_MOST // 4, 2, CP, CP), bf16)
    returning, even, odd = pl.pallas_call(
        first_kernel,
        out_shape=(sds(plain, bf16), some, some),
        in_specs=[SMEM] + [VMEM] * 4,
        out_specs=(VMEM,) * 3,
        scratch_shapes=work + terms,
        compiler_params=room(24),
        name="first_operator",
    )(slots, incoming, factor, far_left_factor, far_right)

    def exchange(x):
        return all_to_all(x.reshape(devices, CAP * BLOCK[0], LANES)).reshape(plain)

    totals = [pltpu.VMEM((CDEV + 1,) + BLOCK, f32)] * LOOSE
    image, outgoing = pl.pallas_call(
        turn_kernel,
        out_shape=(sds(field, f32), sds(plain, bf16)),
        in_specs=[VMEM] * 2,
        out_specs=(VMEM,) * 2,
        scratch_shapes=[pltpu.VMEM(field, bf16)] + table + totals,
        compiler_params=room(8),
        name="turn",
    )(wanted, exchange(returning))

    returning = pl.pallas_call(
        second_kernel,
        out_shape=sds(plain, bf16),
        in_specs=[SMEM] + [VMEM] * 5,
        out_specs=VMEM,
        scratch_shapes=work,
        compiler_params=room(24),
        name="second_operator",
    )(slots, exchange(outgoing), far_left_factor, far_right, even, odd)

    second, basis, gram = pl.pallas_call(
        gram_kernel,
        out_shape=(sds(field, f32), sds(field, f32), sds((devices, 128), f32)),
        in_specs=[VMEM] * 5,
        out_specs=(VMEM,) * 3,
        scratch_shapes=table + totals,
        compiler_params=room(8),
        name="gram",
    )(wanted, exchange(returning), met, right_side, image)
    sums = all_to_all(gram.reshape(devices, 1, 128)).reshape(devices, 128)

    return pl.pallas_call(
        final_kernel,
        out_shape=(sds((NRHS, width), f32),) * 2,
        in_specs=[VMEM] * 5,
        out_specs=(VMEM,) * 2,
        compiler_params=room(8),
        name="combine",
    )(sums, met, basis, image, second)


def solution(mesh):
    spread_last = P(None, AXES)
    return jax.shard_map(
        shards,
        mesh=mesh,
        in_specs=(
            spread_last,
            spread_last,
            P(AXES, None),
            P(AXES),
            P(AXES, None, None),
            P(AXES, None, None),
        ),
        out_specs=(spread_last, spread_last),
        check_vma=False,
    )
```

```python
import functools
import math

import jax
import jax.numpy as jnp
from jax import lax
from jax.experimental import pallas as pl
from jax.experimental.pallas import tpu as pltpu
from jax.sharding import PartitionSpec as P

CP = 512
RANK = 32
NRHS = 4
CDEV = 8
CAP = 2
NEAR_MOST = 16
GROUP = 8
EPS = 1e-06
CODE = 32767.0
GEO_MID = (0.0, 0.0, 0.0, 0.275)
GEO_HALF = (5.0, 5.0, 5.0, 0.225)
FOUR_PI = 4.0 * math.pi

bf16 = jnp.bfloat16
f32 = jnp.float32
i32 = jnp.int32
AXES = ("row", "col")
VMEM = pl.BlockSpec(memory_space=pltpu.VMEM)
SMEM = pl.BlockSpec(memory_space=pltpu.SMEM)
BLOCK = (4 * NRHS, CP // 4)
LANES = CP // 4


def room(mib):
    return pltpu.CompilerParams(vmem_limit_bytes=mib * 1024 * 1024)


def sds(shape, dtype):
    return jax.ShapeDtypeStruct(shape, dtype)


def all_to_all(x):
    return lax.all_to_all(x, AXES, split_axis=0, concat_axis=0, tiled=True)


def col4(values):
    row = lax.broadcasted_iota(i32, (4, 1), 0)
    out = jnp.full((4, 1), values[3], f32)
    for k in range(3):
        out = jnp.where(row == k, values[k], out)
    return out


def spread(columns):
    lane = lax.broadcasted_iota(i32, (4, 128), 1)
    row = lax.broadcasted_iota(i32, (4, 128), 0)
    out = jnp.zeros((4, 128), f32)
    for i, column in enumerate(columns):
        out = out + jnp.where(lane == 4 * i + row, column, 0.0)
    return jnp.sum(out, axis=0, keepdims=True)


def pick(row_vector, i):
    lane = lax.broadcasted_iota(i32, (4, 128), 1)
    row = lax.broadcasted_iota(i32, (4, 128), 0)
    return jnp.sum(jnp.where(lane == 4 * i + row, row_vector, 0.0), axis=1, keepdims=True)


def fold(x):
    return jnp.concatenate([x[:, k * LANES : (k + 1) * LANES] for k in range(4)], axis=0)


def upper_half():
    return lax.broadcasted_iota(i32, (8, LANES), 0) < 4


def swap(x):
    return pltpu.roll(x, 4, axis=0)


def fold_two(x):
    up = upper_half()
    a, b, c, d = (x[:, k * LANES : (k + 1) * LANES] for k in range(4))
    first = [jnp.where(up, a, swap(b)), jnp.where(up, c, swap(d))]
    second = [jnp.where(up, swap(a), b), jnp.where(up, swap(c), d)]
    return jnp.concatenate(first, axis=0), jnp.concatenate(second, axis=0)


def unfold_two(u, w):
    up = upper_half()
    out = []
    for at in (slice(0, 8), slice(8, 16)):
        out += [jnp.where(up, u[at], swap(w[at])), jnp.where(up, swap(u[at]), w[at])]
    return jnp.concatenate(out, axis=1)


def unfold(x):
    return jnp.concatenate([x[4 * k : 4 * k + 4] for k in range(4)], axis=1)


def wish_kernel(live, pairs, given, payload, slots, codes):
    n = slots.shape[1] - 8
    sub = lax.broadcasted_iota(i32, (n, n), 0)
    lane = lax.broadcasted_iota(i32, (n, n), 1)
    homes, locals_, columns = [], [], []
    for k in range(2):
        ends = pairs[k : k + 1, :]
        homes.append(ends // CDEV)
        locals_.append(ends % CDEV)
        columns.append(jnp.sum(jnp.where(sub == lane, homes[k], 0), axis=1, keepdims=True))

    def count(column, row, limit):
        hit = jnp.logical_and(column == row, limit) if limit is not None else column == row
        return jnp.sum(hit.astype(i32), axis=0, keepdims=True)

    earlier = sub < lane
    ranks = [
        count(columns[0], homes[0], earlier),
        count(columns[0], homes[1], None) + count(columns[1], homes[1], earlier),
    ]
    peers = payload.shape[0]
    peer = lax.broadcasted_iota(i32, (peers, n), 0)
    wide = lax.broadcasted_iota(i32, (peers, 128), 1)
    out = jnp.zeros((peers, 128), f32)
    for j in range(CAP):
        wish = jnp.full((peers, 1), -1, i32)
        for k in range(2):
            hit = jnp.logical_and(peer == homes[k], ranks[k] == j)
            wish = wish + jnp.sum(jnp.where(hit, locals_[k] + 1, 0), axis=1, keepdims=True)
        out = jnp.where(wide == j, wish.astype(f32), out)
    for k in range(2):
        slots[k : k + 1, 0:n] = homes[k] * CAP + ranks[k]
        slots[k : k + 1, n : n + 8] = jnp.broadcast_to(live[0], (1, 8))
    r = given[0:NRHS, :]
    squares = jnp.sum(r * r, axis=1, keepdims=True)
    largest = jnp.max(jnp.abs(r), axis=1, keepdims=True)
    payload[...] = out + spread([jnp.zeros((4, 1), f32), squares, largest, largest])
    scale = CODE / jnp.maximum(largest, 1e-30)
    mid, half = col4(GEO_MID), col4([CODE / h for h in GEO_HALF])
    for c in range(CDEV):
        cut = slice(c * CP, (c + 1) * CP)
        both = jnp.concatenate(
            [fold(r[:, cut] * scale), fold((given[NRHS:8, cut] - mid) * half)], axis=0
        )
        both = jnp.minimum(jnp.maximum(both, -CODE), CODE)
        codes[c] = jnp.floor(both + 0.5).astype(i32).astype(jnp.int16)


def pack_kernel(wishes, codes, met, out, factor, wanted, sem):
    table = pltpu.make_async_copy(wishes, wanted, sem)
    table.start()
    columns = met[...].T
    beta = jnp.sqrt(jnp.sum(columns[4:8], axis=1, keepdims=True) + EPS)
    units = columns[8:16] * ((1.0 / CODE) / jnp.concatenate([beta, beta], axis=0))
    for sender in range(met.shape[0]):
        factor[sender] = jnp.broadcast_to(units[:, sender : sender + 1], factor.shape[1:])
    table.wait()

    def step(s, carry):
        out[s] = codes[jnp.maximum(wanted[s], 0)]
        return carry

    lax.fori_loop(0, out.shape[0], step, 0, unroll=16)


TRANSPOSED = (((1,), (1,)), ((), ()))


def far_products(left, right, x_first, x_second, t_first, t_second, y_first, y_second, load, beside=None):
    rows, wide = GROUP * NRHS, GROUP * RANK
    diagonal = (
        lax.broadcasted_iota(i32, (rows, wide), 0) // NRHS
        == lax.broadcasted_iota(i32, (rows, wide), 1) // RANK
    )
    groups = left.shape[0] // GROUP
    for g in range(groups):
        at = slice(g * rows, (g + 1) * rows)
        for q in range(g * GROUP // 2, (g + 1) * GROUP // 2):
            load(q)
        for x, factor, t in ((x_second, right, t_first), (x_first, left, t_second)):
            f = factor[g * GROUP : (g + 1) * GROUP].reshape(wide, CP)
            value = lax.dot_general(x[at, :].astype(bf16), f, TRANSPOSED, preferred_element_type=f32)
            t[at, :] = jnp.where(diagonal, value, 0.0).astype(bf16)
        if beside:
            beside(g)
    for g in range(groups):
        at = slice(g * rows, (g + 1) * rows)
        for t, factor, y in ((t_first, left, y_first), (t_second, right, y_second)):
            f = factor[g * GROUP : (g + 1) * GROUP].reshape(wide, CP)
            y[at, :] = jnp.dot(t[at, :], f, preferred_element_type=f32)


def near_products(q, near, tiles, x_first, x_second, y_first, y_second, between=None):
    at = pl.ds(pl.multiple_of(q * 8, 8), 8)
    row = lax.broadcasted_iota(i32, (8, CP), 0)
    mine = 2 * q + row // NRHS < near
    x1, x2 = x_first[at, :], x_second[at, :]
    n1 = n2 = 0.0
    for k in range(2):
        tile = tiles[q // 2, k]
        here = row // NRHS == k
        n1 += lax.dot_general(
            jnp.where(here, x2, 0.0).astype(bf16), tile, TRANSPOSED, preferred_element_type=f32
        )
        if between:
            between(2 * k)
        n2 += jnp.dot(jnp.where(here, x1, 0.0).astype(bf16), tile, preferred_element_type=f32)
        if between:
            between(2 * k + 1)
    y_first[at, :] = jnp.where(mine, n1, y_first[at, :])
    y_second[at, :] = jnp.where(mine, n2, y_second[at, :])


def send_products(q, slots, y_first, y_second, out):
    at = pl.ds(pl.multiple_of(q * 8, 8), 8)
    for side, y in ((0, y_first), (1, y_second)):
        a, b = fold_two(y[at, :])
        out[slots[side, 2 * q]] = a.astype(bf16)
        out[slots[side, 2 * q + 1]] = b.astype(bf16)


def halves(x, parts):
    out = []
    for _ in range(parts):
        piece = x.astype(bf16).astype(f32)
        out.append(piece)
        x = x - piece
    return out


TERMS = 48


def distance_terms(code, side):
    unit = GEO_HALF[0] / CODE
    row = lax.broadcasted_iota(i32, (8, CP), 0)
    place = row % 4 < 3
    squares = jnp.where(place, code * code, 0.0)
    sizes = (GEO_MID[3] + code * (GEO_HALF[3] / CODE)) * (1.0 / unit**2)
    squares = jnp.where(place, squares, sizes)
    totals = [jnp.sum(squares[k : k + 4], axis=0, keepdims=True) for k in (0, 4)]
    total = jnp.where(row < 4, totals[0], totals[1])
    n1, n2, n3 = halves(total, 3)
    high, low = halves(code, 2)
    one = jnp.ones((8, CP), f32)
    zero = jnp.zeros((8, CP), f32)
    if side == 0:
        parts = [
            jnp.where(place, high, n1), jnp.where(place, high, n2), jnp.where(place, low, n3),
            jnp.where(place, low, one), jnp.where(row % 4 < 2, one, zero),
        ]
    else:
        high, low = -2.0 * high, -2.0 * low
        parts = [
            jnp.where(place, high, one), jnp.where(place, low, one), jnp.where(place, high, one),
            jnp.where(place, low, n1),
            jnp.where(row % 4 == 0, n2, jnp.where(row % 4 == 1, n3, zero)),
        ]
    return jnp.concatenate(parts + [zero], axis=0)


def first_kernel(
    slots, got, factor, left, right, out, even, odd,
    x_first, x_second, y_first, y_second, t_first, t_second, terms_first, terms_second,
):
    npair = left.shape[0]
    near = slots[0, npair]

    def load(q):
        for side, x in ((0, x_first), (1, x_second)):
            s, t = slots[side, 2 * q], slots[side, 2 * q + 1]
            f, g = factor[s // CAP], factor[t // CAP]
            u = got[s, : BLOCK[0]].astype(i32).astype(f32) * jnp.concatenate([f, f], axis=0)
            w = got[t, : BLOCK[0]].astype(i32).astype(f32) * jnp.concatenate([g, g], axis=0)
            x[8 * q : 8 * q + 8, :] = unfold_two(u, w)

    term = lax.broadcasted_iota(i32, (TERMS, CP), 0)

    def load_terms(q):
        place = [
            unfold_two(*(got[slots[side, 2 * q + k], BLOCK[0] :].astype(i32).astype(f32) for k in range(2)))
            for side in range(2)
        ]
        terms_first[q] = distance_terms(place[0], 0).T.astype(bf16)
        both = distance_terms(place[1], 1)
        for k in range(2):
            terms_second[2 * q + k] = jnp.where(term % 8 // 4 == k, both, 0.0).astype(bf16)

    last = NEAR_MOST // 2 - 1
    far_products(
        left, right, x_first, x_second, t_first, t_second, y_first, y_second, load, load_terms
    )
    load_terms(last)
    unit = CODE / (GEO_HALF[0] * FOUR_PI)

    def make(q, tiles, part):
        k = part // 2
        for cut in range(part % 2 * 256, part % 2 * 256 + 256, 128):
            d = jnp.dot(
                terms_first[q, cut : cut + 128, :], terms_second[2 * q + k],
                preferred_element_type=f32,
            )
            tiles[q // 2, k, cut : cut + 128, :] = (lax.rsqrt(d) * unit).astype(bf16)

    def use(q, tiles, between=None):
        near_products(q, near, tiles, x_first, x_second, y_first, y_second, between)

    def near_step(h, carry):
        use(2 * h, even, lambda part: make(2 * h + 1, odd, part))
        for k in range(spread_out):
            send_products(last + 1 + spread_out * h + k, slots, y_first, y_second, out)
        use(2 * h + 1, odd, lambda part: make(2 * h + 2, even, part))
        return carry

    spread_out = (npair // 2 - last - 1) // (last // 2)
    for part in range(4):
        make(0, even, part)
    lax.fori_loop(0, last // 2, near_step, 0)
    use(last - 1, even, lambda part: make(last, odd, part))
    use(last, odd)
    for q in [*range(last + 1), *range(last + 1 + spread_out * (last // 2), npair // 2)]:
        send_products(q, slots, y_first, y_second, out)


def second_kernel(
    slots, got, left, right, even, odd, out,
    x_first, x_second, y_first, y_second, t_first, t_second,
):
    npair = left.shape[0]
    near = slots[0, npair]

    def load(q):
        for side, x in ((0, x_first), (1, x_second)):
            u, w = got[slots[side, 2 * q]], got[slots[side, 2 * q + 1]]
            x[8 * q : 8 * q + 8, :] = unfold_two(u.astype(f32), w.astype(f32))

    far_products(left, right, x_first, x_second, t_first, t_second, y_first, y_second, load)
    blocks = NEAR_MOST // 2
    spread_out = (npair // 2 - blocks) // (blocks // 2)

    def near_step(h, carry):
        near_products(2 * h, near, even, x_first, x_second, y_first, y_second)
        for k in range(spread_out):
            send_products(blocks + spread_out * h + k, slots, y_first, y_second, out)
        near_products(2 * h + 1, near, odd, x_first, x_second, y_first, y_second)
        return carry

    lax.fori_loop(0, blocks // 2, near_step, 0, unroll=2)
    for q in [*range(blocks), *range(blocks + spread_out * (blocks // 2), npair // 2)]:
        send_products(q, slots, y_first, y_second, out)


LOOSE = 4


def clear(totals):
    for total in totals:
        total[...] = jnp.zeros(total.shape, f32)


def gather_sum(wanted, got, totals):
    def step(q, carry):
        for k, total in enumerate(totals):
            w = wanted[q * LOOSE + k]
            c = jnp.where(w < 0, CDEV, w)
            total[c] = total[c] + got[q * LOOSE + k].astype(f32)
        return carry

    lax.fori_loop(0, got.shape[0] // LOOSE, step, 0, unroll=4)
    parts = [total[0:CDEV] for total in totals]
    while len(parts) > 1:
        parts = [a + b for a, b in zip(parts[::2], parts[1::2])]
    return parts[0]


def turn_kernel(wishes, got, image, out, half, wanted, sem, *totals):
    table = pltpu.make_async_copy(wishes, wanted, sem)
    table.start()
    clear(totals)
    table.wait()
    total = gather_sum(wanted, got, totals)
    image[...] = total
    half[...] = total.astype(bf16)

    def step(s, carry):
        out[s] = half[jnp.maximum(wanted[s], 0)]
        return carry

    lax.fori_loop(0, out.shape[0], step, 0, unroll=16)


def inner(x, y):
    rows = jnp.sum(jnp.sum(x * y, axis=0), axis=1, keepdims=True)
    return rows[0:4] + rows[4:8] + rows[8:12] + rows[12:16]


def gram_kernel(wishes, got, met, rhs, image, second, basis, payload, wanted, sem, *totals):
    table = pltpu.make_async_copy(wishes, wanted, sem)
    table.start()
    clear(totals)
    beta = jnp.sqrt(pick(jnp.sum(met[...], axis=0, keepdims=True), 1) + EPS)
    r = rhs[...] / beta
    for c in range(CDEV):
        basis[c] = fold(r[:, c * CP : (c + 1) * CP])
    v, p = basis[...], image[...]
    known = [inner(v, v), inner(v, p), inner(p, p)]
    table.wait()
    s = gather_sum(wanted, got, totals)
    second[...] = s
    row = spread(known + [inner(v, s), inner(p, s), inner(s, s)])
    payload[...] = jnp.broadcast_to(row, payload.shape)


def final_kernel(got, norms, basis, image, second, solution_out, residual_out):
    total = jnp.sum(got[...], axis=0, keepdims=True)
    vv, vp, pp, vs, ps, ss = (pick(total, i) for i in range(6))
    beta = jnp.sqrt(pick(jnp.sum(norms[...], axis=0, keepdims=True), 1) + EPS)
    zero = jnp.zeros_like(vv)
    h11 = vp
    first = jnp.maximum(pp - 2.0 * h11 * vp + h11 * h11 * vv, zero)
    h21 = jnp.sqrt(first + EPS)
    inv = 1.0 / h21
    v1w = (vs - h11 * vp) * inv
    v2w = (ps - h11 * pp - h11 * vs + h11 * h11 * vp) * inv * inv
    ww = (ss - 2.0 * h11 * ps + h11 * h11 * pp) * inv * inv
    v1v2 = (vp - h11 * vv) * inv
    v2v2 = first * inv * inv
    h12, h22 = v1w, v2w
    third = ww + h12 * h12 * vv + h22 * h22 * v2v2
    third = third - 2.0 * h12 * v1w - 2.0 * h22 * v2w + 2.0 * h12 * h22 * v1v2
    h32 = jnp.sqrt(jnp.maximum(third, zero) + EPS)
    rho_one = jnp.sqrt(h11 * h11 + h21 * h21)
    cos_one = h11 / rho_one
    sin_one = h21 / rho_one
    upper = cos_one * h12 + sin_one * h22
    lower = cos_one * h22 - sin_one * h12
    rho_two = jnp.sqrt(lower * lower + h32 * h32)
    coef_two = lower / rho_two * (-sin_one * beta) / rho_two
    coef_one = (cos_one * beta - upper * coef_two) / rho_one
    q_one = beta - h11 * coef_one - h12 * coef_two
    q_two = -h21 * coef_one - h22 * coef_two
    q_three = -h32 * coef_two / h32
    sol_v = coef_one - coef_two * h11 * inv
    sol_p = coef_two * inv
    res_v = q_one - q_two * h11 * inv + q_three * (h22 * h11 * inv - h12)
    res_p = q_two * inv - q_three * (h11 + h22) * inv
    res_s = q_three * inv
    sol_v, sol_p, res_v, res_p, res_s = (
        jnp.concatenate([x, x, x, x], axis=0) for x in (sol_v, sol_p, res_v, res_p, res_s)
    )
    for c in range(CDEV):
        cut = slice(c * CP, (c + 1) * CP)
        v, p, s = basis[c], image[c], second[c]
        solution_out[:, cut] = unfold(sol_v * v + sol_p * p)
        residual_out[:, cut] = unfold(res_v * v + res_p * p + res_s * s)


def shards(right_side, geometry, pairs, near_count, far_left_factor, far_right):
    devices = lax.axis_size(AXES)
    npair = pairs.shape[0]
    nslot = devices * CAP
    width = right_side.shape[1]
    field = (CDEV,) + BLOCK
    plain = (nslot,) + BLOCK
    coded = (nslot, 2 * BLOCK[0], BLOCK[1])

    given = jnp.concatenate([right_side, geometry], axis=0)
    payload, slots, codes = pl.pallas_call(
        wish_kernel,
        out_shape=(
            sds((devices, 128), f32),
            sds((2, npair + 8), i32),
            sds((CDEV,) + coded[1:], jnp.int16),
        ),
        in_specs=[SMEM, VMEM, VMEM],
        out_specs=(VMEM,) * 3,
        compiler_params=room(8),
        name="wishes",
    )(near_count, pairs.T, given)
    met = all_to_all(payload.reshape(devices, 1, 128)).reshape(devices, 128)
    wanted = met[:, :CAP].astype(i32).reshape(nslot)

    table = [pltpu.SMEM((nslot,), i32), pltpu.SemaphoreType.DMA(())]
    outgoing, factor = pl.pallas_call(
        pack_kernel,
        out_shape=(sds(coded, jnp.int16), sds((devices, 2 * NRHS, 128), f32)),
        in_specs=[VMEM] * 3,
        out_specs=(VMEM,) * 2,
        scratch_shapes=table,
        compiler_params=room(8),
        name="pack",
    )(wanted, codes, met)
    incoming = all_to_all(outgoing.reshape(devices, CAP * coded[1], LANES)).reshape(coded)

    work = [pltpu.VMEM((npair * NRHS, CP), f32)] * 4
    work += [pltpu.VMEM((npair * NRHS, GROUP * RANK), bf16)] * 2
    terms = [
        pltpu.VMEM((NEAR_MOST // 2, CP, TERMS), bf16),
        pltpu.VMEM((NEAR_MOST, TERMS, CP), bf16),
    ]
    some = sds((NEAR_MOST // 4, 2, CP, CP), bf16)
    returning, even, odd = pl.pallas_call(
        first_kernel,
        out_shape=(sds(plain, bf16), some, some),
        in_specs=[SMEM] + [VMEM] * 4,
        out_specs=(VMEM,) * 3,
        scratch_shapes=work + terms,
        compiler_params=room(24),
        name="first_operator",
    )(slots, incoming, factor, far_left_factor, far_right)

    def exchange(x):
        return all_to_all(x.reshape(devices, CAP * BLOCK[0], LANES)).reshape(plain)

    totals = [pltpu.VMEM((CDEV + 1,) + BLOCK, f32)] * LOOSE
    image, outgoing = pl.pallas_call(
        turn_kernel,
        out_shape=(sds(field, f32), sds(plain, bf16)),
        in_specs=[VMEM] * 2,
        out_specs=(VMEM,) * 2,
        scratch_shapes=[pltpu.VMEM(field, bf16)] + table + totals,
        compiler_params=room(8),
        name="turn",
    )(wanted, exchange(returning))

    returning = pl.pallas_call(
        second_kernel,
        out_shape=sds(plain, bf16),
        in_specs=[SMEM] + [VMEM] * 5,
        out_specs=VMEM,
        scratch_shapes=work,
        compiler_params=room(24),
        name="second_operator",
    )(slots, exchange(outgoing), far_left_factor, far_right, even, odd)

    second, basis, gram = pl.pallas_call(
        gram_kernel,
        out_shape=(sds(field, f32), sds(field, f32), sds((devices, 128), f32)),
        in_specs=[VMEM] * 5,
        out_specs=(VMEM,) * 3,
        scratch_shapes=table + totals,
        compiler_params=room(8),
        name="gram",
    )(wanted, exchange(returning), met, right_side, image)
    sums = all_to_all(gram.reshape(devices, 1, 128)).reshape(devices, 128)

    return pl.pallas_call(
        final_kernel,
        out_shape=(sds((NRHS, width), f32),) * 2,
        in_specs=[VMEM] * 5,
        out_specs=(VMEM,) * 2,
        compiler_params=room(8),
        name="combine",
    )(sums, met, basis, image, second)


def solution(mesh):
    spread_last = P(None, AXES)
    return jax.shard_map(
        shards,
        mesh=mesh,
        in_specs=(
            spread_last,
            spread_last,
            P(AXES, None),
            P(AXES),
            P(AXES, None, None),
            P(AXES, None, None),
        ),
        out_specs=(spread_last, spread_last),
        check_vma=False,
    )
```

```python
import functools
import math

import jax
import jax.numpy as jnp
from jax import lax
from jax.experimental import pallas as pl
from jax.experimental.pallas import tpu as pltpu
from jax.sharding import PartitionSpec as P

CP = 512
RANK = 32
NRHS = 4
CDEV = 8
CAP = 2
NEAR_MOST = 16
GROUP = 8
EPS = 1e-06
CODE = 32767.0
GEO_MID = (0.0, 0.0, 0.0, 0.275)
GEO_HALF = (5.0, 5.0, 5.0, 0.225)
FOUR_PI = 4.0 * math.pi

bf16 = jnp.bfloat16
f32 = jnp.float32
i32 = jnp.int32
AXES = ("row", "col")
VMEM = pl.BlockSpec(memory_space=pltpu.VMEM)
SMEM = pl.BlockSpec(memory_space=pltpu.SMEM)
BLOCK = (4 * NRHS, CP // 4)
LANES = CP // 4


def room(mib):
    return pltpu.CompilerParams(vmem_limit_bytes=mib * 1024 * 1024)


def sds(shape, dtype):
    return jax.ShapeDtypeStruct(shape, dtype)


def all_to_all(x):
    return lax.all_to_all(x, AXES, split_axis=0, concat_axis=0, tiled=True)


def col4(values):
    row = lax.broadcasted_iota(i32, (4, 1), 0)
    out = jnp.full((4, 1), values[3], f32)
    for k in range(3):
        out = jnp.where(row == k, values[k], out)
    return out


def spread(columns):
    lane = lax.broadcasted_iota(i32, (4, 128), 1)
    row = lax.broadcasted_iota(i32, (4, 128), 0)
    out = jnp.zeros((4, 128), f32)
    for i, column in enumerate(columns):
        out = out + jnp.where(lane == 4 * i + row, column, 0.0)
    return jnp.sum(out, axis=0, keepdims=True)


def pick(row_vector, i):
    lane = lax.broadcasted_iota(i32, (4, 128), 1)
    row = lax.broadcasted_iota(i32, (4, 128), 0)
    return jnp.sum(jnp.where(lane == 4 * i + row, row_vector, 0.0), axis=1, keepdims=True)


def fold(x):
    return jnp.concatenate([x[:, k * LANES : (k + 1) * LANES] for k in range(4)], axis=0)


def upper_half():
    return lax.broadcasted_iota(i32, (8, LANES), 0) < 4


def swap(x):
    return pltpu.roll(x, 4, axis=0)


def fold_two(x):
    up = upper_half()
    a, b, c, d = (x[:, k * LANES : (k + 1) * LANES] for k in range(4))
    first = [jnp.where(up, a, swap(b)), jnp.where(up, c, swap(d))]
    second = [jnp.where(up, swap(a), b), jnp.where(up, swap(c), d)]
    return jnp.concatenate(first, axis=0), jnp.concatenate(second, axis=0)


def unfold_two(u, w):
    up = upper_half()
    out = []
    for at in (slice(0, 8), slice(8, 16)):
        out += [jnp.where(up, u[at], swap(w[at])), jnp.where(up, swap(u[at]), w[at])]
    return jnp.concatenate(out, axis=1)


def unfold(x):
    return jnp.concatenate([x[4 * k : 4 * k + 4] for k in range(4)], axis=1)


def wish_kernel(live, pairs, given, payload, slots, codes):
    n = slots.shape[1] - 8
    sub = lax.broadcasted_iota(i32, (n, n), 0)
    lane = lax.broadcasted_iota(i32, (n, n), 1)
    homes, locals_, columns = [], [], []
    for k in range(2):
        ends = pairs[k : k + 1, :]
        homes.append(ends // CDEV)
        locals_.append(ends % CDEV)
        columns.append(jnp.sum(jnp.where(sub == lane, homes[k], 0), axis=1, keepdims=True))

    def count(column, row, limit):
        hit = jnp.logical_and(column == row, limit) if limit is not None else column == row
        return jnp.sum(hit.astype(i32), axis=0, keepdims=True)

    earlier = sub < lane
    ranks = [
        count(columns[0], homes[0], earlier),
        count(columns[0], homes[1], None) + count(columns[1], homes[1], earlier),
    ]
    peers = payload.shape[0]
    peer = lax.broadcasted_iota(i32, (peers, n), 0)
    wide = lax.broadcasted_iota(i32, (peers, 128), 1)
    out = jnp.zeros((peers, 128), f32)
    for j in range(CAP):
        wish = jnp.full((peers, 1), -1, i32)
        for k in range(2):
            hit = jnp.logical_and(peer == homes[k], ranks[k] == j)
            wish = wish + jnp.sum(jnp.where(hit, locals_[k] + 1, 0), axis=1, keepdims=True)
        out = jnp.where(wide == j, wish.astype(f32), out)
    for k in range(2):
        slots[k : k + 1, 0:n] = homes[k] * CAP + ranks[k]
        slots[k : k + 1, n : n + 8] = jnp.broadcast_to(live[0], (1, 8))
    r = given[0:NRHS, :]
    squares = jnp.sum(r * r, axis=1, keepdims=True)
    largest = jnp.max(jnp.abs(r), axis=1, keepdims=True)
    payload[...] = out + spread([jnp.zeros((4, 1), f32), squares, largest, largest])
    scale = CODE / jnp.maximum(largest, 1e-30)
    mid, half = col4(GEO_MID), col4([CODE / h for h in GEO_HALF])
    for c in range(CDEV):
        cut = slice(c * CP, (c + 1) * CP)
        both = jnp.concatenate(
            [fold(r[:, cut] * scale), fold((given[NRHS:8, cut] - mid) * half)], axis=0
        )
        both = jnp.minimum(jnp.maximum(both, -CODE), CODE)
        codes[c] = jnp.floor(both + 0.5).astype(i32).astype(jnp.int16)


def pack_kernel(wishes, codes, met, out, factor, wanted, sem):
    table = pltpu.make_async_copy(wishes, wanted, sem)
    table.start()
    columns = met[...].T
    beta = jnp.sqrt(jnp.sum(columns[4:8], axis=1, keepdims=True) + EPS)
    units = columns[8:16] * ((1.0 / CODE) / jnp.concatenate([beta, beta], axis=0))
    for sender in range(met.shape[0]):
        factor[sender] = jnp.broadcast_to(units[:, sender : sender + 1], factor.shape[1:])
    table.wait()

    def step(s, carry):
        out[s] = codes[jnp.maximum(wanted[s], 0)]
        return carry

    lax.fori_loop(0, out.shape[0], step, 0, unroll=32)


TRANSPOSED = (((1,), (1,)), ((), ()))


def far_products(left, right, x_first, x_second, t_first, t_second, y_first, y_second, load, beside=None):
    rows, wide = GROUP * NRHS, GROUP * RANK
    diagonal = (
        lax.broadcasted_iota(i32, (rows, wide), 0) // NRHS
        == lax.broadcasted_iota(i32, (rows, wide), 1) // RANK
    )
    groups = left.shape[0] // GROUP
    for g in range(groups):
        at = slice(g * rows, (g + 1) * rows)
        for q in range(g * GROUP // 2, (g + 1) * GROUP // 2):
            load(q)
        for x, factor, t in ((x_second, right, t_first), (x_first, left, t_second)):
            f = factor[g * GROUP : (g + 1) * GROUP].reshape(wide, CP)
            value = lax.dot_general(x[at, :].astype(bf16), f, TRANSPOSED, preferred_element_type=f32)
            t[at, :] = jnp.where(diagonal, value, 0.0).astype(bf16)
        if beside:
            beside(g)
    for g in range(groups):
        at = slice(g * rows, (g + 1) * rows)
        for t, factor, y in ((t_first, left, y_first), (t_second, right, y_second)):
            f = factor[g * GROUP : (g + 1) * GROUP].reshape(wide, CP)
            y[at, :] = jnp.dot(t[at, :], f, preferred_element_type=f32)


def near_products(q, near, tiles, x_first, x_second, y_first, y_second, between=None):
    at = pl.ds(pl.multiple_of(q * 8, 8), 8)
    row = lax.broadcasted_iota(i32, (8, CP), 0)
    mine = 2 * q + row // NRHS < near
    x1, x2 = x_first[at, :], x_second[at, :]
    n1 = n2 = 0.0
    for k in range(2):
        tile = tiles[q // 2, k]
        here = row // NRHS == k
        n1 += lax.dot_general(
            jnp.where(here, x2, 0.0).astype(bf16), tile, TRANSPOSED, preferred_element_type=f32
        )
        if between:
            between(2 * k)
        n2 += jnp.dot(jnp.where(here, x1, 0.0).astype(bf16), tile, preferred_element_type=f32)
        if between:
            between(2 * k + 1)
    y_first[at, :] = jnp.where(mine, n1, y_first[at, :])
    y_second[at, :] = jnp.where(mine, n2, y_second[at, :])


def send_products(q, slots, y_first, y_second, out):
    at = pl.ds(pl.multiple_of(q * 8, 8), 8)
    for side, y in ((0, y_first), (1, y_second)):
        a, b = fold_two(y[at, :])
        out[slots[side, 2 * q]] = a.astype(bf16)
        out[slots[side, 2 * q + 1]] = b.astype(bf16)


def halves(x, parts):
    out = []
    for _ in range(parts):
        piece = x.astype(bf16).astype(f32)
        out.append(piece)
        x = x - piece
    return out


TERMS = 48


def distance_terms(code, side):
    unit = GEO_HALF[0] / CODE
    row = lax.broadcasted_iota(i32, (8, CP), 0)
    place = row % 4 < 3
    squares = jnp.where(place, code * code, 0.0)
    sizes = (GEO_MID[3] + code * (GEO_HALF[3] / CODE)) * (1.0 / unit**2)
    squares = jnp.where(place, squares, sizes)
    totals = [jnp.sum(squares[k : k + 4], axis=0, keepdims=True) for k in (0, 4)]
    total = jnp.where(row < 4, totals[0], totals[1])
    n1, n2, n3 = halves(total, 3)
    high, low = halves(code, 2)
    one = jnp.ones((8, CP), f32)
    zero = jnp.zeros((8, CP), f32)
    if side == 0:
        parts = [
            jnp.where(place, high, n1), jnp.where(place, high, n2), jnp.where(place, low, n3),
            jnp.where(place, low, one), jnp.where(row % 4 < 2, one, zero),
        ]
    else:
        high, low = -2.0 * high, -2.0 * low
        parts = [
            jnp.where(place, high, one), jnp.where(place, low, one), jnp.where(place, high, one),
            jnp.where(place, low, n1),
            jnp.where(row % 4 == 0, n2, jnp.where(row % 4 == 1, n3, zero)),
        ]
    return jnp.concatenate(parts + [zero], axis=0)


def first_kernel(
    slots, got, factor, left, right, out, even, odd,
    x_first, x_second, y_first, y_second, t_first, t_second, terms_first, terms_second,
):
    npair = left.shape[0]
    near = slots[0, npair]

    def load(q):
        for side, x in ((0, x_first), (1, x_second)):
            s, t = slots[side, 2 * q], slots[side, 2 * q + 1]
            f, g = factor[s // CAP], factor[t // CAP]
            u = got[s, : BLOCK[0]].astype(i32).astype(f32) * jnp.concatenate([f, f], axis=0)
            w = got[t, : BLOCK[0]].astype(i32).astype(f32) * jnp.concatenate([g, g], axis=0)
            x[8 * q : 8 * q + 8, :] = unfold_two(u, w)

    term = lax.broadcasted_iota(i32, (TERMS, CP), 0)

    def load_terms(q):
        place = [
            unfold_two(*(got[slots[side, 2 * q + k], BLOCK[0] :].astype(i32).astype(f32) for k in range(2)))
            for side in range(2)
        ]
        terms_first[q] = distance_terms(place[0], 0).T.astype(bf16)
        both = distance_terms(place[1], 1)
        for k in range(2):
            terms_second[2 * q + k] = jnp.where(term % 8 // 4 == k, both, 0.0).astype(bf16)

    last = NEAR_MOST // 2 - 1

    def beside(g):
        load_terms(g)
        if g < 4:
            make(0, even, g)

    unit = CODE / (GEO_HALF[0] * FOUR_PI)

    def make(q, tiles, part):
        k = part // 2
        for cut in range(part % 2 * 256, part % 2 * 256 + 256, 128):
            d = jnp.dot(
                terms_first[q, cut : cut + 128, :], terms_second[2 * q + k],
                preferred_element_type=f32,
            )
            tiles[q // 2, k, cut : cut + 128, :] = (lax.rsqrt(d) * unit).astype(bf16)

    far_products(
        left, right, x_first, x_second, t_first, t_second, y_first, y_second, load, beside
    )
    load_terms(last)

    def use(q, tiles, between=None):
        near_products(q, near, tiles, x_first, x_second, y_first, y_second, between)

    def near_step(h, carry):
        use(2 * h, even, lambda part: make(2 * h + 1, odd, part))
        for k in range(spread_out):
            send_products(last + 1 + spread_out * h + k, slots, y_first, y_second, out)
        use(2 * h + 1, odd, lambda part: make(2 * h + 2, even, part))
        return carry

    spread_out = (npair // 2 - last - 1) // (last // 2)
    for h in range(last // 2):
        near_step(h, 0)
    use(last - 1, even, lambda part: make(last, odd, part))
    use(last, odd)
    for q in [*range(last + 1), *range(last + 1 + spread_out * (last // 2), npair // 2)]:
        send_products(q, slots, y_first, y_second, out)


def second_kernel(
    slots, got, left, right, even, odd, out,
    x_first, x_second, y_first, y_second, t_first, t_second,
):
    npair = left.shape[0]
    near = slots[0, npair]

    def load(q):
        for side, x in ((0, x_first), (1, x_second)):
            u, w = got[slots[side, 2 * q]], got[slots[side, 2 * q + 1]]
            x[8 * q : 8 * q + 8, :] = unfold_two(u.astype(f32), w.astype(f32))

    far_products(left, right, x_first, x_second, t_first, t_second, y_first, y_second, load)
    blocks = NEAR_MOST // 2
    spread_out = (npair // 2 - blocks) // (blocks // 2)

    def near_step(h, carry):
        near_products(2 * h, near, even, x_first, x_second, y_first, y_second)
        for k in range(spread_out):
            send_products(blocks + spread_out * h + k, slots, y_first, y_second, out)
        near_products(2 * h + 1, near, odd, x_first, x_second, y_first, y_second)
        return carry

    for h in range(blocks // 2):
        near_step(h, 0)
    for q in [*range(blocks), *range(blocks + spread_out * (blocks // 2), npair // 2)]:
        send_products(q, slots, y_first, y_second, out)


LOOSE = 4


def clear(totals):
    for total in totals:
        total[...] = jnp.zeros(total.shape, f32)


def gather_sum(wanted, got, totals):
    def step(q, carry):
        for k, total in enumerate(totals):
            w = wanted[q * LOOSE + k]
            c = jnp.where(w < 0, CDEV, w)
            total[c] = total[c] + got[q * LOOSE + k].astype(f32)
        return carry

    lax.fori_loop(0, got.shape[0] // LOOSE, step, 0, unroll=8)
    parts = [total[0:CDEV] for total in totals]
    while len(parts) > 1:
        parts = [a + b for a, b in zip(parts[::2], parts[1::2])]
    return parts[0]


def turn_kernel(wishes, got, image, out, half, wanted, sem, *totals):
    table = pltpu.make_async_copy(wishes, wanted, sem)
    table.start()
    clear(totals)
    table.wait()
    total = gather_sum(wanted, got, totals)
    image[...] = total
    half[...] = total.astype(bf16)

    def step(s, carry):
        out[s] = half[jnp.maximum(wanted[s], 0)]
        return carry

    lax.fori_loop(0, out.shape[0], step, 0, unroll=32)


def inner(x, y):
    rows = jnp.sum(jnp.sum(x * y, axis=0), axis=1, keepdims=True)
    return rows[0:4] + rows[4:8] + rows[8:12] + rows[12:16]


def gram_kernel(wishes, got, met, rhs, image, second, basis, payload, wanted, sem, *totals):
    table = pltpu.make_async_copy(wishes, wanted, sem)
    table.start()
    clear(totals)
    beta = jnp.sqrt(pick(jnp.sum(met[...], axis=0, keepdims=True), 1) + EPS)
    r = rhs[...] / beta
    for c in range(CDEV):
        basis[c] = fold(r[:, c * CP : (c + 1) * CP])
    v, p = basis[...], image[...]
    known = [inner(v, v), inner(v, p), inner(p, p)]
    table.wait()
    s = gather_sum(wanted, got, totals)
    second[...] = s
    row = spread(known + [inner(v, s), inner(p, s), inner(s, s)])
    payload[...] = jnp.broadcast_to(row, payload.shape)


def final_kernel(got, norms, basis, image, second, solution_out, residual_out):
    total = jnp.sum(got[...], axis=0, keepdims=True)
    vv, vp, pp, vs, ps, ss = (pick(total, i) for i in range(6))
    beta = jnp.sqrt(pick(jnp.sum(norms[...], axis=0, keepdims=True), 1) + EPS)
    zero = jnp.zeros_like(vv)
    h11 = vp
    first = jnp.maximum(pp - 2.0 * h11 * vp + h11 * h11 * vv, zero)
    h21 = jnp.sqrt(first + EPS)
    inv = 1.0 / h21
    v1w = (vs - h11 * vp) * inv
    v2w = (ps - h11 * pp - h11 * vs + h11 * h11 * vp) * inv * inv
    ww = (ss - 2.0 * h11 * ps + h11 * h11 * pp) * inv * inv
    v1v2 = (vp - h11 * vv) * inv
    v2v2 = first * inv * inv
    h12, h22 = v1w, v2w
    third = ww + h12 * h12 * vv + h22 * h22 * v2v2
    third = third - 2.0 * h12 * v1w - 2.0 * h22 * v2w + 2.0 * h12 * h22 * v1v2
    h32 = jnp.sqrt(jnp.maximum(third, zero) + EPS)
    rho_one = jnp.sqrt(h11 * h11 + h21 * h21)
    cos_one = h11 / rho_one
    sin_one = h21 / rho_one
    upper = cos_one * h12 + sin_one * h22
    lower = cos_one * h22 - sin_one * h12
    rho_two = jnp.sqrt(lower * lower + h32 * h32)
    coef_two = lower / rho_two * (-sin_one * beta) / rho_two
    coef_one = (cos_one * beta - upper * coef_two) / rho_one
    q_one = beta - h11 * coef_one - h12 * coef_two
    q_two = -h21 * coef_one - h22 * coef_two
    q_three = -h32 * coef_two / h32
    sol_v = coef_one - coef_two * h11 * inv
    sol_p = coef_two * inv
    res_v = q_one - q_two * h11 * inv + q_three * (h22 * h11 * inv - h12)
    res_p = q_two * inv - q_three * (h11 + h22) * inv
    res_s = q_three * inv
    sol_v, sol_p, res_v, res_p, res_s = (
        jnp.concatenate([x, x, x, x], axis=0) for x in (sol_v, sol_p, res_v, res_p, res_s)
    )
    for c in range(CDEV):
        cut = slice(c * CP, (c + 1) * CP)
        v, p, s = basis[c], image[c], second[c]
        solution_out[:, cut] = unfold(sol_v * v + sol_p * p)
        residual_out[:, cut] = unfold(res_v * v + res_p * p + res_s * s)


def shards(right_side, geometry, pairs, near_count, far_left_factor, far_right):
    devices = lax.axis_size(AXES)
    npair = pairs.shape[0]
    nslot = devices * CAP
    width = right_side.shape[1]
    field = (CDEV,) + BLOCK
    plain = (nslot,) + BLOCK
    coded = (nslot, 2 * BLOCK[0], BLOCK[1])

    given = jnp.concatenate([right_side, geometry], axis=0)
    payload, slots, codes = pl.pallas_call(
        wish_kernel,
        out_shape=(
            sds((devices, 128), f32),
            sds((2, npair + 8), i32),
            sds((CDEV,) + coded[1:], jnp.int16),
        ),
        in_specs=[SMEM, VMEM, VMEM],
        out_specs=(VMEM,) * 3,
        compiler_params=room(8),
        name="wishes",
    )(near_count, pairs.T, given)
    met = all_to_all(payload.reshape(devices, 1, 128)).reshape(devices, 128)
    wanted = met[:, :CAP].astype(i32).reshape(nslot)

    table = [pltpu.SMEM((nslot,), i32), pltpu.SemaphoreType.DMA(())]
    outgoing, factor = pl.pallas_call(
        pack_kernel,
        out_shape=(sds(coded, jnp.int16), sds((devices, 2 * NRHS, 128), f32)),
        in_specs=[VMEM] * 3,
        out_specs=(VMEM,) * 2,
        scratch_shapes=table,
        compiler_params=room(8),
        name="pack",
    )(wanted, codes, met)
    incoming = all_to_all(outgoing.reshape(devices, CAP * coded[1], LANES)).reshape(coded)

    work = [pltpu.VMEM((npair * NRHS, CP), f32)] * 4
    work += [pltpu.VMEM((npair * NRHS, GROUP * RANK), bf16)] * 2
    terms = [
        pltpu.VMEM((NEAR_MOST // 2, CP, TERMS), bf16),
        pltpu.VMEM((NEAR_MOST, TERMS, CP), bf16),
    ]
    some = sds((NEAR_MOST // 4, 2, CP, CP), bf16)
    returning, even, odd = pl.pallas_call(
        first_kernel,
        out_shape=(sds(plain, bf16), some, some),
        in_specs=[SMEM] + [VMEM] * 4,
        out_specs=(VMEM,) * 3,
        scratch_shapes=work + terms,
        compiler_params=room(24),
        name="first_operator",
    )(slots, incoming, factor, far_left_factor, far_right)

    def exchange(x):
        return all_to_all(x.reshape(devices, CAP * BLOCK[0], LANES)).reshape(plain)

    totals = [pltpu.VMEM((CDEV + 1,) + BLOCK, f32)] * LOOSE
    image, outgoing = pl.pallas_call(
        turn_kernel,
        out_shape=(sds(field, f32), sds(plain, bf16)),
        in_specs=[VMEM] * 2,
        out_specs=(VMEM,) * 2,
        scratch_shapes=[pltpu.VMEM(field, bf16)] + table + totals,
        compiler_params=room(8),
        name="turn",
    )(wanted, exchange(returning))

    returning = pl.pallas_call(
        second_kernel,
        out_shape=sds(plain, bf16),
        in_specs=[SMEM] + [VMEM] * 5,
        out_specs=VMEM,
        scratch_shapes=work,
        compiler_params=room(24),
        name="second_operator",
    )(slots, exchange(outgoing), far_left_factor, far_right, even, odd)

    second, basis, gram = pl.pallas_call(
        gram_kernel,
        out_shape=(sds(field, f32), sds(field, f32), sds((devices, 128), f32)),
        in_specs=[VMEM] * 5,
        out_specs=(VMEM,) * 3,
        scratch_shapes=table + totals,
        compiler_params=room(8),
        name="gram",
    )(wanted, exchange(returning), met, right_side, image)
    sums = all_to_all(gram.reshape(devices, 1, 128)).reshape(devices, 128)

    return pl.pallas_call(
        final_kernel,
        out_shape=(sds((NRHS, width), f32),) * 2,
        in_specs=[VMEM] * 5,
        out_specs=(VMEM,) * 2,
        compiler_params=room(8),
        name="combine",
    )(sums, met, basis, image, second)


def solution(mesh):
    spread_last = P(None, AXES)
    return jax.shard_map(
        shards,
        mesh=mesh,
        in_specs=(
            spread_last,
            spread_last,
            P(AXES, None),
            P(AXES),
            P(AXES, None, None),
            P(AXES, None, None),
        ),
        out_specs=(spread_last, spread_last),
        check_vma=False,
    )
```

```python
import functools
import math

import jax
import jax.numpy as jnp
from jax import lax
from jax.experimental import pallas as pl
from jax.experimental.pallas import tpu as pltpu
from jax.sharding import PartitionSpec as P

CP = 512
RANK = 32
NRHS = 4
CDEV = 8
CAP = 2
NEAR_MOST = 16
GROUP = 8
EPS = 1e-06
CODE = 32767.0
GEO_MID = (0.0, 0.0, 0.0, 0.275)
GEO_HALF = (5.0, 5.0, 5.0, 0.225)
FOUR_PI = 4.0 * math.pi

bf16 = jnp.bfloat16
f32 = jnp.float32
i32 = jnp.int32
AXES = ("row", "col")
VMEM = pl.BlockSpec(memory_space=pltpu.VMEM)
SMEM = pl.BlockSpec(memory_space=pltpu.SMEM)
BLOCK = (4 * NRHS, CP // 4)
LANES = CP // 4


def room(mib):
    return pltpu.CompilerParams(vmem_limit_bytes=mib * 1024 * 1024)


def sds(shape, dtype):
    return jax.ShapeDtypeStruct(shape, dtype)


def entry(table, row):
    return table[row : row + 1, :][0, 0]


def all_to_all(x):
    return lax.all_to_all(x, AXES, split_axis=0, concat_axis=0, tiled=True)


def col4(values):
    row = lax.broadcasted_iota(i32, (4, 1), 0)
    out = jnp.full((4, 1), values[3], f32)
    for k in range(3):
        out = jnp.where(row == k, values[k], out)
    return out


def spread(columns):
    lane = lax.broadcasted_iota(i32, (4, 128), 1)
    row = lax.broadcasted_iota(i32, (4, 128), 0)
    out = jnp.zeros((4, 128), f32)
    for i, column in enumerate(columns):
        out = out + jnp.where(lane == 4 * i + row, column, 0.0)
    return jnp.sum(out, axis=0, keepdims=True)


def pick(row_vector, i):
    lane = lax.broadcasted_iota(i32, (4, 128), 1)
    row = lax.broadcasted_iota(i32, (4, 128), 0)
    return jnp.sum(jnp.where(lane == 4 * i + row, row_vector, 0.0), axis=1, keepdims=True)


def fold(x):
    return jnp.concatenate([x[:, k * LANES : (k + 1) * LANES] for k in range(4)], axis=0)


def upper_half():
    return lax.broadcasted_iota(i32, (8, LANES), 0) < 4


def swap(x):
    return pltpu.roll(x, 4, axis=0)


def fold_two(x):
    up = upper_half()
    a, b, c, d = (x[:, k * LANES : (k + 1) * LANES] for k in range(4))
    first = [jnp.where(up, a, swap(b)), jnp.where(up, c, swap(d))]
    second = [jnp.where(up, swap(a), b), jnp.where(up, swap(c), d)]
    return jnp.concatenate(first, axis=0), jnp.concatenate(second, axis=0)


def unfold_two(u, w):
    up = upper_half()
    out = []
    for at in (slice(0, 8), slice(8, 16)):
        out += [jnp.where(up, u[at], swap(w[at])), jnp.where(up, swap(u[at]), w[at])]
    return jnp.concatenate(out, axis=1)


def unfold(x):
    return jnp.concatenate([x[4 * k : 4 * k + 4] for k in range(4)], axis=1)


def wish_kernel(live, pairs, given, payload, slots, codes):
    n = pairs.shape[1]
    sub = lax.broadcasted_iota(i32, (n, n), 0)
    lane = lax.broadcasted_iota(i32, (n, n), 1)
    homes, locals_, columns = [], [], []
    for k in range(2):
        ends = pairs[k : k + 1, :]
        homes.append(ends // CDEV)
        locals_.append(ends % CDEV)
        columns.append(jnp.sum(jnp.where(sub == lane, homes[k], 0), axis=1, keepdims=True))

    def count(column, row, limit):
        hit = jnp.logical_and(column == row, limit) if limit is not None else column == row
        return jnp.sum(hit.astype(i32), axis=0, keepdims=True)

    earlier = sub < lane
    ranks = [
        count(columns[0], homes[0], earlier),
        count(columns[0], homes[1], None) + count(columns[1], homes[1], earlier),
    ]
    peers = payload.shape[0]
    peer = lax.broadcasted_iota(i32, (peers, n), 0)
    wide = lax.broadcasted_iota(i32, (peers, 128), 1)
    out = jnp.zeros((peers, 128), f32)
    for j in range(CAP):
        wish = jnp.full((peers, 1), -1, i32)
        for k in range(2):
            hit = jnp.logical_and(peer == homes[k], ranks[k] == j)
            wish = wish + jnp.sum(jnp.where(hit, locals_[k] + 1, 0), axis=1, keepdims=True)
        out = jnp.where(wide == j, wish.astype(f32), out)
    for k in range(2):
        row = homes[k] * CAP + ranks[k]
        column = jnp.sum(jnp.where(sub == lane, row, 0), axis=1, keepdims=True)
        slots[k * n : (k + 1) * n, :] = jnp.broadcast_to(column, (n, 128))
    slots[2 * n : 2 * n + 8, :] = jnp.broadcast_to(live[0], (8, 128))
    r = given[0:NRHS, :]
    squares = jnp.sum(r * r, axis=1, keepdims=True)
    largest = jnp.max(jnp.abs(r), axis=1, keepdims=True)
    payload[...] = out + spread([jnp.zeros((4, 1), f32), squares, largest, largest])
    scale = CODE / jnp.maximum(largest, 1e-30)
    mid, half = col4(GEO_MID), col4([CODE / h for h in GEO_HALF])
    for c in range(CDEV):
        cut = slice(c * CP, (c + 1) * CP)
        both = jnp.concatenate(
            [fold(r[:, cut] * scale), fold((given[NRHS:8, cut] - mid) * half)], axis=0
        )
        both = jnp.minimum(jnp.maximum(both, -CODE), CODE)
        codes[c] = jnp.floor(both + 0.5).astype(i32).astype(jnp.int16)


def pack_kernel(wishes, codes, met, out, factor, wanted, sem):
    table = pltpu.make_async_copy(wishes, wanted, sem)
    table.start()
    columns = met[...].T
    beta = jnp.sqrt(jnp.sum(columns[4:8], axis=1, keepdims=True) + EPS)
    units = columns[8:16] * ((1.0 / CODE) / jnp.concatenate([beta, beta], axis=0))
    for sender in range(met.shape[0]):
        factor[sender] = jnp.broadcast_to(units[:, sender : sender + 1], factor.shape[1:])
    table.wait()

    def step(s, carry):
        out[s] = codes[jnp.maximum(wanted[s], 0)]
        return carry

    lax.fori_loop(0, out.shape[0], step, 0, unroll=32)


TRANSPOSED = (((1,), (1,)), ((), ()))


def far_products(left, right, x_first, x_second, t_first, t_second, y_first, y_second, load, beside=None):
    rows, wide = GROUP * NRHS, GROUP * RANK
    diagonal = (
        lax.broadcasted_iota(i32, (rows, wide), 0) // NRHS
        == lax.broadcasted_iota(i32, (rows, wide), 1) // RANK
    )
    groups = left.shape[0] // GROUP
    for g in range(groups):
        at = slice(g * rows, (g + 1) * rows)
        for q in range(g * GROUP // 2, (g + 1) * GROUP // 2):
            load(q)
        for x, factor, t in ((x_second, right, t_first), (x_first, left, t_second)):
            f = factor[g * GROUP : (g + 1) * GROUP].reshape(wide, CP)
            value = lax.dot_general(x[at, :].astype(bf16), f, TRANSPOSED, preferred_element_type=f32)
            t[at, :] = jnp.where(diagonal, value, 0.0).astype(bf16)
        if beside:
            beside(g)
    for g in range(groups):
        at = slice(g * rows, (g + 1) * rows)
        for t, factor, y in ((t_first, left, y_first), (t_second, right, y_second)):
            f = factor[g * GROUP : (g + 1) * GROUP].reshape(wide, CP)
            y[at, :] = jnp.dot(t[at, :], f, preferred_element_type=f32)


def near_products(q, near, tiles, x_first, x_second, y_first, y_second, between=None):
    at = pl.ds(pl.multiple_of(q * 8, 8), 8)
    row = lax.broadcasted_iota(i32, (8, CP), 0)
    mine = 2 * q + row // NRHS < near
    x1, x2 = x_first[at, :], x_second[at, :]
    n1 = n2 = 0.0
    for k in range(2):
        tile = tiles[q // 2, k]
        here = row // NRHS == k
        n1 += lax.dot_general(
            jnp.where(here, x2, 0.0).astype(bf16), tile, TRANSPOSED, preferred_element_type=f32
        )
        if between:
            between(2 * k)
        n2 += jnp.dot(jnp.where(here, x1, 0.0).astype(bf16), tile, preferred_element_type=f32)
        if between:
            between(2 * k + 1)
    y_first[at, :] = jnp.where(mine, n1, y_first[at, :])
    y_second[at, :] = jnp.where(mine, n2, y_second[at, :])


def send_products(q, slot, y_first, y_second, out):
    at = pl.ds(pl.multiple_of(q * 8, 8), 8)
    for side, y in ((0, y_first), (1, y_second)):
        a, b = fold_two(y[at, :])
        out[slot(side, 2 * q)] = a.astype(bf16)
        out[slot(side, 2 * q + 1)] = b.astype(bf16)


def halves(x, parts):
    out = []
    for _ in range(parts):
        piece = x.astype(bf16).astype(f32)
        out.append(piece)
        x = x - piece
    return out


TERMS = 48


def distance_terms(code, side):
    unit = GEO_HALF[0] / CODE
    row = lax.broadcasted_iota(i32, (8, CP), 0)
    place = row % 4 < 3
    squares = jnp.where(place, code * code, 0.0)
    sizes = (GEO_MID[3] + code * (GEO_HALF[3] / CODE)) * (1.0 / unit**2)
    squares = jnp.where(place, squares, sizes)
    totals = [jnp.sum(squares[k : k + 4], axis=0, keepdims=True) for k in (0, 4)]
    total = jnp.where(row < 4, totals[0], totals[1])
    n1, n2, n3 = halves(total, 3)
    high, low = halves(code, 2)
    one = jnp.ones((8, CP), f32)
    zero = jnp.zeros((8, CP), f32)
    if side == 0:
        parts = [
            jnp.where(place, high, n1), jnp.where(place, high, n2), jnp.where(place, low, n3),
            jnp.where(place, low, one), jnp.where(row % 4 < 2, one, zero),
        ]
    else:
        high, low = -2.0 * high, -2.0 * low
        parts = [
            jnp.where(place, high, one), jnp.where(place, low, one), jnp.where(place, high, one),
            jnp.where(place, low, n1),
            jnp.where(row % 4 == 0, n2, jnp.where(row % 4 == 1, n3, zero)),
        ]
    return jnp.concatenate(parts + [zero], axis=0)


def first_kernel(
    slots, got, factor, left, right, out, even, odd,
    x_first, x_second, y_first, y_second, t_first, t_second, terms_first, terms_second,
):
    npair = left.shape[0]
    near = entry(slots, 2 * npair)

    def slot(side, p):
        return entry(slots, side * npair + p)

    def load(q):
        for side, x in ((0, x_first), (1, x_second)):
            s, t = slot(side, 2 * q), slot(side, 2 * q + 1)
            f, g = factor[s // CAP], factor[t // CAP]
            u = got[s, : BLOCK[0]].astype(i32).astype(f32) * jnp.concatenate([f, f], axis=0)
            w = got[t, : BLOCK[0]].astype(i32).astype(f32) * jnp.concatenate([g, g], axis=0)
            x[8 * q : 8 * q + 8, :] = unfold_two(u, w)

    term = lax.broadcasted_iota(i32, (TERMS, CP), 0)

    def load_terms(q):
        place = [
            unfold_two(*(got[slot(side, 2 * q + k), BLOCK[0] :].astype(i32).astype(f32) for k in range(2)))
            for side in range(2)
        ]
        terms_first[q] = distance_terms(place[0], 0).T.astype(bf16)
        both = distance_terms(place[1], 1)
        for k in range(2):
            terms_second[2 * q + k] = jnp.where(term % 8 // 4 == k, both, 0.0).astype(bf16)

    last = NEAR_MOST // 2 - 1

    def beside(g):
        load_terms(g)
        if g < 4:
            make(0, even, g)

    unit = CODE / (GEO_HALF[0] * FOUR_PI)

    def make(q, tiles, part):
        k = part // 2
        for cut in range(part % 2 * 256, part % 2 * 256 + 256, 128):
            d = jnp.dot(
                terms_first[q, cut : cut + 128, :], terms_second[2 * q + k],
                preferred_element_type=f32,
            )
            tiles[q // 2, k, cut : cut + 128, :] = (lax.rsqrt(d) * unit).astype(bf16)

    far_products(
        left, right, x_first, x_second, t_first, t_second, y_first, y_second, load, beside
    )
    load_terms(last)

    def use(q, tiles, between=None):
        near_products(q, near, tiles, x_first, x_second, y_first, y_second, between)

    def near_step(h, carry):
        use(2 * h, even, lambda part: make(2 * h + 1, odd, part))
        for k in range(spread_out):
            send_products(last + 1 + spread_out * h + k, slot, y_first, y_second, out)
        use(2 * h + 1, odd, lambda part: make(2 * h + 2, even, part))
        return carry

    spread_out = (npair // 2 - last - 1) // (last // 2)
    for h in range(last // 2):
        near_step(h, 0)
    use(last - 1, even, lambda part: make(last, odd, part))
    use(last, odd)
    for q in [*range(last + 1), *range(last + 1 + spread_out * (last // 2), npair // 2)]:
        send_products(q, slot, y_first, y_second, out)


def second_kernel(
    slots, got, left, right, even, odd, out,
    x_first, x_second, y_first, y_second, t_first, t_second,
):
    npair = left.shape[0]
    near = entry(slots, 2 * npair)

    def slot(side, p):
        return entry(slots, side * npair + p)

    def load(q):
        for side, x in ((0, x_first), (1, x_second)):
            u, w = got[slot(side, 2 * q)], got[slot(side, 2 * q + 1)]
            x[8 * q : 8 * q + 8, :] = unfold_two(u.astype(f32), w.astype(f32))

    far_products(left, right, x_first, x_second, t_first, t_second, y_first, y_second, load)
    blocks = NEAR_MOST // 2
    spread_out = (npair // 2 - blocks) // (blocks // 2)

    def near_step(h, carry):
        near_products(2 * h, near, even, x_first, x_second, y_first, y_second)
        for k in range(spread_out):
            send_products(blocks + spread_out * h + k, slot, y_first, y_second, out)
        near_products(2 * h + 1, near, odd, x_first, x_second, y_first, y_second)
        return carry

    for h in range(blocks // 2):
        near_step(h, 0)
    for q in [*range(blocks), *range(blocks + spread_out * (blocks // 2), npair // 2)]:
        send_products(q, slot, y_first, y_second, out)


LOOSE = 4


def clear(totals):
    for total in totals:
        total[...] = jnp.zeros(total.shape, f32)


def gather_sum(wanted, got, totals):
    def step(q, carry):
        for k, total in enumerate(totals):
            w = wanted[q * LOOSE + k]
            c = jnp.where(w < 0, CDEV, w)
            total[c] = total[c] + got[q * LOOSE + k].astype(f32)
        return carry

    lax.fori_loop(0, got.shape[0] // LOOSE, step, 0, unroll=8)
    parts = [total[0:CDEV] for total in totals]
    while len(parts) > 1:
        parts = [a + b for a, b in zip(parts[::2], parts[1::2])]
    return parts[0]


def turn_kernel(wishes, got, image, out, half, wanted, sem, *totals):
    table = pltpu.make_async_copy(wishes, wanted, sem)
    table.start()
    clear(totals)
    table.wait()
    total = gather_sum(wanted, got, totals)
    image[...] = total
    half[...] = total.astype(bf16)

    def step(s, carry):
        out[s] = half[jnp.maximum(wanted[s], 0)]
        return carry

    lax.fori_loop(0, out.shape[0], step, 0, unroll=32)


def inner(x, y):
    rows = jnp.sum(jnp.sum(x * y, axis=0), axis=1, keepdims=True)
    return rows[0:4] + rows[4:8] + rows[8:12] + rows[12:16]


def gram_kernel(wishes, got, met, rhs, image, second, basis, payload, wanted, sem, *totals):
    table = pltpu.make_async_copy(wishes, wanted, sem)
    table.start()
    clear(totals)
    beta = jnp.sqrt(pick(jnp.sum(met[...], axis=0, keepdims=True), 1) + EPS)
    r = rhs[...] / beta
    for c in range(CDEV):
        basis[c] = fold(r[:, c * CP : (c + 1) * CP])
    v, p = basis[...], image[...]
    known = [inner(v, v), inner(v, p), inner(p, p)]
    table.wait()
    s = gather_sum(wanted, got, totals)
    second[...] = s
    row = spread(known + [inner(v, s), inner(p, s), inner(s, s)])
    payload[...] = jnp.broadcast_to(row, payload.shape)


def final_kernel(got, norms, basis, image, second, solution_out, residual_out):
    total = jnp.sum(got[...], axis=0, keepdims=True)
    vv, vp, pp, vs, ps, ss = (pick(total, i) for i in range(6))
    beta = jnp.sqrt(pick(jnp.sum(norms[...], axis=0, keepdims=True), 1) + EPS)
    zero = jnp.zeros_like(vv)
    h11 = vp
    first = jnp.maximum(pp - 2.0 * h11 * vp + h11 * h11 * vv, zero)
    h21 = jnp.sqrt(first + EPS)
    inv = 1.0 / h21
    v1w = (vs - h11 * vp) * inv
    v2w = (ps - h11 * pp - h11 * vs + h11 * h11 * vp) * inv * inv
    ww = (ss - 2.0 * h11 * ps + h11 * h11 * pp) * inv * inv
    v1v2 = (vp - h11 * vv) * inv
    v2v2 = first * inv * inv
    h12, h22 = v1w, v2w
    third = ww + h12 * h12 * vv + h22 * h22 * v2v2
    third = third - 2.0 * h12 * v1w - 2.0 * h22 * v2w + 2.0 * h12 * h22 * v1v2
    h32 = jnp.sqrt(jnp.maximum(third, zero) + EPS)
    rho_one = jnp.sqrt(h11 * h11 + h21 * h21)
    cos_one = h11 / rho_one
    sin_one = h21 / rho_one
    upper = cos_one * h12 + sin_one * h22
    lower = cos_one * h22 - sin_one * h12
    rho_two = jnp.sqrt(lower * lower + h32 * h32)
    coef_two = lower / rho_two * (-sin_one * beta) / rho_two
    coef_one = (cos_one * beta - upper * coef_two) / rho_one
    q_one = beta - h11 * coef_one - h12 * coef_two
    q_two = -h21 * coef_one - h22 * coef_two
    q_three = -h32 * coef_two / h32
    sol_v = coef_one - coef_two * h11 * inv
    sol_p = coef_two * inv
    res_v = q_one - q_two * h11 * inv + q_three * (h22 * h11 * inv - h12)
    res_p = q_two * inv - q_three * (h11 + h22) * inv
    res_s = q_three * inv
    sol_v, sol_p, res_v, res_p, res_s = (
        jnp.concatenate([x, x, x, x], axis=0) for x in (sol_v, sol_p, res_v, res_p, res_s)
    )
    for c in range(CDEV):
        cut = slice(c * CP, (c + 1) * CP)
        v, p, s = basis[c], image[c], second[c]
        solution_out[:, cut] = unfold(sol_v * v + sol_p * p)
        residual_out[:, cut] = unfold(res_v * v + res_p * p + res_s * s)


def shards(right_side, geometry, pairs, near_count, far_left_factor, far_right):
    devices = lax.axis_size(AXES)
    npair = pairs.shape[0]
    nslot = devices * CAP
    width = right_side.shape[1]
    field = (CDEV,) + BLOCK
    plain = (nslot,) + BLOCK
    coded = (nslot, 2 * BLOCK[0], BLOCK[1])

    given = jnp.concatenate([right_side, geometry], axis=0)
    payload, slots, codes = pl.pallas_call(
        wish_kernel,
        out_shape=(
            sds((devices, 128), f32),
            sds((2 * npair + 8, 128), i32),
            sds((CDEV,) + coded[1:], jnp.int16),
        ),
        in_specs=[SMEM, VMEM, VMEM],
        out_specs=(VMEM,) * 3,
        compiler_params=room(8),
        name="wishes",
    )(near_count, pairs.T, given)
    met = all_to_all(payload.reshape(devices, 1, 128)).reshape(devices, 128)
    wanted = met[:, :CAP].astype(i32).reshape(nslot)

    table = [pltpu.SMEM((nslot,), i32), pltpu.SemaphoreType.DMA(())]
    outgoing, factor = pl.pallas_call(
        pack_kernel,
        out_shape=(sds(coded, jnp.int16), sds((devices, 2 * NRHS, 128), f32)),
        in_specs=[VMEM] * 3,
        out_specs=(VMEM,) * 2,
        scratch_shapes=table,
        compiler_params=room(8),
        name="pack",
    )(wanted, codes, met)
    incoming = all_to_all(outgoing.reshape(devices, CAP * coded[1], LANES)).reshape(coded)

    work = [pltpu.VMEM((npair * NRHS, CP), f32)] * 4
    work += [pltpu.VMEM((npair * NRHS, GROUP * RANK), bf16)] * 2
    terms = [
        pltpu.VMEM((NEAR_MOST // 2, CP, TERMS), bf16),
        pltpu.VMEM((NEAR_MOST, TERMS, CP), bf16),
    ]
    some = sds((NEAR_MOST // 4, 2, CP, CP), bf16)
    returning, even, odd = pl.pallas_call(
        first_kernel,
        out_shape=(sds(plain, bf16), some, some),
        in_specs=[VMEM] * 5,
        out_specs=(VMEM,) * 3,
        scratch_shapes=work + terms,
        compiler_params=room(24),
        name="first_operator",
    )(slots, incoming, factor, far_left_factor, far_right)

    def exchange(x):
        return all_to_all(x.reshape(devices, CAP * BLOCK[0], LANES)).reshape(plain)

    totals = [pltpu.VMEM((CDEV + 1,) + BLOCK, f32)] * LOOSE
    image, outgoing = pl.pallas_call(
        turn_kernel,
        out_shape=(sds(field, f32), sds(plain, bf16)),
        in_specs=[VMEM] * 2,
        out_specs=(VMEM,) * 2,
        scratch_shapes=[pltpu.VMEM(field, bf16)] + table + totals,
        compiler_params=room(8),
        name="turn",
    )(wanted, exchange(returning))

    returning = pl.pallas_call(
        second_kernel,
        out_shape=sds(plain, bf16),
        in_specs=[VMEM] * 6,
        out_specs=VMEM,
        scratch_shapes=work,
        compiler_params=room(24),
        name="second_operator",
    )(slots, exchange(outgoing), far_left_factor, far_right, even, odd)

    second, basis, gram = pl.pallas_call(
        gram_kernel,
        out_shape=(sds(field, f32), sds(field, f32), sds((devices, 128), f32)),
        in_specs=[VMEM] * 5,
        out_specs=(VMEM,) * 3,
        scratch_shapes=table + totals,
        compiler_params=room(8),
        name="gram",
    )(wanted, exchange(returning), met, right_side, image)
    sums = all_to_all(gram.reshape(devices, 1, 128)).reshape(devices, 128)

    return pl.pallas_call(
        final_kernel,
        out_shape=(sds((NRHS, width), f32),) * 2,
        in_specs=[VMEM] * 5,
        out_specs=(VMEM,) * 2,
        compiler_params=room(8),
        name="combine",
    )(sums, met, basis, image, second)


def solution(mesh):
    spread_last = P(None, AXES)
    return jax.shard_map(
        shards,
        mesh=mesh,
        in_specs=(
            spread_last,
            spread_last,
            P(AXES, None),
            P(AXES),
            P(AXES, None, None),
            P(AXES, None, None),
        ),
        out_specs=(spread_last, spread_last),
        check_vma=False,
    )
```

```python
import functools
import math

import jax
import jax.numpy as jnp
from jax import lax
from jax.experimental import pallas as pl
from jax.experimental.pallas import tpu as pltpu
from jax.sharding import PartitionSpec as P

CP = 512
RANK = 32
NRHS = 4
CDEV = 8
CAP = 2
NEAR_MOST = 16
GROUP = 8
EPS = 1e-06
CODE = 32767.0
GEO_MID = (0.0, 0.0, 0.0, 0.275)
GEO_HALF = (5.0, 5.0, 5.0, 0.225)
FOUR_PI = 4.0 * math.pi

bf16 = jnp.bfloat16
f32 = jnp.float32
i32 = jnp.int32
AXES = ("row", "col")
VMEM = pl.BlockSpec(memory_space=pltpu.VMEM)
SMEM = pl.BlockSpec(memory_space=pltpu.SMEM)
BLOCK = (4 * NRHS, CP // 4)
LANES = CP // 4


def room(mib):
    return pltpu.CompilerParams(vmem_limit_bytes=mib * 1024 * 1024)


def sds(shape, dtype):
    return jax.ShapeDtypeStruct(shape, dtype)


def all_to_all(x):
    return lax.all_to_all(x, AXES, split_axis=0, concat_axis=0, tiled=True)


def col4(values):
    row = lax.broadcasted_iota(i32, (4, 1), 0)
    out = jnp.full((4, 1), values[3], f32)
    for k in range(3):
        out = jnp.where(row == k, values[k], out)
    return out


def spread(columns):
    lane = lax.broadcasted_iota(i32, (4, 128), 1)
    row = lax.broadcasted_iota(i32, (4, 128), 0)
    out = jnp.zeros((4, 128), f32)
    for i, column in enumerate(columns):
        out = out + jnp.where(lane == 4 * i + row, column, 0.0)
    return jnp.sum(out, axis=0, keepdims=True)


def pick(row_vector, i):
    lane = lax.broadcasted_iota(i32, (4, 128), 1)
    row = lax.broadcasted_iota(i32, (4, 128), 0)
    return jnp.sum(jnp.where(lane == 4 * i + row, row_vector, 0.0), axis=1, keepdims=True)


def fold(x):
    return jnp.concatenate([x[:, k * LANES : (k + 1) * LANES] for k in range(4)], axis=0)


def upper_half():
    return lax.broadcasted_iota(i32, (8, LANES), 0) < 4


def swap(x):
    return pltpu.roll(x, 4, axis=0)


def fold_two(x):
    up = upper_half()
    a, b, c, d = (x[:, k * LANES : (k + 1) * LANES] for k in range(4))
    first = [jnp.where(up, a, swap(b)), jnp.where(up, c, swap(d))]
    second = [jnp.where(up, swap(a), b), jnp.where(up, swap(c), d)]
    return jnp.concatenate(first, axis=0), jnp.concatenate(second, axis=0)


def unfold_two(u, w):
    up = upper_half()
    out = []
    for at in (slice(0, 8), slice(8, 16)):
        out += [jnp.where(up, u[at], swap(w[at])), jnp.where(up, swap(u[at]), w[at])]
    return jnp.concatenate(out, axis=1)


def unfold(x):
    return jnp.concatenate([x[4 * k : 4 * k + 4] for k in range(4)], axis=1)


def wish_kernel(live, pairs, given, payload, slots, codes):
    n = slots.shape[1] - 8
    sub = lax.broadcasted_iota(i32, (n, n), 0)
    lane = lax.broadcasted_iota(i32, (n, n), 1)
    homes, locals_, columns = [], [], []
    for k in range(2):
        ends = pairs[k : k + 1, :]
        homes.append(ends // CDEV)
        locals_.append(ends % CDEV)
        columns.append(jnp.sum(jnp.where(sub == lane, homes[k], 0), axis=1, keepdims=True))

    def count(column, row, limit):
        hit = jnp.logical_and(column == row, limit) if limit is not None else column == row
        return jnp.sum(hit.astype(i32), axis=0, keepdims=True)

    earlier = sub < lane
    ranks = [
        count(columns[0], homes[0], earlier),
        count(columns[0], homes[1], None) + count(columns[1], homes[1], earlier),
    ]
    peers = payload.shape[0]
    peer = lax.broadcasted_iota(i32, (peers, n), 0)
    wide = lax.broadcasted_iota(i32, (peers, 128), 1)
    out = jnp.zeros((peers, 128), f32)
    for j in range(CAP):
        wish = jnp.full((peers, 1), -1, i32)
        for k in range(2):
            hit = jnp.logical_and(peer == homes[k], ranks[k] == j)
            wish = wish + jnp.sum(jnp.where(hit, locals_[k] + 1, 0), axis=1, keepdims=True)
        out = jnp.where(wide == j, wish.astype(f32), out)
    for k in range(2):
        slots[k : k + 1, 0:n] = homes[k] * CAP + ranks[k]
        slots[k : k + 1, n : n + 8] = jnp.broadcast_to(live[0], (1, 8))
    r = given[0:NRHS, :]
    squares = jnp.sum(r * r, axis=1, keepdims=True)
    largest = jnp.max(jnp.abs(r), axis=1, keepdims=True)
    payload[...] = out + spread([jnp.zeros((4, 1), f32), squares, largest, largest])
    scale = CODE / jnp.maximum(largest, 1e-30)
    mid, half = col4(GEO_MID), col4([CODE / h for h in GEO_HALF])
    for c in range(CDEV):
        cut = slice(c * CP, (c + 1) * CP)
        both = jnp.concatenate(
            [fold(r[:, cut] * scale), fold((given[NRHS:8, cut] - mid) * half)], axis=0
        )
        both = jnp.minimum(jnp.maximum(both, -CODE), CODE)
        codes[c] = jnp.floor(both + 0.5).astype(i32).astype(jnp.int16)


def pack_kernel(wishes, codes, met, out, factor, wanted, sem):
    table = pltpu.make_async_copy(wishes, wanted, sem)
    table.start()
    columns = met[...].T
    beta = jnp.sqrt(jnp.sum(columns[4:8], axis=1, keepdims=True) + EPS)
    units = columns[8:16] * ((1.0 / CODE) / jnp.concatenate([beta, beta], axis=0))
    for sender in range(met.shape[0]):
        factor[sender] = jnp.broadcast_to(units[:, sender : sender + 1], factor.shape[1:])
    table.wait()

    def step(s, carry):
        out[s] = codes[jnp.minimum(wanted[s], CDEV - 1)]
        return carry

    lax.fori_loop(0, out.shape[0], step, 0, unroll=32)


TRANSPOSED = (((1,), (1,)), ((), ()))


def far_products(left, right, x_first, x_second, t_first, t_second, y_first, y_second, load, beside=None):
    rows, wide = GROUP * NRHS, GROUP * RANK
    diagonal = (
        lax.broadcasted_iota(i32, (rows, wide), 0) // NRHS
        == lax.broadcasted_iota(i32, (rows, wide), 1) // RANK
    )
    groups = left.shape[0] // GROUP
    for g in range(groups):
        at = slice(g * rows, (g + 1) * rows)
        for q in range(g * GROUP // 2, (g + 1) * GROUP // 2):
            load(q)
        for x, factor, t in ((x_second, right, t_first), (x_first, left, t_second)):
            f = factor[g * GROUP : (g + 1) * GROUP].reshape(wide, CP)
            value = lax.dot_general(x[at, :].astype(bf16), f, TRANSPOSED, preferred_element_type=f32)
            t[at, :] = jnp.where(diagonal, value, 0.0).astype(bf16)
        if beside:
            beside(g)
    for g in range(groups):
        at = slice(g * rows, (g + 1) * rows)
        for t, factor, y in ((t_first, left, y_first), (t_second, right, y_second)):
            f = factor[g * GROUP : (g + 1) * GROUP].reshape(wide, CP)
            y[at, :] = jnp.dot(t[at, :], f, preferred_element_type=f32)


def near_products(q, near, tiles, x_first, x_second, y_first, y_second, between=None):
    at = pl.ds(pl.multiple_of(q * 8, 8), 8)
    row = lax.broadcasted_iota(i32, (8, CP), 0)
    mine = 2 * q + row // NRHS < near
    x1, x2 = x_first[at, :], x_second[at, :]
    n1 = n2 = 0.0
    for k in range(2):
        tile = tiles[q // 2, k]
        here = row // NRHS == k
        n1 += lax.dot_general(
            jnp.where(here, x2, 0.0).astype(bf16), tile, TRANSPOSED, preferred_element_type=f32
        )
        if between:
            between(2 * k)
        n2 += jnp.dot(jnp.where(here, x1, 0.0).astype(bf16), tile, preferred_element_type=f32)
        if between:
            between(2 * k + 1)
    y_first[at, :] = jnp.where(mine, n1, y_first[at, :])
    y_second[at, :] = jnp.where(mine, n2, y_second[at, :])


def send_products(q, slots, y_first, y_second, out):
    at = pl.ds(pl.multiple_of(q * 8, 8), 8)
    for side, y in ((0, y_first), (1, y_second)):
        a, b = fold_two(y[at, :])
        out[slots[side, 2 * q]] = a.astype(bf16)
        out[slots[side, 2 * q + 1]] = b.astype(bf16)


def halves(x, parts):
    out = []
    for _ in range(parts):
        piece = x.astype(bf16).astype(f32)
        out.append(piece)
        x = x - piece
    return out


TERMS = 48


def distance_terms(code, side):
    unit = GEO_HALF[0] / CODE
    row = lax.broadcasted_iota(i32, (8, CP), 0)
    place = row % 4 < 3
    squares = jnp.where(place, code * code, 0.0)
    sizes = (GEO_MID[3] + code * (GEO_HALF[3] / CODE)) * (1.0 / unit**2)
    squares = jnp.where(place, squares, sizes)
    totals = [jnp.sum(squares[k : k + 4], axis=0, keepdims=True) for k in (0, 4)]
    total = jnp.where(row < 4, totals[0], totals[1])
    n1, n2, n3 = halves(total, 3)
    high, low = halves(code, 2)
    one = jnp.ones((8, CP), f32)
    zero = jnp.zeros((8, CP), f32)
    if side == 0:
        parts = [
            jnp.where(place, high, n1), jnp.where(place, high, n2), jnp.where(place, low, n3),
            jnp.where(place, low, one), jnp.where(row % 4 < 2, one, zero),
        ]
    else:
        high, low = -2.0 * high, -2.0 * low
        parts = [
            jnp.where(place, high, one), jnp.where(place, low, one), jnp.where(place, high, one),
            jnp.where(place, low, n1),
            jnp.where(row % 4 == 0, n2, jnp.where(row % 4 == 1, n3, zero)),
        ]
    return jnp.concatenate(parts + [zero], axis=0)


def first_kernel(
    slots, got, factor, left, right, out, even, odd,
    x_first, x_second, y_first, y_second, t_first, t_second, terms_first, terms_second,
):
    npair = left.shape[0]
    near = slots[0, npair]

    def load(q):
        for side, x in ((0, x_first), (1, x_second)):
            s, t = slots[side, 2 * q], slots[side, 2 * q + 1]
            f, g = factor[s // CAP], factor[t // CAP]
            u = got[s, : BLOCK[0]].astype(i32).astype(f32) * jnp.concatenate([f, f], axis=0)
            w = got[t, : BLOCK[0]].astype(i32).astype(f32) * jnp.concatenate([g, g], axis=0)
            x[8 * q : 8 * q + 8, :] = unfold_two(u, w)

    term = lax.broadcasted_iota(i32, (TERMS, CP), 0)

    def load_terms(q):
        place = [
            unfold_two(*(got[slots[side, 2 * q + k], BLOCK[0] :].astype(i32).astype(f32) for k in range(2)))
            for side in range(2)
        ]
        terms_first[q] = distance_terms(place[0], 0).T.astype(bf16)
        both = distance_terms(place[1], 1)
        for k in range(2):
            terms_second[2 * q + k] = jnp.where(term % 8 // 4 == k, both, 0.0).astype(bf16)

    last = NEAR_MOST // 2 - 1

    def beside(g):
        load_terms(g)
        if g < 4:
            make(0, even, g)

    unit = CODE / (GEO_HALF[0] * FOUR_PI)

    def make(q, tiles, part):
        k = part // 2
        for cut in range(part % 2 * 256, part % 2 * 256 + 256, 128):
            d = jnp.dot(
                terms_first[q, cut : cut + 128, :], terms_second[2 * q + k],
                preferred_element_type=f32,
            )
            tiles[q // 2, k, cut : cut + 128, :] = (lax.rsqrt(d) * unit).astype(bf16)

    far_products(
        left, right, x_first, x_second, t_first, t_second, y_first, y_second, load, beside
    )
    load_terms(last)

    def use(q, tiles, between=None):
        near_products(q, near, tiles, x_first, x_second, y_first, y_second, between)

    def near_step(h, carry):
        use(2 * h, even, lambda part: make(2 * h + 1, odd, part))
        for k in range(spread_out):
            send_products(last + 1 + spread_out * h + k, slots, y_first, y_second, out)
        use(2 * h + 1, odd, lambda part: make(2 * h + 2, even, part))
        return carry

    spread_out = (npair // 2 - last - 1) // (last // 2)
    for h in range(last // 2):
        near_step(h, 0)
    use(last - 1, even, lambda part: make(last, odd, part))
    use(last, odd)
    for q in [*range(last + 1), *range(last + 1 + spread_out * (last // 2), npair // 2)]:
        send_products(q, slots, y_first, y_second, out)


def second_kernel(
    slots, got, left, right, even, odd, out,
    x_first, x_second, y_first, y_second, t_first, t_second,
):
    npair = left.shape[0]
    near = slots[0, npair]

    def load(q):
        for side, x in ((0, x_first), (1, x_second)):
            u, w = got[slots[side, 2 * q]], got[slots[side, 2 * q + 1]]
            x[8 * q : 8 * q + 8, :] = unfold_two(u.astype(f32), w.astype(f32))

    far_products(left, right, x_first, x_second, t_first, t_second, y_first, y_second, load)
    blocks = NEAR_MOST // 2
    spread_out = (npair // 2 - blocks) // (blocks // 2)

    def near_step(h, carry):
        near_products(2 * h, near, even, x_first, x_second, y_first, y_second)
        for k in range(spread_out):
            send_products(blocks + spread_out * h + k, slots, y_first, y_second, out)
        near_products(2 * h + 1, near, odd, x_first, x_second, y_first, y_second)
        return carry

    for h in range(blocks // 2):
        near_step(h, 0)
    for q in [*range(blocks), *range(blocks + spread_out * (blocks // 2), npair // 2)]:
        send_products(q, slots, y_first, y_second, out)


LOOSE = 4


def clear(totals):
    for total in totals:
        total[...] = jnp.zeros(total.shape, f32)


def gather_sum(wanted, got, totals):
    def step(q, carry):
        for k, total in enumerate(totals):
            c = wanted[q * LOOSE + k]
            total[c] = total[c] + got[q * LOOSE + k].astype(f32)
        return carry

    lax.fori_loop(0, got.shape[0] // LOOSE, step, 0, unroll=8)
    parts = [total[0:CDEV] for total in totals]
    while len(parts) > 1:
        parts = [a + b for a, b in zip(parts[::2], parts[1::2])]
    return parts[0]


def turn_kernel(wishes, got, image, out, half, wanted, sem, *totals):
    table = pltpu.make_async_copy(wishes, wanted, sem)
    table.start()
    clear(totals)
    table.wait()
    total = gather_sum(wanted, got, totals)
    image[...] = total
    half[...] = total.astype(bf16)

    def step(s, carry):
        out[s] = half[jnp.minimum(wanted[s], CDEV - 1)]
        return carry

    lax.fori_loop(0, out.shape[0], step, 0, unroll=32)


def inner(x, y):
    rows = jnp.sum(jnp.sum(x * y, axis=0), axis=1, keepdims=True)
    return rows[0:4] + rows[4:8] + rows[8:12] + rows[12:16]


def gram_kernel(wishes, got, met, rhs, image, second, basis, payload, wanted, sem, *totals):
    table = pltpu.make_async_copy(wishes, wanted, sem)
    table.start()
    clear(totals)
    beta = jnp.sqrt(pick(jnp.sum(met[...], axis=0, keepdims=True), 1) + EPS)
    r = rhs[...] / beta
    for c in range(CDEV):
        basis[c] = fold(r[:, c * CP : (c + 1) * CP])
    v, p = basis[...], image[...]
    known = [inner(v, v), inner(v, p), inner(p, p)]
    table.wait()
    s = gather_sum(wanted, got, totals)
    second[...] = s
    row = spread(known + [inner(v, s), inner(p, s), inner(s, s)])
    payload[...] = jnp.broadcast_to(row, payload.shape)


def final_kernel(got, norms, basis, image, second, solution_out, residual_out):
    total = jnp.sum(got[...], axis=0, keepdims=True)
    vv, vp, pp, vs, ps, ss = (pick(total, i) for i in range(6))
    beta = jnp.sqrt(pick(jnp.sum(norms[...], axis=0, keepdims=True), 1) + EPS)
    zero = jnp.zeros_like(vv)
    h11 = vp
    first = jnp.maximum(pp - 2.0 * h11 * vp + h11 * h11 * vv, zero)
    h21 = jnp.sqrt(first + EPS)
    inv = 1.0 / h21
    v1w = (vs - h11 * vp) * inv
    v2w = (ps - h11 * pp - h11 * vs + h11 * h11 * vp) * inv * inv
    ww = (ss - 2.0 * h11 * ps + h11 * h11 * pp) * inv * inv
    v1v2 = (vp - h11 * vv) * inv
    v2v2 = first * inv * inv
    h12, h22 = v1w, v2w
    third = ww + h12 * h12 * vv + h22 * h22 * v2v2
    third = third - 2.0 * h12 * v1w - 2.0 * h22 * v2w + 2.0 * h12 * h22 * v1v2
    h32 = jnp.sqrt(jnp.maximum(third, zero) + EPS)
    rho_one = jnp.sqrt(h11 * h11 + h21 * h21)
    cos_one = h11 / rho_one
    sin_one = h21 / rho_one
    upper = cos_one * h12 + sin_one * h22
    lower = cos_one * h22 - sin_one * h12
    rho_two = jnp.sqrt(lower * lower + h32 * h32)
    coef_two = lower / rho_two * (-sin_one * beta) / rho_two
    coef_one = (cos_one * beta - upper * coef_two) / rho_one
    q_one = beta - h11 * coef_one - h12 * coef_two
    q_two = -h21 * coef_one - h22 * coef_two
    q_three = -h32 * coef_two / h32
    sol_v = coef_one - coef_two * h11 * inv
    sol_p = coef_two * inv
    res_v = q_one - q_two * h11 * inv + q_three * (h22 * h11 * inv - h12)
    res_p = q_two * inv - q_three * (h11 + h22) * inv
    res_s = q_three * inv
    sol_v, sol_p, res_v, res_p, res_s = (
        jnp.concatenate([x, x, x, x], axis=0) for x in (sol_v, sol_p, res_v, res_p, res_s)
    )
    for c in range(CDEV):
        cut = slice(c * CP, (c + 1) * CP)
        v, p, s = basis[c], image[c], second[c]
        solution_out[:, cut] = unfold(sol_v * v + sol_p * p)
        residual_out[:, cut] = unfold(res_v * v + res_p * p + res_s * s)


def shards(right_side, geometry, pairs, near_count, far_left_factor, far_right):
    devices = lax.axis_size(AXES)
    npair = pairs.shape[0]
    nslot = devices * CAP
    width = right_side.shape[1]
    field = (CDEV,) + BLOCK
    plain = (nslot,) + BLOCK
    coded = (nslot, 2 * BLOCK[0], BLOCK[1])

    given = jnp.concatenate([right_side, geometry], axis=0)
    payload, slots, codes = pl.pallas_call(
        wish_kernel,
        out_shape=(
            sds((devices, 128), f32),
            sds((2, npair + 8), i32),
            sds((CDEV,) + coded[1:], jnp.int16),
        ),
        in_specs=[SMEM, VMEM, VMEM],
        out_specs=(VMEM,) * 3,
        compiler_params=room(8),
        name="wishes",
    )(near_count, pairs.T, given)
    met = all_to_all(payload.reshape(devices, 1, 128)).reshape(devices, 128)
    wanted = met[:, :CAP].astype(i32).reshape(nslot)
    wanted = jnp.where(wanted < 0, CDEV, wanted)

    table = [pltpu.SMEM((nslot,), i32), pltpu.SemaphoreType.DMA(())]
    outgoing, factor = pl.pallas_call(
        pack_kernel,
        out_shape=(sds(coded, jnp.int16), sds((devices, 2 * NRHS, 128), f32)),
        in_specs=[VMEM] * 3,
        out_specs=(VMEM,) * 2,
        scratch_shapes=table,
        compiler_params=room(8),
        name="pack",
    )(wanted, codes, met)
    incoming = all_to_all(outgoing.reshape(devices, CAP * coded[1], LANES)).reshape(coded)

    work = [pltpu.VMEM((npair * NRHS, CP), f32)] * 4
    work += [pltpu.VMEM((npair * NRHS, GROUP * RANK), bf16)] * 2
    terms = [
        pltpu.VMEM((NEAR_MOST // 2, CP, TERMS), bf16),
        pltpu.VMEM((NEAR_MOST, TERMS, CP), bf16),
    ]
    some = sds((NEAR_MOST // 4, 2, CP, CP), bf16)
    returning, even, odd = pl.pallas_call(
        first_kernel,
        out_shape=(sds(plain, bf16), some, some),
        in_specs=[SMEM] + [VMEM] * 4,
        out_specs=(VMEM,) * 3,
        scratch_shapes=work + terms,
        compiler_params=room(24),
        name="first_operator",
    )(slots, incoming, factor, far_left_factor, far_right)

    def exchange(x):
        return all_to_all(x.reshape(devices, CAP * BLOCK[0], LANES)).reshape(plain)

    totals = [pltpu.VMEM((CDEV + 1,) + BLOCK, f32)] * LOOSE
    image, outgoing = pl.pallas_call(
        turn_kernel,
        out_shape=(sds(field, f32), sds(plain, bf16)),
        in_specs=[VMEM] * 2,
        out_specs=(VMEM,) * 2,
        scratch_shapes=[pltpu.VMEM(field, bf16)] + table + totals,
        compiler_params=room(8),
        name="turn",
    )(wanted, exchange(returning))

    returning = pl.pallas_call(
        second_kernel,
        out_shape=sds(plain, bf16),
        in_specs=[SMEM] + [VMEM] * 5,
        out_specs=VMEM,
        scratch_shapes=work,
        compiler_params=room(24),
        name="second_operator",
    )(slots, exchange(outgoing), far_left_factor, far_right, even, odd)

    second, basis, gram = pl.pallas_call(
        gram_kernel,
        out_shape=(sds(field, f32), sds(field, f32), sds((devices, 128), f32)),
        in_specs=[VMEM] * 5,
        out_specs=(VMEM,) * 3,
        scratch_shapes=table + totals,
        compiler_params=room(8),
        name="gram",
    )(wanted, exchange(returning), met, right_side, image)
    sums = all_to_all(gram.reshape(devices, 1, 128)).reshape(devices, 128)

    return pl.pallas_call(
        final_kernel,
        out_shape=(sds((NRHS, width), f32),) * 2,
        in_specs=[VMEM] * 5,
        out_specs=(VMEM,) * 2,
        compiler_params=room(8),
        name="combine",
    )(sums, met, basis, image, second)


def solution(mesh):
    spread_last = P(None, AXES)
    return jax.shard_map(
        shards,
        mesh=mesh,
        in_specs=(
            spread_last,
            spread_last,
            P(AXES, None),
            P(AXES),
            P(AXES, None, None),
            P(AXES, None, None),
        ),
        out_specs=(spread_last, spread_last),
        check_vma=False,
    )
```
